32 devices in a mesh: sample: 4 (over z), marker: 8 (over y, x, core).
Axes of the slice: x: 2, y: 2, z: 4, core: 2. Of those that a mesh axis runs over, the one named last changes fastest.
Arguments:
- genotypes: bfloat16 [8192, 131072], P('sample', 'marker'), may hold values from -6 to 6
- phenotypes: float32 [16, 8192], P(None, 'sample'), may hold values from -6 to 6
- message: float32 [16, 131072], P(None, 'marker'), may hold values from -6 to 6
- probes: float32 [112, 131072], P(None, 'marker'), may hold values from -16 to 16
- inclusion: float32 [16], replicated, may hold values from 0.3 to 0.6
- slab_ratio: float32 [16], replicated, may hold values from 0.25 to 0.67
- input_precision: float32 [16], replicated, may hold values from 0.5 to 2
- noise_precision: float32 [16], replicated, may hold values from 4 to 16
Outputs:
- estimate: float32 [16, 131072], P(None, 'marker')
- lmmse_estimate: float32 [16, 131072], P(None, 'marker')
The draws below stay inside these ranges and needn't reach their ends.
All inputs are finite; a program needn't handle non-finite values.
Results may differ from the reference program's by a relative error of at most 0.0013.
Values may be sent and summed in bfloat16 or wider, within the bound.
No kernel may reach another device: no remote copies, remote signals or barrier semaphores. Data moves between devices by JAX's collectives and lax.ppermute only.
A program may use at most 192 MiB of HBM per device.

```python
import math
import jax
import jax.numpy as jnp
from jax import lax

MARKERS = 131072
TRAITS = 16
PROBES = 7
ITERS = 2
PEOPLE = 8192


def draw_genotypes(key, part):
    block_span = 64
    blocks = MARKERS // block_span
    key_own = jax.random.fold_in(key, 21)
    key_shared = jax.random.fold_in(key, 22)
    key_strength = jax.random.fold_in(key, 23)
    key_jitter = jax.random.fold_in(key, 24)
    strength = jnp.exp(jax.random.uniform(key_strength, (1, blocks, 1), jnp.float32, math.log(0.15), math.log(0.7)))
    jitter = jax.random.uniform(key_jitter, (1, blocks, block_span), jnp.float32, 0.8, 1.2)
    sharing = strength * jitter
    shared = jax.random.truncated_normal(key_shared, -4.0, 4.0, (PEOPLE, blocks, 1), jnp.float32)
    private = jax.random.truncated_normal(key_own, -4.0, 4.0, (PEOPLE, blocks, block_span), jnp.float32)
    values = jnp.sqrt(1.0 - sharing) * private + jnp.sqrt(sharing) * shared
    return values.reshape(PEOPLE, MARKERS).astype(jnp.bfloat16)


def draw_probes(key, part):
    block_span = 64
    blocks = MARKERS // block_span
    probe_rows = PROBES * TRAITS
    key_noise = jax.random.fold_in(key, 11)
    key_factor = jax.random.fold_in(key, 12)
    key_block = jax.random.fold_in(key, 13)
    key_coherence = jax.random.fold_in(key, 14)
    key_rowscale = jax.random.fold_in(key, 15)
    position = jnp.arange(MARKERS, dtype=jnp.float32) / (MARKERS - 1.0)
    factor = jax.random.uniform(key_factor, (1, MARKERS), jnp.float32, 1.0, 2.0)
    coherence = jnp.exp(jax.random.uniform(key_coherence, (probe_rows, 1, 1), jnp.float32, math.log(0.05), math.log(4.0)))
    row_scale = jnp.exp(jax.random.uniform(key_rowscale, (probe_rows, 1), jnp.float32, math.log(0.5), math.log(2.0)))
    growth = jnp.exp(math.log(3.0) * position)[None, :]
    block_part = jax.random.truncated_normal(key_block, -4.0, 4.0, (probe_rows, blocks, 1), jnp.float32)
    noise_part = jax.random.truncated_normal(key_noise, -4.0, 4.0, (probe_rows, blocks, block_span), jnp.float32)
    blended = (coherence * block_part + noise_part) / jnp.sqrt(1.0 + coherence * coherence)
    values = blended.reshape(probe_rows, MARKERS) * row_scale * growth * factor * 0.18
    return jnp.clip(values, -16.0, 16.0).astype(jnp.float32)


def block_scale(stream_key, shape, cuts, smallest, high):
    def one(axis_at, parts):
        steps = jax.random.uniform(jax.random.fold_in(jax.random.fold_in(stream_key, 6), axis_at), (parts,), jnp.float32, smallest / len(cuts), high / len(cuts))
        return jnp.repeat(jnp.exp(steps), shape[axis_at] // parts).reshape((-1,) + (1,) * (len(shape) - axis_at - 1))

    gain = one(*cuts[0])
    for cut in cuts[1:]:
        gain = gain * one(*cut)
    return gain


def noise(stream_key, dims, scale, bound, shards=(), kind=jnp.bfloat16):
    factor_of = block_scale(stream_key, dims, shards, -0.22, 0.18) if shards else 1.0
    result = jax.random.normal(stream_key, dims, jnp.float32) * scale * factor_of
    return jnp.minimum(jnp.maximum(result, -bound), bound).astype(kind)


def setup_inputs(seed: int = 0) -> dict:
    keys = jax.random.split(jax.random.key(seed), 9)
    genotypes = draw_genotypes(jax.random.fold_in(keys[8], 71), 0)
    phenotypes = noise(keys[1], (TRAITS, PEOPLE), 1.0, 6.0, ((1, 4),), jnp.float32)
    message = noise(keys[2], (TRAITS, MARKERS), 1.0, 6.0, ((1, 8),), jnp.float32)
    probes = draw_probes(jax.random.fold_in(keys[8], 71), 0)
    inclusion = jnp.clip(jax.random.uniform(keys[4], (TRAITS,), jnp.float32, 0.3, 0.6), 0.3, 0.6)
    slab_ratio = jnp.clip(jax.random.uniform(keys[5], (TRAITS,), jnp.float32, 0.25, 0.67), 0.25, 0.67)
    input_precision = jnp.clip(jnp.exp(jax.random.uniform(keys[6], (TRAITS,), jnp.float32, math.log(0.5), math.log(2.0))), 0.5, 2.0)
    noise_precision = jnp.clip(jnp.exp(jax.random.uniform(keys[7], (TRAITS,), jnp.float32, math.log(4.0), math.log(16.0))), 4.0, 16.0)
    return dict(genotypes=genotypes, phenotypes=phenotypes, message=message, probes=probes, inclusion=inclusion, slab_ratio=slab_ratio, input_precision=input_precision, noise_precision=noise_precision)


def denoise(signal, precision, shrink, logit_base):
    energy = shrink * precision * signal * signal
    weight = jax.nn.sigmoid(logit_base + 0.5 * energy)
    return shrink * weight * signal, shrink * weight * (1.0 + (1.0 - weight) * energy)


def contract_rows(vectors, genotypes):
    return lax.dot_general(vectors, genotypes, (((1,), (1,)), ((), ())), preferred_element_type=jnp.float32)


def reference(genotypes, phenotypes, message, probes, inclusion, slab_ratio, input_precision, noise_precision):
    shrink = (slab_ratio / (1.0 + slab_ratio))[:, None]
    odds = jnp.log(inclusion / (1.0 - inclusion))[:, None]
    logit_base = odds + 0.5 * jnp.log(1.0 - shrink)
    first, slopes = denoise(message, input_precision[:, None], shrink, logit_base)
    first_slope = jnp.sum(slopes, axis=1) / MARKERS
    second_precision = input_precision * (1.0 - first_slope) / first_slope
    centre = (first - first_slope[:, None] * message) / (1.0 - first_slope)[:, None]
    centre_b = centre.astype(jnp.bfloat16)
    misfit = phenotypes - contract_rows(centre_b, genotypes)
    misfit_b = misfit.astype(jnp.bfloat16)
    start_res = (noise_precision[:, None] / PEOPLE) * jnp.dot(misfit_b, genotypes, preferred_element_type=jnp.float32)
    copies = 1 + PROBES
    scale_col = jnp.tile(noise_precision / PEOPLE, copies)[:, None]
    prec_col = jnp.tile(second_precision, copies)[:, None]
    iterate = jnp.concatenate([centre, jnp.zeros((PROBES * TRAITS, MARKERS), jnp.float32)], axis=0)
    residual = jnp.concatenate([start_res, probes], axis=0)
    direction = residual
    norm_start = jnp.sum(residual * residual, axis=1)
    norm_now = norm_start
    for iteration in range(ITERS):
        direction_b = direction.astype(jnp.bfloat16)
        predicted = contract_rows(direction_b, genotypes).astype(jnp.bfloat16)
        applied = scale_col * jnp.dot(predicted, genotypes, preferred_element_type=jnp.float32) + prec_col * direction
        step_size = norm_now / jnp.sum(direction * applied, axis=1)
        iterate = iterate + step_size[:, None] * direction
        if iteration + 1 < ITERS:
            residual = residual - step_size[:, None] * applied
            norm_next = jnp.sum(residual * residual, axis=1)
            direction = residual + (norm_next / norm_now)[:, None] * direction
            norm_now = norm_next
    lmmse_estimate = iterate[:TRAITS]
    probe_dot = jnp.sum(jnp.sum(probes * iterate[TRAITS:], axis=1).reshape(PROBES, TRAITS), axis=0)
    probe_norm = jnp.sum(norm_start[TRAITS:].reshape(PROBES, TRAITS), axis=0)
    second_slope = second_precision * probe_dot / (probe_norm + 1e-6)
    next_precision = second_precision * (1.0 - second_slope) / second_slope
    next_message = (lmmse_estimate - second_slope[:, None] * centre) / (1.0 - second_slope)[:, None]
    slab_var = slab_ratio / input_precision
    next_shrink = (slab_var * next_precision / (1.0 + slab_var * next_precision))[:, None]
    next_base = odds + 0.5 * jnp.log(1.0 - next_shrink)
    estimate, unused_slopes = denoise(next_message, next_precision[:, None], next_shrink, next_base)
    return estimate, lmmse_estimate
```

```python
import functools

import jax
import jax.numpy as jnp
from jax import lax
from jax.experimental import pallas as pl
from jax.experimental.pallas import tpu as pltpu
from jax.sharding import PartitionSpec as P

F32 = jnp.float32
BF16 = jnp.bfloat16
LIMIT = 44 << 20
SLOTS = 4
VMEM = pl.BlockSpec(memory_space=pltpu.VMEM)
ANY = pl.BlockSpec(memory_space=pl.ANY)


def block_of(size, most):
    while size % most:
        most //= 2
    return most


def swap(x, axis, bits):
    n = lax.axis_size(axis)
    return lax.ppermute(x, axis, [(i, i ^ bits) for i in range(n)])


def tree(parts):
    while len(parts) > 1:
        parts = [parts[i] + parts[i + 1] for i in range(0, len(parts), 2)]
    return parts[0]


def sum_direct(x, axis, unit=1):
    n = lax.axis_size(axis)
    return tree([x if k == 0 else swap(x, axis, k) for k in range(0, n, unit)])


def sum_marker(x):
    return sum_direct(x + swap(x, "marker", 1), "marker", 2)


def denoise(signal, precision, shrink, logit_base):
    energy = shrink * precision * signal * signal
    weight = jax.nn.sigmoid(logit_base + 0.5 * energy)
    return (shrink * weight * signal, shrink * weight * (1.0 + (1.0 - weight) * energy))


def stream(place, held, sems, total, prepare, use):
    slots = held.shape[0]

    def copy(c):
        slot = lax.rem(c, slots)
        return pltpu.make_async_copy(place(c), held.at[slot], sems.at[slot])

    for c in range(min(slots, total)):
        copy(c).start()
    prepare()

    def step(c, carry):
        copy(c).wait()
        use(c, held.at[lax.rem(c, slots)])

        @pl.when(c + slots < total)
        def _():
            copy(c + slots).start()

        return carry

    lax.fori_loop(0, total, step, 0)


def ring(rows, columns):
    return [pltpu.VMEM((SLOTS, rows, columns), BF16), pltpu.SemaphoreType.DMA((SLOTS,))]


def forward_loop(g, rows, total, held, sems, off, span, pieces, wide, fresh, prepare):
    people = g.shape[0]
    slots, pb, kb = held.shape
    steps, blocks = span // kb, people // pb

    def place(c):
        k, i = c // blocks, lax.rem(c, blocks)
        col = off[k // steps] * span + lax.rem(k, steps) * kb
        return g.at[pl.ds(pl.multiple_of(i * pb, pb), pb), pl.ds(pl.multiple_of(col, kb), kb)]

    def use(c, slot):
        k, i = c // blocks, lax.rem(c, blocks)
        d = rows[:, pl.ds(pl.multiple_of(k * kb, kb), kb)]
        here = pl.ds(pl.multiple_of(i * pb, pb), pb)
        across = (((1,), (1,)), ((), ()))
        if wide:
            at = (here, slice(None))
            value = lax.dot_general(slot[...], d, across, preferred_element_type=F32)
        else:
            at = (slice(None), here)
            value = lax.dot_general(d, slot[...], across, preferred_element_type=F32)
        if fresh:

            @pl.when(k == 0)
            def _():
                total[at] = value

            @pl.when(k > 0)
            def _():
                total[at] += value

        else:
            total[at] += value

    stream(place, held, sems, pieces * steps * blocks, prepare, use)


def split_people(out, total):
    n, _, share = out.shape
    for b in range(n):
        out[b] = total[b * share : (b + 1) * share, :].T


def first_body(off, message, cols, probes, g, out, centre, rows, held, sems, total):
    t = message.shape[0]

    def prepare():
        precision, shrink, base, slope = [cols[:, j : j + 1] for j in range(4)]
        first, _ = denoise(message[...], precision, shrink, base)
        made = (first - slope * message[...]) / (1.0 - slope)
        centre[...] = made
        rows[:t, :] = made.astype(BF16)
        rows[t:, :] = probes[...].astype(BF16)

    forward_loop(g, rows, total, held, sems, off, g.shape[1], 1, True, True, prepare)
    split_people(out, total)


def cost(rows, people, markers):
    return pl.CostEstimate(
        flops=2 * rows * people * markers, transcendentals=0, bytes_accessed=2 * people * markers
    )


def first_forward(message, cols, probes, genotypes, columns):
    people, markers = genotypes.shape
    r = message.shape[0] + probes.shape[0]
    pb, kb = block_of(people, 1024), block_of(markers, 2048)
    return pl.pallas_call(
        first_body,
        grid_spec=pltpu.PrefetchScalarGridSpec(
            num_scalar_prefetch=1,
            grid=(),
            in_specs=[VMEM, VMEM, VMEM, ANY],
            out_specs=[VMEM, VMEM],
            scratch_shapes=[
                pltpu.VMEM((r, markers), BF16),
                *ring(pb, kb),
                pltpu.VMEM((people, r), F32),
            ],
        ),
        out_shape=[
            jax.ShapeDtypeStruct((columns, r, people // columns), F32),
            jax.ShapeDtypeStruct(message.shape, F32),
        ],
        compiler_params=pltpu.CompilerParams(vmem_limit_bytes=LIMIT),
        cost_estimate=cost(r, people, markers),
        name="first_forward",
    )(jnp.zeros((1,), jnp.int32), message, cols, probes, genotypes)


def narrow_body(n, with_acc, off, *refs):
    refs = list(refs)
    pieces = [refs.pop(0) for _ in range(n)]
    acc = refs.pop(0) if with_acc else None
    g, out, rows, held, sems = refs
    span = pieces[0].shape[1]

    def prepare():
        for j in range(n):
            rows[:, j * span : (j + 1) * span] = pieces[j][...]
        if with_acc:
            out[...] = acc[...]

    forward_loop(g, rows, out, held, sems, off, span, n, False, not with_acc, prepare)


def narrow_forward(pieces, places, acc, genotypes, name):
    people = genotypes.shape[0]
    n, (t, span) = len(pieces), pieces[0].shape
    pb, kb = block_of(people, 1024), block_of(span, 2048)
    operands = [*pieces, *([] if acc is None else [acc]), genotypes]
    return pl.pallas_call(
        functools.partial(narrow_body, n, acc is not None),
        grid_spec=pltpu.PrefetchScalarGridSpec(
            num_scalar_prefetch=1,
            grid=(),
            in_specs=[VMEM] * (len(operands) - 1) + [ANY],
            out_specs=VMEM,
            scratch_shapes=[pltpu.VMEM((t, n * span), BF16), *ring(pb, kb)],
        ),
        out_shape=jax.ShapeDtypeStruct((t, people), F32),
        compiler_params=pltpu.CompilerParams(vmem_limit_bytes=LIMIT),
        cost_estimate=cost(t, people, n * span),
        name=name,
    )(places, *operands)


def wide_body(n, with_acc, off, *refs):
    refs = list(refs)
    pieces = [refs.pop(0) for _ in range(n)]
    probes = refs.pop(0)
    acc = refs.pop(0) if with_acc else None
    if with_acc:
        g, out, rows, held, sems, total = refs
    else:
        g, total, rows, held, sems = refs
    t, span = pieces[0].shape

    def prepare():
        for j in range(n):
            here = slice(j * span, (j + 1) * span)
            rows[:t, here] = pieces[j][...]
            rows[t:, here] = probes[:, pl.ds(pl.multiple_of(off[j] * span, span), span)]
        if with_acc:
            total[...] = acc[...]

    forward_loop(g, rows, total, held, sems, off, span, n, True, not with_acc, prepare)
    if with_acc:
        split_people(out, total)


def wide_forward(pieces, probes, places, acc, genotypes, columns, name):
    people = genotypes.shape[0]
    n, (t, span) = len(pieces), pieces[0].shape
    r = t + probes.shape[0]
    pb, kb = block_of(people, 1024), block_of(span, 2048)
    operands = [*pieces, probes, *([] if acc is None else [acc]), genotypes]
    scratch = [pltpu.VMEM((r, n * span), BF16), *ring(pb, kb)]
    if acc is None:
        shape = (people, r)
    else:
        shape = (columns, r, people // columns)
        scratch.append(pltpu.VMEM((people, r), F32))
    return pl.pallas_call(
        functools.partial(wide_body, n, acc is not None),
        grid_spec=pltpu.PrefetchScalarGridSpec(
            num_scalar_prefetch=1,
            grid=(),
            in_specs=[VMEM] * (len(operands) - 1) + [ANY],
            out_specs=VMEM,
            scratch_shapes=scratch,
        ),
        out_shape=jax.ShapeDtypeStruct(shape, F32),
        compiler_params=pltpu.CompilerParams(vmem_limit_bytes=LIMIT),
        cost_estimate=cost(r, people, n * span),
        name=name,
    )(places, *operands)


def backward_loop(g, rows, total, held, sems, off, span, pieces):
    people = g.shape[0]
    slots, pk, mb = held.shape
    steps, blocks = span // mb, people // pk

    def place(c):
        k, i = c // blocks, lax.rem(c, blocks)
        col = off[k // steps] * span + lax.rem(k, steps) * mb
        return g.at[pl.ds(pl.multiple_of(i * pk, pk), pk), pl.ds(pl.multiple_of(col, mb), mb)]

    def use(c, slot):
        k, i = c // blocks, lax.rem(c, blocks)
        here = pl.ds(pl.multiple_of(k * mb, mb), mb)
        d = rows[:, pl.ds(pl.multiple_of(i * pk, pk), pk)]
        value = jnp.dot(d, slot[...], preferred_element_type=F32)

        @pl.when(i == 0)
        def _():
            total[:, here] = value

        @pl.when(i > 0)
        def _():
            total[:, here] += value

    stream(place, held, sems, pieces * steps * blocks, lambda: None, use)


def narrow_back_body(n, span, off, rows, g, out, held, sems):
    backward_loop(g, rows, out, held, sems, off, span, n)


def wide_back_body(n, span, t, off, rows, g, *refs):
    out, whole, total, made, sent, held, sems = refs[-7:]
    backward_loop(g, rows, total, held, sems, off, span, n)
    made[...] = total[t:, :].astype(BF16)
    copies = []
    for j in range(n):
        cols = pl.ds(pl.multiple_of(off[j] * span, span), span)
        copies.append(
            pltpu.make_async_copy(made.at[:, pl.ds(j * span, span)], whole.at[:, cols], sent.at[j])
        )
        copies[-1].start()
    out[...] = total[:t, :]
    for copy in copies:
        copy.wait()


def backward(rows, places, genotypes, span, t, whole, name):
    people, markers = genotypes.shape
    r, n = rows.shape[0], places.shape[0]
    pk, mb = block_of(people, 1024), block_of(span, 2048)
    operands, specs, aliases = [rows, genotypes], [VMEM, ANY], {}
    if t is None:
        body = functools.partial(narrow_back_body, n, span)
        out_specs, out_shape = VMEM, jax.ShapeDtypeStruct((r, n * span), F32)
        scratch = ring(pk, mb)
    else:
        body = functools.partial(wide_back_body, n, span, t)
        out_specs = [VMEM, ANY]
        out_shape = [
            jax.ShapeDtypeStruct((t, n * span), F32),
            jax.ShapeDtypeStruct((r - t, markers), BF16),
        ]
        scratch = [
            pltpu.VMEM((r, n * span), F32),
            pltpu.VMEM((r - t, n * span), BF16),
            pltpu.SemaphoreType.DMA((n,)),
            *ring(pk, mb),
        ]
        if whole is not None:
            operands.append(whole)
            specs.append(ANY)
            aliases = {3: 1}
    return pl.pallas_call(
        body,
        grid_spec=pltpu.PrefetchScalarGridSpec(
            num_scalar_prefetch=1,
            grid=(),
            in_specs=specs,
            out_specs=out_specs,
            scratch_shapes=scratch,
        ),
        out_shape=out_shape,
        input_output_aliases=aliases,
        compiler_params=pltpu.CompilerParams(vmem_limit_bytes=LIMIT),
        cost_estimate=cost(r, people, n * span),
        name=name,
    )(places, *operands)


def finish_body(n, copies, off, sums, wide_cols, cols, centre, *refs):
    start_hi, back_hi, low = refs[:n], refs[n : 2 * n], refs[2 * n : 3 * n]
    estimate, lmmse = refs[3 * n :]
    t, span = start_hi[0].shape
    norm_start, du, uu, xx, xw, ww = [sums[:, j : j + 1] for j in range(6)]
    tau, gamma = wide_cols[:, 0:1], wide_cols[:, 1:2]
    second_precision, slab_var, odds = [cols[:, j : j + 1] for j in range(3)]

    step_0 = norm_start / (tau * du + gamma * norm_start)
    left, b = 1.0 - step_0 * gamma, step_0 * tau
    norm_next = left * left * norm_start - 2.0 * left * b * du + b * b * uu
    a = left + norm_next / norm_start
    dir_norm = a * a * norm_start - 2.0 * a * b * du + b * b * uu
    dir_square = a * a * xx - 2.0 * a * b * xw + b * b * ww
    step_1 = norm_next / (tau * dir_square + gamma * dir_norm)

    start_coef = (step_0 + step_1 * a)[:t]
    back_coef = (step_1 * b)[:t]
    dots = step_0 * norm_start + step_1 * (a * norm_start - b * du)
    probe_dot = sum(dots[i * t : (i + 1) * t] for i in range(1, copies))
    probe_norm = sum(norm_start[i * t : (i + 1) * t] for i in range(1, copies))
    second_slope = second_precision * probe_dot / (probe_norm + 1e-06)
    next_precision = second_precision * (1.0 - second_slope) / second_slope
    next_shrink = slab_var * next_precision / (1.0 + slab_var * next_precision)
    next_base = odds + 0.5 * jnp.log(1.0 - next_shrink)
    for j in range(n):
        here = pl.ds(pl.multiple_of(off[j] * span, span), span)
        start = start_hi[j][...].astype(F32) + low[j][:t, :].astype(F32)
        back = back_hi[j][...].astype(F32) + low[j][t:, :].astype(F32)
        middle = centre[:, here]
        made = middle + start_coef * start - back_coef * back
        lmmse[:, here] = made
        next_message = (made - second_slope * middle) / (1.0 - second_slope)
        value, _ = denoise(next_message, next_precision, next_shrink, next_base)
        estimate[:, here] = value


def finish(places, sums, wide_cols, cols, centre, start_hi, back_hi, low):
    n = len(low)
    shape = jax.ShapeDtypeStruct(centre.shape, F32)
    copies = sums.shape[0] // centre.shape[0]
    operands = [sums, wide_cols, cols, centre, *start_hi, *back_hi, *low]
    return pl.pallas_call(
        functools.partial(finish_body, n, copies),
        grid_spec=pltpu.PrefetchScalarGridSpec(
            num_scalar_prefetch=1, grid=(), in_specs=[VMEM] * len(operands), out_specs=[VMEM, VMEM]
        ),
        out_shape=[shape, shape],
        compiler_params=pltpu.CompilerParams(vmem_limit_bytes=LIMIT),
        name="finish",
    )(places, *operands)


def per_device(
    genotypes, phenotypes, message, probes, inclusion, slab_ratio, input_precision, noise_precision
):
    samples, columns = lax.axis_size("sample"), lax.axis_size("marker")
    people_here, markers_here = genotypes.shape
    people, markers = people_here * samples, markers_here * columns
    traits = message.shape[0]
    copies = probes.shape[0] // traits + 1
    me, column = lax.axis_index("sample"), lax.axis_index("marker")
    quarter, share = markers_here // samples, people_here // columns
    order = jnp.arange(samples, dtype=jnp.int32) ^ me
    near, far = order[: samples // 2], order[samples // 2 :]
    halves = samples // 2

    shrink = slab_ratio / (1.0 + slab_ratio)
    odds = jnp.log(inclusion / (1.0 - inclusion))
    logit_base = odds + 0.5 * jnp.log(1.0 - shrink)
    _, slopes = denoise(message, input_precision[:, None], shrink[:, None], logit_base[:, None])
    first_slope = sum_marker(jnp.sum(slopes, axis=1, keepdims=True))[:, 0] / markers
    second_precision = input_precision * (1.0 - first_slope) / first_slope
    scale = (noise_precision / people)[:, None]

    cols = jnp.stack([input_precision, shrink, logit_base, first_slope], axis=1)
    value, centre = first_forward(message, cols, probes, genotypes, columns)
    kept_x = jnp.sum(lax.all_to_all(value, "marker", 0, 0), axis=0)
    own = lax.dynamic_slice_in_dim(phenotypes, column * share, share, 1) - kept_x[:traits]
    rows = jnp.concatenate([own, kept_x[traits:]], axis=0).astype(BF16)
    rows = lax.all_gather(rows, "marker", axis=1, tiled=True)
    part, whole = backward(rows, far, genotypes, quarter, traits, None, "first_back_far")
    sent = {k: swap(part[:, (k - halves) * quarter :][:, :quarter], "sample", k) for k in range(halves, samples)}
    part, whole = backward(rows, near, genotypes, quarter, traits, whole, "first_back_near")
    for k in range(halves):
        mine = part[:, k * quarter : (k + 1) * quarter]
        sent[k] = swap(mine, "sample", k) if k else mine
    start = scale * tree([sent[k] for k in range(samples)])
    start_hi = start.astype(BF16)

    probe_back = lax.psum(whole, "sample")

    start_pieces = [swap(start_hi, "sample", k) if k else start_hi for k in range(samples)]
    value = narrow_forward(start_pieces[:halves], near, None, genotypes, "second_forward_near")
    value = narrow_forward(start_pieces[halves:], far, value, genotypes, "second_forward_far")
    value = sum_marker(value)
    kept_s = lax.dynamic_slice_in_dim(value, column * share, share, 1)
    rows = value.astype(BF16)
    part = backward(rows, far, genotypes, quarter, None, None, "second_back_far")
    sent = {k: swap(part[:, (k - halves) * quarter :][:, :quarter], "sample", k) for k in range(halves, samples)}
    part = backward(rows, near, genotypes, quarter, None, None, "second_back_near")
    for k in range(halves):
        mine = part[:, k * quarter : (k + 1) * quarter]
        sent[k] = swap(mine, "sample", k) if k else mine
    back = tree([sent[k] for k in range(samples)])
    back_hi = back.astype(BF16)
    back_pieces = [swap(back_hi, "sample", k) if k else back_hi for k in range(samples)]

    total = wide_forward(
        back_pieces[:halves], probe_back, near, None, genotypes, columns, "third_forward_near"
    )
    low = jnp.concatenate([start - start_hi.astype(F32), back - back_hi.astype(F32)], axis=0)
    low, total = lax.optimization_barrier((low.astype(BF16), total))
    low_pieces = [swap(low, "sample", k) if k else low for k in range(samples)]
    value = wide_forward(
        back_pieces[halves:], probe_back, far, total, genotypes, columns, "third_forward_far"
    )
    last = jnp.sum(lax.all_to_all(value, "marker", 0, 0), axis=0)
    before = jnp.concatenate([kept_s, kept_x[traits:]], axis=0)

    def quarter_of(x):
        return lax.dynamic_slice_in_dim(x, me * quarter, quarter, 1)

    def three(d, u):
        return jnp.stack([jnp.sum(d * d, 1), jnp.sum(d * u, 1), jnp.sum(u * u, 1)], axis=1)

    norms = jnp.concatenate(
        [three(start, back), three(quarter_of(probes), quarter_of(probe_back).astype(F32))], axis=0
    )
    sums = jnp.concatenate([norms, three(before, last)], axis=1)
    sums = sum_direct(sum_marker(sums), "sample")

    wide_cols = jnp.stack(
        [jnp.tile(noise_precision / people, copies), jnp.tile(second_precision, copies)], axis=1
    )
    cols = jnp.stack([second_precision, slab_ratio / input_precision, odds], axis=1)
    return tuple(
        finish(order, sums, wide_cols, cols, centre, start_pieces, back_pieces, low_pieces)
    )


def solution(mesh):
    return jax.shard_map(
        per_device,
        mesh=mesh,
        in_specs=(
            P("sample", "marker"),
            P(None, "sample"),
            P(None, "marker"),
            P(None, "marker"),
            P(),
            P(),
            P(),
            P(),
        ),
        out_specs=(P(None, "marker"), P(None, "marker")),
        check_vma=False,
    )
```

```python
import functools

import jax
import jax.numpy as jnp
from jax import lax
from jax.experimental import pallas as pl
from jax.experimental.pallas import tpu as pltpu
from jax.sharding import PartitionSpec as P

F32 = jnp.float32
BF16 = jnp.bfloat16
LIMIT = 44 << 20
SLOTS = 4
VMEM = pl.BlockSpec(memory_space=pltpu.VMEM)
ANY = pl.BlockSpec(memory_space=pl.ANY)


def block_of(size, most):
    while size % most:
        most //= 2
    return most


def swap(x, axis, bits):
    n = lax.axis_size(axis)
    return lax.ppermute(x, axis, [(i, i ^ bits) for i in range(n)])


def tree(parts):
    while len(parts) > 1:
        parts = [parts[i] + parts[i + 1] for i in range(0, len(parts), 2)]
    return parts[0]


def sum_direct(x, axis, unit=1):
    n = lax.axis_size(axis)
    return tree([x if k == 0 else swap(x, axis, k) for k in range(0, n, unit)])


def sum_marker(x):
    return sum_direct(x + swap(x, "marker", 1), "marker", 2)


def denoise(signal, precision, shrink, logit_base):
    energy = shrink * precision * signal * signal
    weight = jax.nn.sigmoid(logit_base + 0.5 * energy)
    return (shrink * weight * signal, shrink * weight * (1.0 + (1.0 - weight) * energy))


def stream(place, held, sems, total, prepare, use):
    slots = held.shape[0]

    def copy(c):
        slot = lax.rem(c, slots)
        return pltpu.make_async_copy(place(c), held.at[slot], sems.at[slot])

    for c in range(min(slots, total)):
        copy(c).start()
    prepare()

    def step(c, carry):
        copy(c).wait()
        use(c, held.at[lax.rem(c, slots)])

        @pl.when(c + slots < total)
        def _():
            copy(c + slots).start()

        return carry

    lax.fori_loop(0, total, step, 0)


def ring(rows, columns):
    return [pltpu.VMEM((SLOTS, rows, columns), BF16), pltpu.SemaphoreType.DMA((SLOTS,))]


def forward_loop(g, rows, total, held, sems, off, span, pieces, wide, fresh, prepare):
    people = g.shape[0]
    slots, pb, kb = held.shape
    steps, blocks = span // kb, people // pb

    def place(c):
        k, i = c // blocks, lax.rem(c, blocks)
        col = off[k // steps] * span + lax.rem(k, steps) * kb
        return g.at[pl.ds(pl.multiple_of(i * pb, pb), pb), pl.ds(pl.multiple_of(col, kb), kb)]

    def use(c, slot):
        k, i = c // blocks, lax.rem(c, blocks)
        d = rows[:, pl.ds(pl.multiple_of(k * kb, kb), kb)]
        here = pl.ds(pl.multiple_of(i * pb, pb), pb)
        across = (((1,), (1,)), ((), ()))
        if wide:
            at = (here, slice(None))
            value = lax.dot_general(slot[...], d, across, preferred_element_type=F32)
        else:
            at = (slice(None), here)
            value = lax.dot_general(d, slot[...], across, preferred_element_type=F32)
        if fresh:

            @pl.when(k == 0)
            def _():
                total[at] = value

            @pl.when(k > 0)
            def _():
                total[at] += value

        else:
            total[at] += value

    stream(place, held, sems, pieces * steps * blocks, prepare, use)


def split_people(out, total, t):
    n, r, share = out.shape
    for b in range(n):
        value = total[b * share : (b + 1) * share, :].T
        high = value.astype(BF16)
        out[b, : r - t, :] = high
        if t:
            out[b, r - t :, :] = (value[:t] - high[:t].astype(F32)).astype(BF16)


def prior(cols):
    inclusion, ratio, precision = [cols[:, j : j + 1] for j in range(3)]
    shrink = ratio / (1.0 + ratio)
    base = jnp.log(inclusion / (1.0 - inclusion)) + 0.5 * jnp.log(1.0 - shrink)
    return precision, shrink, base


def slope_body(message, cols, out):
    _, slopes = denoise(message[...], *prior(cols))
    out[...] = jnp.sum(slopes, axis=1, keepdims=True)


def slope_sum(message, cols):
    return pl.pallas_call(
        slope_body,
        in_specs=[VMEM, VMEM],
        out_specs=VMEM,
        out_shape=jax.ShapeDtypeStruct((message.shape[0], 1), F32),
        compiler_params=pltpu.CompilerParams(vmem_limit_bytes=LIMIT),
        name="slope_sum",
    )(message, cols)


def first_body(markers, off, message, cols, slopes, probes, g, out, centre, rows, held, sems, total):
    t = message.shape[0]

    def prepare():
        slope = slopes[...] / markers
        first, _ = denoise(message[...], *prior(cols))
        made = (first - slope * message[...]) / (1.0 - slope)
        centre[...] = made
        rows[:t, :] = made.astype(BF16)
        rows[t:, :] = probes[...].astype(BF16)

    forward_loop(g, rows, total, held, sems, off, g.shape[1], 1, True, True, prepare)
    split_people(out, total, t)


def cost(rows, people, markers):
    return pl.CostEstimate(
        flops=2 * rows * people * markers, transcendentals=0, bytes_accessed=2 * people * markers
    )


def first_forward(message, cols, slopes, probes, genotypes, columns):
    people, markers = genotypes.shape
    t = message.shape[0]
    r = t + probes.shape[0]
    pb, kb = block_of(people, 1024), block_of(markers, 2048)
    return pl.pallas_call(
        functools.partial(first_body, markers * columns),
        grid_spec=pltpu.PrefetchScalarGridSpec(
            num_scalar_prefetch=1,
            grid=(),
            in_specs=[VMEM, VMEM, VMEM, VMEM, ANY],
            out_specs=[VMEM, VMEM],
            scratch_shapes=[
                pltpu.VMEM((r, markers), BF16),
                *ring(pb, kb),
                pltpu.VMEM((people, r), F32),
            ],
        ),
        out_shape=[
            jax.ShapeDtypeStruct((columns, r + t, people // columns), BF16),
            jax.ShapeDtypeStruct(message.shape, F32),
        ],
        compiler_params=pltpu.CompilerParams(vmem_limit_bytes=LIMIT),
        cost_estimate=cost(r, people, markers),
        name="first_forward",
    )(jnp.zeros((1,), jnp.int32), message, cols, slopes, probes, genotypes)


def narrow_body(n, unit, with_acc, off, *refs):
    refs = list(refs)
    pieces = [refs.pop(0) for _ in range(n)]
    acc = refs.pop(0) if with_acc else None
    g, out, rows, held, sems = refs
    span = pieces[0].shape[1]

    def prepare():
        for j in range(n):
            rows[:, j * span : (j + 1) * span] = pieces[j][...]
        if with_acc:
            out[...] = acc[...]

    count = n * span // unit
    forward_loop(g, rows, out, held, sems, off, unit, count, False, not with_acc, prepare)


def narrow_forward(pieces, places, acc, genotypes, name):
    people = genotypes.shape[0]
    n, (t, span) = len(pieces), pieces[0].shape
    unit = n * span // places.shape[0]
    pb, kb = block_of(people, 1024), block_of(unit, 2048)
    operands = [*pieces, *([] if acc is None else [acc]), genotypes]
    return pl.pallas_call(
        functools.partial(narrow_body, n, unit, acc is not None),
        grid_spec=pltpu.PrefetchScalarGridSpec(
            num_scalar_prefetch=1,
            grid=(),
            in_specs=[VMEM] * (len(operands) - 1) + [ANY],
            out_specs=VMEM,
            scratch_shapes=[pltpu.VMEM((t, n * span), BF16), *ring(pb, kb)],
        ),
        out_shape=jax.ShapeDtypeStruct((t, people), F32),
        compiler_params=pltpu.CompilerParams(vmem_limit_bytes=LIMIT),
        cost_estimate=cost(t, people, n * span),
        name=name,
    )(places, *operands)


def wide_body(n, half, with_acc, off, *refs):
    refs = list(refs)
    pieces = [refs.pop(0) for _ in range(n)]
    probes = refs.pop(0)
    acc = refs.pop(0) if with_acc else None
    if with_acc:
        g, out, rows, held, sems, total = refs
    else:
        g, total, rows, held, sems = refs
    t, unit = pieces[0].shape[0], pieces[0].shape[1] // 2

    def prepare():
        for j in range(n):
            here = slice(j * unit, (j + 1) * unit)
            rows[:t, here] = pieces[j][:, half * unit : (half + 1) * unit]
            there = pl.multiple_of((off[j] - half * n) * unit, unit)
            rows[t:, here] = probes[:, pl.ds(there, unit)]
        if with_acc:
            total[...] = acc[...]

    forward_loop(g, rows, total, held, sems, off, unit, n, True, not with_acc, prepare)
    if with_acc:
        split_people(out, total, 0)


def wide_forward(pieces, probes, places, half, acc, genotypes, columns, name):
    people = genotypes.shape[0]
    n, t, unit = len(pieces), pieces[0].shape[0], pieces[0].shape[1] // 2
    r = t + probes.shape[0]
    pb, kb = block_of(people, 1024), block_of(unit, 2048)
    operands = [*pieces, probes, *([] if acc is None else [acc]), genotypes]
    scratch = [pltpu.VMEM((r, n * unit), BF16), *ring(pb, kb)]
    if acc is None:
        shape = jax.ShapeDtypeStruct((people, r), F32)
    else:
        shape = jax.ShapeDtypeStruct((columns, r, people // columns), BF16)
        scratch.append(pltpu.VMEM((people, r), F32))
    return pl.pallas_call(
        functools.partial(wide_body, n, half, acc is not None),
        grid_spec=pltpu.PrefetchScalarGridSpec(
            num_scalar_prefetch=1,
            grid=(),
            in_specs=[VMEM] * (len(operands) - 1) + [ANY],
            out_specs=VMEM,
            scratch_shapes=scratch,
        ),
        out_shape=shape,
        compiler_params=pltpu.CompilerParams(vmem_limit_bytes=LIMIT),
        cost_estimate=cost(r, people, n * unit),
        name=name,
    )(places, *operands)


def backward_loop(g, rows, total, held, sems, off, span, pieces):
    people = g.shape[0]
    slots, pk, mb = held.shape
    steps, blocks = span // mb, people // pk

    def place(c):
        k, i = c // blocks, lax.rem(c, blocks)
        col = off[k // steps] * span + lax.rem(k, steps) * mb
        return g.at[pl.ds(pl.multiple_of(i * pk, pk), pk), pl.ds(pl.multiple_of(col, mb), mb)]

    def use(c, slot):
        k, i = c // blocks, lax.rem(c, blocks)
        here = pl.ds(pl.multiple_of(k * mb, mb), mb)
        d = rows[:, pl.ds(pl.multiple_of(i * pk, pk), pk)]
        value = jnp.dot(d, slot[...], preferred_element_type=F32)

        @pl.when(i == 0)
        def _():
            total[:, here] = value

        @pl.when(i > 0)
        def _():
            total[:, here] += value

    stream(place, held, sems, pieces * steps * blocks, lambda: None, use)


def back_body(n, unit, t, base, off, rows, g, *refs):
    refs = list(refs)
    held, sems = refs[-2:]
    if t == rows.shape[0]:
        outs, total = refs[:-3], refs[-3]
    else:
        outs, (whole, total, made, sent) = refs[:-6], refs[-6:-2]
    backward_loop(g, rows, total, held, sems, off, unit, n)
    copies = []
    if t != rows.shape[0]:
        made[...] = total[t:, :].astype(BF16)
        for j in range(n):
            cols = pl.ds(pl.multiple_of((off[j] - base) * unit, unit), unit)
            copies.append(
                pltpu.make_async_copy(
                    made.at[:, pl.ds(j * unit, unit)], whole.at[:, cols], sent.at[j]
                )
            )
            copies[-1].start()
    span = outs[0].shape[1]
    for j, out in enumerate(outs):
        out[...] = total[:t, j * span : (j + 1) * span]
    for copy in copies:
        copy.wait()


def backward(rows, places, genotypes, unit, t, base, arrays, name):
    people = genotypes.shape[0]
    r, n = rows.shape[0], places.shape[0]
    pk, mb = block_of(people, 1024), block_of(unit, 2048)
    out_specs = [VMEM] * arrays
    out_shape = [jax.ShapeDtypeStruct((t, n * unit // arrays), F32)] * arrays
    scratch = [pltpu.VMEM((r, n * unit), F32)]
    if t != r:
        out_specs.append(ANY)
        out_shape.append(jax.ShapeDtypeStruct((r - t, n * unit), BF16))
        scratch += [pltpu.VMEM((r - t, n * unit), BF16), pltpu.SemaphoreType.DMA((n,))]
    return pl.pallas_call(
        functools.partial(back_body, n, unit, t, base),
        grid_spec=pltpu.PrefetchScalarGridSpec(
            num_scalar_prefetch=1,
            grid=(),
            in_specs=[VMEM, ANY],
            out_specs=out_specs,
            scratch_shapes=[*scratch, *ring(pk, mb)],
        ),
        out_shape=out_shape,
        compiler_params=pltpu.CompilerParams(vmem_limit_bytes=LIMIT),
        cost_estimate=cost(r, people, n * unit),
        name=name,
    )(places, rows, genotypes)


def finish_body(n, copies, off, sums, wide_cols, cols, centre, *refs):
    start_hi, back_hi, low = refs[:n], refs[n : 2 * n], refs[2 * n : 3 * n]
    estimate, lmmse = refs[3 * n :]
    t, unit = start_hi[0].shape[0], start_hi[0].shape[1] // 2
    norm_start, du, uu, xx, xw, ww = [sums[:, j : j + 1] for j in range(6)]
    tau, gamma = wide_cols[:, 0:1], wide_cols[:, 1:2]
    second_precision, slab_var, odds = [cols[:, j : j + 1] for j in range(3)]

    step_0 = norm_start / (tau * du + gamma * norm_start)
    left, b = 1.0 - step_0 * gamma, step_0 * tau
    norm_next = left * left * norm_start - 2.0 * left * b * du + b * b * uu
    a = left + norm_next / norm_start
    dir_norm = a * a * norm_start - 2.0 * a * b * du + b * b * uu
    dir_square = a * a * xx - 2.0 * a * b * xw + b * b * ww
    step_1 = norm_next / (tau * dir_square + gamma * dir_norm)

    start_coef = (step_0 + step_1 * a)[:t]
    back_coef = (step_1 * b)[:t]
    dots = step_0 * norm_start + step_1 * (a * norm_start - b * du)
    probe_dot = sum(dots[i * t : (i + 1) * t] for i in range(1, copies))
    probe_norm = sum(norm_start[i * t : (i + 1) * t] for i in range(1, copies))
    second_slope = second_precision * probe_dot / (probe_norm + 1e-06)
    next_precision = second_precision * (1.0 - second_slope) / second_slope
    next_shrink = slab_var * next_precision / (1.0 + slab_var * next_precision)
    next_base = odds + 0.5 * jnp.log(1.0 - next_shrink)
    for j, half in [(j, half) for j in range(n) for half in range(2)]:
        here = pl.ds(pl.multiple_of((half * n + off[j]) * unit, unit), unit)
        part = slice(half * unit, (half + 1) * unit)
        start = start_hi[j][:, part].astype(F32) + low[j][:t, part].astype(F32)
        back = back_hi[j][:, part].astype(F32) + low[j][t:, part].astype(F32)
        middle = centre[:, here]
        made = middle + start_coef * start - back_coef * back
        lmmse[:, here] = made
        next_message = (made - second_slope * middle) / (1.0 - second_slope)
        value, _ = denoise(next_message, next_precision, next_shrink, next_base)
        estimate[:, here] = value


def finish(places, sums, wide_cols, cols, centre, start_hi, back_hi, low):
    n = len(low)
    shape = jax.ShapeDtypeStruct(centre.shape, F32)
    copies = sums.shape[0] // centre.shape[0]
    operands = [sums, wide_cols, cols, centre, *start_hi, *back_hi, *low]
    return pl.pallas_call(
        functools.partial(finish_body, n, copies),
        grid_spec=pltpu.PrefetchScalarGridSpec(
            num_scalar_prefetch=1, grid=(), in_specs=[VMEM] * len(operands), out_specs=[VMEM, VMEM]
        ),
        out_shape=[shape, shape],
        compiler_params=pltpu.CompilerParams(vmem_limit_bytes=LIMIT),
        name="finish",
    )(places, *operands)


def per_device(
    genotypes, phenotypes, message, probes, inclusion, slab_ratio, input_precision, noise_precision
):
    samples, columns = lax.axis_size("sample"), lax.axis_size("marker")
    people_here, markers_here = genotypes.shape
    people, markers = people_here * samples, markers_here * columns
    traits = message.shape[0]
    copies = probes.shape[0] // traits + 1
    me, column = lax.axis_index("sample"), lax.axis_index("marker")
    unit, share = markers_here // (2 * samples), people_here // columns
    order = jnp.arange(samples, dtype=jnp.int32) ^ me
    some = samples // 2
    near, far = [jnp.stack([o, o + samples], axis=1).reshape(-1) for o in (order[:some], order[some:])]

    cols = jnp.stack([inclusion, slab_ratio, input_precision], axis=1)
    slopes = sum_marker(slope_sum(message, cols))
    value, centre = first_forward(message, cols, slopes, probes, genotypes, columns)
    kept_x = jnp.sum(lax.all_to_all(value, "marker", 0, 0).astype(F32), axis=0)
    kept_x, low_x = kept_x[: traits * copies], kept_x[traits * copies :]
    own = lax.dynamic_slice_in_dim(phenotypes, column * share, share, 1) - (kept_x[:traits] + low_x)
    rows = jnp.concatenate([own, kept_x[traits:]], axis=0).astype(BF16)
    rows = lax.all_gather(rows, "marker", axis=1, tiled=True)
    starts, probe_back = [], []
    for half in range(2):
        *parts, whole = backward(
            rows, order + half * samples, genotypes, unit, traits, half * samples, samples, f"first_back_{half}"
        )
        starts.append([swap(part, "sample", k) if k else part for k, part in enumerate(parts)])
        if half:
            whole = lax.psum_scatter(whole, "sample", scatter_dimension=1, tiled=True)
            probe_back.append(lax.all_gather(whole, "sample", axis=1, tiled=True))
        else:
            probe_back.append(lax.psum(whole, "sample"))
    scale = (noise_precision / people)[:, None]
    start = scale * jnp.concatenate([tree(parts) for parts in starts], axis=1)
    start_high = lax.reduce_precision(start, 8, 7)
    start_low = (start - start_high).astype(BF16)
    start_high = start_high.astype(BF16)

    start_pieces = [swap(start_high, "sample", k) if k else start_high for k in range(samples)]
    value = narrow_forward(start_pieces[:some], near, None, genotypes, "second_forward_near")
    value = narrow_forward(start_pieces[some:], far, value, genotypes, "second_forward_far")
    value = sum_marker(value)
    kept_s = lax.dynamic_slice_in_dim(value, column * share, share, 1)
    rows = value.astype(BF16)
    parts = backward(rows, far, genotypes, unit, traits, 0, some, "second_back_far")
    sent = [swap(part, "sample", k + some) for k, part in enumerate(parts)]
    parts = backward(rows, near, genotypes, unit, traits, 0, some, "second_back_near")
    back = tree([swap(part, "sample", k) if k else part for k, part in enumerate(parts)] + sent)
    back_high = lax.reduce_precision(back, 8, 7)
    back_low = (back - back_high).astype(BF16)
    back_high = back_high.astype(BF16)
    back_pieces = [swap(back_high, "sample", k) if k else back_high for k in range(samples)]
    low = jnp.concatenate([start_low, back_low], axis=0)
    low, *back_pieces = lax.optimization_barrier((low, *back_pieces))
    low_pieces = [swap(low, "sample", k) if k else low for k in range(samples)]

    total = wide_forward(
        back_pieces, probe_back[0], order, 0, None, genotypes, columns, "third_forward_0"
    )
    total, *low_pieces = lax.optimization_barrier((total, *low_pieces))
    value = wide_forward(
        back_pieces, probe_back[1], order + samples, 1, total, genotypes, columns, "third_forward_1"
    )
    last = jnp.sum(lax.all_to_all(value, "marker", 0, 0).astype(F32), axis=0)
    before = jnp.concatenate([kept_s, kept_x[traits:]], axis=0)

    def own_units(*halves):
        return jnp.concatenate(
            [lax.dynamic_slice_in_dim(x, me * unit, unit, 1) for x in halves], axis=1
        )

    def three(d, u):
        return jnp.stack([jnp.sum(d * d, 1), jnp.sum(d * u, 1), jnp.sum(u * u, 1)], axis=1)

    probes_here = own_units(probes[:, : samples * unit], probes[:, samples * unit :])
    norms = jnp.concatenate(
        [three(start, back), three(probes_here, own_units(*probe_back).astype(F32))], axis=0
    )
    sums = jnp.concatenate([norms, three(before, last)], axis=1)
    sums = sum_direct(sum_marker(sums), "sample")

    first_slope = slopes[:, 0] / markers
    second_precision = input_precision * (1.0 - first_slope) / first_slope
    odds = jnp.log(inclusion / (1.0 - inclusion))
    wide_cols = jnp.stack(
        [jnp.tile(noise_precision / people, copies), jnp.tile(second_precision, copies)], axis=1
    )
    cols = jnp.stack([second_precision, slab_ratio / input_precision, odds], axis=1)
    return tuple(
        finish(order, sums, wide_cols, cols, centre, start_pieces, back_pieces, low_pieces)
    )


def solution(mesh):
    return jax.shard_map(
        per_device,
        mesh=mesh,
        in_specs=(
            P("sample", "marker"),
            P(None, "sample"),
            P(None, "marker"),
            P(None, "marker"),
            P(),
            P(),
            P(),
            P(),
        ),
        out_specs=(P(None, "marker"), P(None, "marker")),
        check_vma=False,
    )
```

```python
import functools

import jax
import jax.numpy as jnp
from jax import lax
from jax.experimental import pallas as pl
from jax.experimental.pallas import tpu as pltpu
from jax.sharding import PartitionSpec as P

F32 = jnp.float32
BF16 = jnp.bfloat16
LIMIT = 44 << 20
SLOTS = 4
VMEM = pl.BlockSpec(memory_space=pltpu.VMEM)
ANY = pl.BlockSpec(memory_space=pl.ANY)


def block_of(size, most):
    while size % most:
        most //= 2
    return most


def swap(x, axis, bits):
    n = lax.axis_size(axis)
    return lax.ppermute(x, axis, [(i, i ^ bits) for i in range(n)])


def tree(parts):
    while len(parts) > 1:
        parts = [parts[i] + parts[i + 1] for i in range(0, len(parts), 2)]
    return parts[0]


def sum_direct(x, axis, unit=1):
    n = lax.axis_size(axis)
    return tree([x if k == 0 else swap(x, axis, k) for k in range(0, n, unit)])


def sum_marker(x):
    return sum_direct(x + swap(x, "marker", 1), "marker", 2)


def denoise(signal, precision, shrink, logit_base):
    energy = shrink * precision * signal * signal
    weight = jax.nn.sigmoid(logit_base + 0.5 * energy)
    return (shrink * weight * signal, shrink * weight * (1.0 + (1.0 - weight) * energy))


def stream(place, held, sems, total, prepare, use):
    slots = held.shape[0]

    def copy(c):
        slot = lax.rem(c, slots)
        return pltpu.make_async_copy(place(c), held.at[slot], sems.at[slot])

    for c in range(min(slots, total)):
        copy(c).start()
    prepare()

    def step(c, carry):
        copy(c).wait()
        use(c, held.at[lax.rem(c, slots)])

        @pl.when(c + slots < total)
        def _():
            copy(c + slots).start()

        return carry

    lax.fori_loop(0, total, step, 0)


def ring(rows, columns):
    return [pltpu.VMEM((SLOTS, rows, columns), BF16), pltpu.SemaphoreType.DMA((SLOTS,))]


def forward_loop(g, rows, total, held, sems, unit_at, span, pieces, wide, fresh, prepare):
    people = g.shape[0]
    slots, pb, kb = held.shape
    steps, blocks = span // kb, people // pb

    def place(c):
        k, i = c // blocks, lax.rem(c, blocks)
        col = unit_at(k // steps) * span + lax.rem(k, steps) * kb
        return g.at[pl.ds(pl.multiple_of(i * pb, pb), pb), pl.ds(pl.multiple_of(col, kb), kb)]

    def use(c, slot):
        k, i = c // blocks, lax.rem(c, blocks)
        d = rows[:, pl.ds(pl.multiple_of(k * kb, kb), kb)]
        here = pl.ds(pl.multiple_of(i * pb, pb), pb)
        across = (((1,), (1,)), ((), ()))
        if wide:
            at = (here, slice(None))
            value = lax.dot_general(slot[...], d, across, preferred_element_type=F32)
        else:
            at = (slice(None), here)
            value = lax.dot_general(d, slot[...], across, preferred_element_type=F32)
        if fresh:

            @pl.when(k == 0)
            def _():
                total[at] = value

            @pl.when(k > 0)
            def _():
                total[at] += value

        else:
            total[at] += value

    stream(place, held, sems, pieces * steps * blocks, prepare, use)


def split_people(out, total, t):
    n, r, share = out.shape
    for b in range(n):
        value = total[b * share : (b + 1) * share, :].T
        high = value.astype(BF16)
        out[b, : r - t, :] = high
        if t:
            out[b, r - t :, :] = (value[:t] - high[:t].astype(F32)).astype(BF16)


def prior(cols):
    inclusion, ratio, precision = [cols[:, j : j + 1] for j in range(3)]
    shrink = ratio / (1.0 + ratio)
    base = jnp.log(inclusion / (1.0 - inclusion)) + 0.5 * jnp.log(1.0 - shrink)
    return precision, shrink, base


def slope_body(message, cols, out):
    _, slopes = denoise(message[...], *prior(cols))
    out[...] = jnp.sum(slopes, axis=1, keepdims=True)


def slope_sum(message, cols):
    return pl.pallas_call(
        slope_body,
        in_specs=[VMEM, VMEM],
        out_specs=VMEM,
        out_shape=jax.ShapeDtypeStruct((message.shape[0], 1), F32),
        compiler_params=pltpu.CompilerParams(vmem_limit_bytes=LIMIT),
        name="slope_sum",
    )(message, cols)


def first_body(markers, off, message, cols, slopes, probes, g, out, centre, rows, held, sems, total):
    t = message.shape[0]

    def prepare():
        slope = slopes[...] / markers
        first, _ = denoise(message[...], *prior(cols))
        made = (first - slope * message[...]) / (1.0 - slope)
        centre[...] = made
        rows[:t, :] = made.astype(BF16)
        rows[t:, :] = probes[...].astype(BF16)

    forward_loop(g, rows, total, held, sems, lambda j: j, g.shape[1], 1, True, True, prepare)
    split_people(out, total, t)


def cost(rows, people, markers):
    return pl.CostEstimate(
        flops=2 * rows * people * markers, transcendentals=0, bytes_accessed=2 * people * markers
    )


def first_forward(message, cols, slopes, probes, genotypes, columns):
    people, markers = genotypes.shape
    t = message.shape[0]
    r = t + probes.shape[0]
    pb, kb = block_of(people, 1024), block_of(markers, 2048)
    return pl.pallas_call(
        functools.partial(first_body, markers * columns),
        grid_spec=pltpu.PrefetchScalarGridSpec(
            num_scalar_prefetch=1,
            grid=(),
            in_specs=[VMEM, VMEM, VMEM, VMEM, ANY],
            out_specs=[VMEM, VMEM],
            scratch_shapes=[
                pltpu.VMEM((r, markers), BF16),
                *ring(pb, kb),
                pltpu.VMEM((people, r), F32),
            ],
        ),
        out_shape=[
            jax.ShapeDtypeStruct((columns, r + t, people // columns), BF16),
            jax.ShapeDtypeStruct(message.shape, F32),
        ],
        compiler_params=pltpu.CompilerParams(vmem_limit_bytes=LIMIT),
        cost_estimate=cost(r, people, markers),
        name="first_forward",
    )(jnp.zeros((1,), jnp.int32), message, cols, slopes, probes, genotypes)


def narrow_body(n, unit, with_acc, off, *refs):
    refs = list(refs)
    pieces = [refs.pop(0) for _ in range(n)]
    acc = refs.pop(0) if with_acc else None
    g, out, rows, held, sems = refs
    span = pieces[0].shape[1]

    def prepare():
        for j in range(n):
            rows[:, j * span : (j + 1) * span] = pieces[j][...]
        if with_acc:
            out[...] = acc[...]

    count = n * span // unit
    forward_loop(
        g, rows, out, held, sems, lambda j: off[j], unit, count, False, not with_acc, prepare
    )


def narrow_forward(pieces, places, acc, genotypes, name):
    people = genotypes.shape[0]
    n, (t, span) = len(pieces), pieces[0].shape
    unit = n * span // places.shape[0]
    pb, kb = block_of(people, 1024), block_of(unit, 2048)
    operands = [*pieces, *([] if acc is None else [acc]), genotypes]
    return pl.pallas_call(
        functools.partial(narrow_body, n, unit, acc is not None),
        grid_spec=pltpu.PrefetchScalarGridSpec(
            num_scalar_prefetch=1,
            grid=(),
            in_specs=[VMEM] * (len(operands) - 1) + [ANY],
            out_specs=VMEM,
            scratch_shapes=[pltpu.VMEM((t, n * span), BF16), *ring(pb, kb)],
        ),
        out_shape=jax.ShapeDtypeStruct((t, people), F32),
        compiler_params=pltpu.CompilerParams(vmem_limit_bytes=LIMIT),
        cost_estimate=cost(t, people, n * span),
        name=name,
    )(places, *operands)


def wide_body(n, half, chunks, with_acc, off, *refs):
    refs = list(refs)
    pieces = [refs.pop(0) for _ in range(n)]
    inner = [refs.pop(0) for _ in range(chunks)]
    outer = [refs.pop(0) for _ in range(chunks)]
    acc = refs.pop(0) if with_acc else None
    if with_acc:
        g, out, rows, held, sems, total = refs
    else:
        g, total, rows, held, sems = refs
    t, unit = pieces[0].shape[0], pieces[0].shape[1] // 2
    span = inner[0].shape[1]

    def prepare():
        for j in range(n):
            here = pl.ds(pl.multiple_of(off[j] * unit, unit), unit)
            rows[:t, here] = pieces[j][:, half * unit : (half + 1) * unit]
        for j in range(chunks):
            here = slice(j * span, (j + 1) * span)

            @pl.when(off[n] == 1)
            def _():
                rows[t:, here] = inner[j][...]

            @pl.when(off[n] == 0)
            def _():
                rows[t:, here] = outer[j][...]

        if with_acc:
            total[...] = acc[...]

    forward_loop(
        g, rows, total, held, sems, lambda j: half * n + j, unit, n, True, not with_acc, prepare
    )
    if with_acc:
        split_people(out, total, 0)


def wide_forward(pieces, inner, outer, places, half, acc, genotypes, columns, name):
    people = genotypes.shape[0]
    n, t, unit = len(pieces), pieces[0].shape[0], pieces[0].shape[1] // 2
    r = t + inner[0].shape[0]
    pb, kb = block_of(people, 1024), block_of(unit, 2048)
    operands = [*pieces, *inner, *outer, *([] if acc is None else [acc]), genotypes]
    scratch = [pltpu.VMEM((r, n * unit), BF16), *ring(pb, kb)]
    if acc is None:
        shape = jax.ShapeDtypeStruct((people, r), F32)
    else:
        shape = jax.ShapeDtypeStruct((columns, r, people // columns), BF16)
        scratch.append(pltpu.VMEM((people, r), F32))
    return pl.pallas_call(
        functools.partial(wide_body, n, half, len(inner), acc is not None),
        grid_spec=pltpu.PrefetchScalarGridSpec(
            num_scalar_prefetch=1,
            grid=(),
            in_specs=[VMEM] * (len(operands) - 1) + [ANY],
            out_specs=VMEM,
            scratch_shapes=scratch,
        ),
        out_shape=shape,
        compiler_params=pltpu.CompilerParams(vmem_limit_bytes=LIMIT),
        cost_estimate=cost(r, people, n * unit),
        name=name,
    )(places, *operands)


def backward_loop(g, rows, total, held, sems, off, span, pieces):
    people = g.shape[0]
    slots, pk, mb = held.shape
    steps, blocks = span // mb, people // pk

    def place(c):
        k, i = c // blocks, lax.rem(c, blocks)
        col = off[k // steps] * span + lax.rem(k, steps) * mb
        return g.at[pl.ds(pl.multiple_of(i * pk, pk), pk), pl.ds(pl.multiple_of(col, mb), mb)]

    def use(c, slot):
        k, i = c // blocks, lax.rem(c, blocks)
        here = pl.ds(pl.multiple_of(k * mb, mb), mb)
        d = rows[:, pl.ds(pl.multiple_of(i * pk, pk), pk)]
        value = jnp.dot(d, slot[...], preferred_element_type=F32)

        @pl.when(i == 0)
        def _():
            total[:, here] = value

        @pl.when(i > 0)
        def _():
            total[:, here] += value

    stream(place, held, sems, pieces * steps * blocks, lambda: None, use)


def back_body(n, unit, t, base, off, rows, g, *refs):
    refs = list(refs)
    held, sems = refs[-2:]
    if t == rows.shape[0]:
        outs, total = refs[:-3], refs[-3]
    else:
        outs, (lower, upper, total, made, sent) = refs[:-7], refs[-7:-2]
    backward_loop(g, rows, total, held, sems, off, unit, n)
    copies = []
    if t != rows.shape[0]:
        made[...] = total[t:, :].astype(BF16)
        for j in range(n):
            place = off[j] - base
            part = made.at[:, pl.ds(j * unit, unit)]

            def copy(whole, first):
                cols = pl.ds(pl.multiple_of((place - first) * unit, unit), unit)
                return pltpu.make_async_copy(part, whole.at[:, cols], sent.at[j])

            @pl.when(place < n // 2)
            def _():
                copy(lower, 0).start()

            @pl.when(place >= n // 2)
            def _():
                copy(upper, n // 2).start()

            copies.append(pltpu.make_async_copy(part, lower.at[:, pl.ds(0, unit)], sent.at[j]))
    span = outs[0].shape[1]
    for j, out in enumerate(outs):
        out[...] = total[:t, j * span : (j + 1) * span]
    for copy in copies:
        copy.wait()


def backward(rows, places, genotypes, unit, t, base, arrays, name):
    people = genotypes.shape[0]
    r, n = rows.shape[0], places.shape[0]
    pk, mb = block_of(people, 1024), block_of(unit, 2048)
    out_specs = [VMEM] * arrays
    out_shape = [jax.ShapeDtypeStruct((t, n * unit // arrays), F32)] * arrays
    scratch = [pltpu.VMEM((r, n * unit), F32)]
    if t != r:
        out_specs += [ANY] * 2
        out_shape += [jax.ShapeDtypeStruct((r - t, n * unit // 2), BF16)] * 2
        scratch += [pltpu.VMEM((r - t, n * unit), BF16), pltpu.SemaphoreType.DMA((n,))]
    return pl.pallas_call(
        functools.partial(back_body, n, unit, t, base),
        grid_spec=pltpu.PrefetchScalarGridSpec(
            num_scalar_prefetch=1,
            grid=(),
            in_specs=[VMEM, ANY],
            out_specs=out_specs,
            scratch_shapes=[*scratch, *ring(pk, mb)],
        ),
        out_shape=out_shape,
        compiler_params=pltpu.CompilerParams(vmem_limit_bytes=LIMIT),
        cost_estimate=cost(r, people, n * unit),
        name=name,
    )(places, rows, genotypes)


def finish_body(n, copies, off, sums, wide_cols, cols, centre, *refs):
    start_hi, back_hi, low = refs[:n], refs[n : 2 * n], refs[2 * n : 3 * n]
    estimate, lmmse = refs[3 * n :]
    t, unit = start_hi[0].shape[0], start_hi[0].shape[1] // 2
    norm_start, du, uu, xx, xw, ww = [sums[:, j : j + 1] for j in range(6)]
    tau, gamma = wide_cols[:, 0:1], wide_cols[:, 1:2]
    second_precision, slab_var, odds = [cols[:, j : j + 1] for j in range(3)]

    step_0 = norm_start / (tau * du + gamma * norm_start)
    left, b = 1.0 - step_0 * gamma, step_0 * tau
    norm_next = left * left * norm_start - 2.0 * left * b * du + b * b * uu
    a = left + norm_next / norm_start
    dir_norm = a * a * norm_start - 2.0 * a * b * du + b * b * uu
    dir_square = a * a * xx - 2.0 * a * b * xw + b * b * ww
    step_1 = norm_next / (tau * dir_square + gamma * dir_norm)

    start_coef = (step_0 + step_1 * a)[:t]
    back_coef = (step_1 * b)[:t]
    dots = step_0 * norm_start + step_1 * (a * norm_start - b * du)
    probe_dot = sum(dots[i * t : (i + 1) * t] for i in range(1, copies))
    probe_norm = sum(norm_start[i * t : (i + 1) * t] for i in range(1, copies))
    second_slope = second_precision * probe_dot / (probe_norm + 1e-06)
    next_precision = second_precision * (1.0 - second_slope) / second_slope
    next_shrink = slab_var * next_precision / (1.0 + slab_var * next_precision)
    next_base = odds + 0.5 * jnp.log(1.0 - next_shrink)
    for j, half in [(j, half) for j in range(n) for half in range(2)]:
        here = pl.ds(pl.multiple_of((half * n + off[j]) * unit, unit), unit)
        part = slice(half * unit, (half + 1) * unit)
        start = start_hi[j][:, part].astype(F32) + low[j][:t, part].astype(F32)
        back = back_hi[j][:, part].astype(F32) + low[j][t:, part].astype(F32)
        middle = centre[:, here]
        made = middle + start_coef * start - back_coef * back
        lmmse[:, here] = made
        next_message = (made - second_slope * middle) / (1.0 - second_slope)
        value, _ = denoise(next_message, next_precision, next_shrink, next_base)
        estimate[:, here] = value


def finish(places, sums, wide_cols, cols, centre, start_hi, back_hi, low):
    n = len(low)
    shape = jax.ShapeDtypeStruct(centre.shape, F32)
    copies = sums.shape[0] // centre.shape[0]
    operands = [sums, wide_cols, cols, centre, *start_hi, *back_hi, *low]
    return pl.pallas_call(
        functools.partial(finish_body, n, copies),
        grid_spec=pltpu.PrefetchScalarGridSpec(
            num_scalar_prefetch=1, grid=(), in_specs=[VMEM] * len(operands), out_specs=[VMEM, VMEM]
        ),
        out_shape=[shape, shape],
        compiler_params=pltpu.CompilerParams(vmem_limit_bytes=LIMIT),
        name="finish",
    )(places, *operands)


def per_device(
    genotypes, phenotypes, message, probes, inclusion, slab_ratio, input_precision, noise_precision
):
    samples, columns = lax.axis_size("sample"), lax.axis_size("marker")
    people_here, markers_here = genotypes.shape
    people, markers = people_here * samples, markers_here * columns
    traits = message.shape[0]
    copies = probes.shape[0] // traits + 1
    me, column = lax.axis_index("sample"), lax.axis_index("marker")
    unit, share = markers_here // (2 * samples), people_here // columns
    order = jnp.arange(samples, dtype=jnp.int32) ^ me
    some = samples // 2
    near, far = [jnp.stack([o, o + samples], axis=1).reshape(-1) for o in (order[:some], order[some:])]

    cols = jnp.stack([inclusion, slab_ratio, input_precision], axis=1)
    slopes = sum_marker(slope_sum(message, cols))
    value, centre = first_forward(message, cols, slopes, probes, genotypes, columns)
    kept_x = jnp.sum(lax.all_to_all(value, "marker", 0, 0).astype(F32), axis=0)
    kept_x, low_x = kept_x[: traits * copies], kept_x[traits * copies :]
    own = lax.dynamic_slice_in_dim(phenotypes, column * share, share, 1) - (kept_x[:traits] + low_x)
    rows = jnp.concatenate([own, kept_x[traits:]], axis=0).astype(BF16)
    pred_x = rows[traits:].astype(F32)
    rows = lax.all_gather(rows, "marker", axis=1, tiled=True)
    starts, chunks = [], []
    for half in range(2):
        *parts, lower, upper = backward(
            rows, order + half * samples, genotypes, unit, traits, half * samples, samples, f"first_back_{half}"
        )
        starts.append([swap(part, "sample", k) if k else part for k, part in enumerate(parts)])
        chunks += [lower, upper]
        rows, *_ = lax.optimization_barrier((rows, lower))

    def add(x, y):
        return (x.astype(F32) + y.astype(F32)).astype(BF16)

    def inward(c):
        return add(chunks[c], lax.ppermute(chunks[c], "sample", [(0, 1), (3, 2)]))

    def across(x):
        return add(x, lax.ppermute(x, "sample", [(1, 2), (2, 1)]))

    def outward(x):
        return lax.ppermute(x, "sample", [(1, 0), (2, 3)])

    def tie(values, *others):
        return lax.optimization_barrier((tuple(values), others))[0]

    pair, full, ends = [None] * 4, [None] * 4, [None] * 4
    pair[0] = inward(0)
    scale = (noise_precision / people)[:, None]
    start = scale * jnp.concatenate([tree(parts) for parts in starts], axis=1)
    start_high = lax.reduce_precision(start, 8, 7)
    start_low = (start - start_high).astype(BF16)
    start_high = start_high.astype(BF16)

    start_pieces = [swap(start_high, "sample", k) if k else start_high for k in range(samples)]
    start_pieces[0], start_pieces[1], chunks[1] = tie(
        (start_pieces[0], start_pieces[1], chunks[1]), pair[0], start_high
    )
    full[0], pair[1] = across(pair[0]), inward(1)
    value = narrow_forward(start_pieces[:some], near, None, genotypes, "second_forward_near")
    value = narrow_forward(start_pieces[some:], far, value, genotypes, "second_forward_far")
    value, chunks[2] = tie((value, chunks[2]), full[0], pair[1])
    ends[0], full[1], pair[2] = outward(full[0]), across(pair[1]), inward(2)
    value = sum_marker(value)
    kept_s = lax.dynamic_slice_in_dim(value, column * share, share, 1)
    rows = value.astype(BF16)
    parts = backward(rows, far, genotypes, unit, traits, 0, some, "second_back_far")
    sent = [swap(part, "sample", k + some) for k, part in enumerate(parts)]
    rows, chunks[3] = tie((rows, chunks[3]), full[1], pair[2], ends[0], *parts)
    ends[1], full[2], pair[3] = outward(full[1]), across(pair[2]), inward(3)
    parts = backward(rows, near, genotypes, unit, traits, 0, some, "second_back_near")
    back = tree([swap(part, "sample", k) if k else part for k, part in enumerate(parts)] + sent)
    back_high = lax.reduce_precision(back, 8, 7)
    back_low = (back - back_high).astype(BF16)
    back_high = back_high.astype(BF16)
    (back_high,) = tie((back_high,), full[2], pair[3], ends[1])
    ends[2], full[3] = outward(full[2]), across(pair[3])
    back_pieces = [swap(back_high, "sample", k) if k else back_high for k in range(samples)]
    back_pieces = tie(back_pieces, full[3], ends[2])
    ends[3] = outward(full[3])

    inner = ((me == 1) | (me == 2)).astype(jnp.int32)
    places = jnp.concatenate([order, inner[None]])
    total = wide_forward(
        back_pieces, full[:2], ends[:2], places, 0, None, genotypes, columns, "third_forward_0"
    )
    total, low = tie((total, jnp.concatenate([start_low, back_low], axis=0)), ends[3], total)
    low_pieces = [swap(low, "sample", k) if k else low for k in range(samples)]
    value = wide_forward(
        back_pieces, full[2:], ends[2:], places, 1, total, genotypes, columns, "third_forward_1"
    )
    (value,) = tie((value,), *low_pieces)
    last = jnp.sum(lax.all_to_all(value, "marker", 0, 0).astype(F32), axis=0)
    before = jnp.concatenate([kept_s, kept_x[traits:]], axis=0)

    def dot(x, y):
        return jnp.sum(x * y, axis=1)

    probes_here = [
        lax.dynamic_slice_in_dim(probes, (half * samples + me) * unit, unit, 1) for half in range(2)
    ]
    kept_p, last_p = kept_x[traits:], last[traits:]
    norms = jnp.concatenate(
        [
            jnp.stack([dot(start, start), dot(start, back), dot(back, back)], axis=1),
            jnp.stack(
                [sum(dot(p, p) for p in probes_here), dot(kept_p, pred_x), dot(last_p, pred_x)], axis=1
            ),
        ],
        axis=0,
    )
    squares = jnp.stack([dot(before, before), dot(before, last), dot(last, last)], axis=1)
    sums = sum_direct(sum_marker(jnp.concatenate([norms, squares], axis=1)), "sample")

    first_slope = slopes[:, 0] / markers
    second_precision = input_precision * (1.0 - first_slope) / first_slope
    odds = jnp.log(inclusion / (1.0 - inclusion))
    wide_cols = jnp.stack(
        [jnp.tile(noise_precision / people, copies), jnp.tile(second_precision, copies)], axis=1
    )
    cols = jnp.stack([second_precision, slab_ratio / input_precision, odds], axis=1)
    return tuple(
        finish(order, sums, wide_cols, cols, centre, start_pieces, back_pieces, low_pieces)
    )


def solution(mesh):
    return jax.shard_map(
        per_device,
        mesh=mesh,
        in_specs=(
            P("sample", "marker"),
            P(None, "sample"),
            P(None, "marker"),
            P(None, "marker"),
            P(),
            P(),
            P(),
            P(),
        ),
        out_specs=(P(None, "marker"), P(None, "marker")),
        check_vma=False,
    )
```

```python
import functools

import jax
import jax.numpy as jnp
from jax import lax
from jax.experimental import pallas as pl
from jax.experimental.pallas import tpu as pltpu
from jax.sharding import PartitionSpec as P

F32 = jnp.float32
BF16 = jnp.bfloat16
LIMIT = 44 << 20
SLOTS = 4
VMEM = pl.BlockSpec(memory_space=pltpu.VMEM)
ANY = pl.BlockSpec(memory_space=pl.ANY)


def block_of(size, most):
    while size % most:
        most //= 2
    return most


def swap(x, axis, bits):
    n = lax.axis_size(axis)
    return lax.ppermute(x, axis, [(i, i ^ bits) for i in range(n)])


def tree(parts):
    while len(parts) > 1:
        parts = [parts[i] + parts[i + 1] for i in range(0, len(parts), 2)]
    return parts[0]


def sum_direct(x, axis, unit=1):
    n = lax.axis_size(axis)
    return tree([x if k == 0 else swap(x, axis, k) for k in range(0, n, unit)])


def sum_marker(x):
    return sum_direct(x + swap(x, "marker", 1), "marker", 2)


def denoise(signal, precision, shrink, logit_base):
    energy = shrink * precision * signal * signal
    weight = jax.nn.sigmoid(logit_base + 0.5 * energy)
    return (shrink * weight * signal, shrink * weight * (1.0 + (1.0 - weight) * energy))


def stream(place, held, sems, total, prepare, use):
    slots = held.shape[0]

    def copy(c):
        slot = lax.rem(c, slots)
        return pltpu.make_async_copy(place(c), held.at[slot], sems.at[slot])

    for c in range(min(slots, total)):
        copy(c).start()
    prepare()

    def step(c, carry):
        copy(c).wait()
        use(c, held.at[lax.rem(c, slots)])

        @pl.when(c + slots < total)
        def _():
            copy(c + slots).start()

        return carry

    lax.fori_loop(0, total, step, 0)


def ring(rows, columns):
    return [pltpu.VMEM((SLOTS, rows, columns), BF16), pltpu.SemaphoreType.DMA((SLOTS,))]


def forward_loop(g, rows, total, held, sems, unit_at, span, pieces, wide, fresh, prepare):
    people = g.shape[0]
    slots, pb, kb = held.shape
    steps, blocks = span // kb, people // pb

    def place(c):
        k, i = c // blocks, lax.rem(c, blocks)
        col = unit_at(k // steps) * span + lax.rem(k, steps) * kb
        return g.at[pl.ds(pl.multiple_of(i * pb, pb), pb), pl.ds(pl.multiple_of(col, kb), kb)]

    def use(c, slot):
        k, i = c // blocks, lax.rem(c, blocks)
        d = rows[:, pl.ds(pl.multiple_of(k * kb, kb), kb)]
        here = pl.ds(pl.multiple_of(i * pb, pb), pb)
        across = (((1,), (1,)), ((), ()))
        if wide:
            at = (here, slice(None))
            value = lax.dot_general(slot[...], d, across, preferred_element_type=F32)
        else:
            at = (slice(None), here)
            value = lax.dot_general(d, slot[...], across, preferred_element_type=F32)
        if fresh:

            @pl.when(k == 0)
            def _():
                total[at] = value

            @pl.when(k > 0)
            def _():
                total[at] += value

        else:
            total[at] += value

    stream(place, held, sems, pieces * steps * blocks, prepare, use)


def split_people(out, total, t):
    n, r, share = out.shape
    for b in range(n):
        value = total[b * share : (b + 1) * share, :].T
        high = value.astype(BF16)
        out[b, : r - t, :] = high
        if t:
            out[b, r - t :, :] = (value[:t] - high[:t].astype(F32)).astype(BF16)


def prior(cols):
    inclusion, ratio, precision = [cols[:, j : j + 1] for j in range(3)]
    shrink = ratio / (1.0 + ratio)
    base = jnp.log(inclusion / (1.0 - inclusion)) + 0.5 * jnp.log(1.0 - shrink)
    return precision, shrink, base


def slope_body(message, cols, out):
    _, slopes = denoise(message[...], *prior(cols))
    out[...] = jnp.sum(slopes, axis=1, keepdims=True)


def slope_sum(message, cols):
    return pl.pallas_call(
        slope_body,
        in_specs=[VMEM, VMEM],
        out_specs=VMEM,
        out_shape=jax.ShapeDtypeStruct((message.shape[0], 1), F32),
        compiler_params=pltpu.CompilerParams(vmem_limit_bytes=LIMIT),
        name="slope_sum",
    )(message, cols)


def first_body(markers, off, message, cols, slopes, probes, g, out, centre, rows, held, sems, total):
    t = message.shape[0]

    def prepare():
        slope = slopes[...] / markers
        first, _ = denoise(message[...], *prior(cols))
        made = (first - slope * message[...]) / (1.0 - slope)
        centre[...] = made
        rows[:t, :] = made.astype(BF16)
        rows[t:, :] = probes[...]

    forward_loop(g, rows, total, held, sems, lambda j: j, g.shape[1], 1, True, True, prepare)
    split_people(out, total, t)


def cost(rows, people, markers):
    return pl.CostEstimate(
        flops=2 * rows * people * markers, transcendentals=0, bytes_accessed=2 * people * markers
    )


def first_forward(message, cols, slopes, probes, genotypes, columns):
    people, markers = genotypes.shape
    t = message.shape[0]
    r = t + probes.shape[0]
    pb, kb = block_of(people, 1024), block_of(markers, 2048)
    return pl.pallas_call(
        functools.partial(first_body, markers * columns),
        grid_spec=pltpu.PrefetchScalarGridSpec(
            num_scalar_prefetch=1,
            grid=(),
            in_specs=[VMEM, VMEM, VMEM, VMEM, ANY],
            out_specs=[VMEM, VMEM],
            scratch_shapes=[
                pltpu.VMEM((r, markers), BF16),
                *ring(pb, kb),
                pltpu.VMEM((people, r), F32),
            ],
        ),
        out_shape=[
            jax.ShapeDtypeStruct((columns, r + t, people // columns), BF16),
            jax.ShapeDtypeStruct(message.shape, F32),
        ],
        compiler_params=pltpu.CompilerParams(vmem_limit_bytes=LIMIT),
        cost_estimate=cost(r, people, markers),
        name="first_forward",
    )(jnp.zeros((1,), jnp.int32), message, cols, slopes, probes, genotypes)


def narrow_body(n, unit, with_acc, off, *refs):
    refs = list(refs)
    pieces = [refs.pop(0) for _ in range(n)]
    acc = refs.pop(0) if with_acc else None
    g, out, rows, held, sems = refs
    span = pieces[0].shape[1]

    def prepare():
        for j in range(n):
            rows[:, j * span : (j + 1) * span] = pieces[j][...]
        if with_acc:
            out[...] = acc[...]

    count = n * span // unit
    forward_loop(
        g, rows, out, held, sems, lambda j: off[j], unit, count, False, not with_acc, prepare
    )


def narrow_forward(pieces, places, acc, genotypes, name):
    people = genotypes.shape[0]
    n, (t, span) = len(pieces), pieces[0].shape
    unit = n * span // places.shape[0]
    pb, kb = block_of(people, 1024), block_of(unit, 2048)
    operands = [*pieces, *([] if acc is None else [acc]), genotypes]
    return pl.pallas_call(
        functools.partial(narrow_body, n, unit, acc is not None),
        grid_spec=pltpu.PrefetchScalarGridSpec(
            num_scalar_prefetch=1,
            grid=(),
            in_specs=[VMEM] * (len(operands) - 1) + [ANY],
            out_specs=VMEM,
            scratch_shapes=[pltpu.VMEM((t, n * span), BF16), *ring(pb, kb)],
        ),
        out_shape=jax.ShapeDtypeStruct((t, people), F32),
        compiler_params=pltpu.CompilerParams(vmem_limit_bytes=LIMIT),
        cost_estimate=cost(t, people, n * span),
        name=name,
    )(places, *operands)


def wide_body(n, begin, chunks, with_acc, off, *refs):
    refs = list(refs)
    pieces = [refs.pop(0) for _ in range(n)]
    inner = [refs.pop(0) for _ in range(chunks)]
    outer = [refs.pop(0) for _ in range(chunks)]
    acc = refs.pop(0) if with_acc else None
    if with_acc:
        g, out, rows, held, sems, total = refs
    else:
        g, total, rows, held, sems = refs
    t, unit = pieces[0].shape[0], pieces[0].shape[1] // 2
    span = inner[0].shape[1]
    count = chunks * span // unit

    def prepare():
        for j, half in [(j, half) for j in range(n) for half in range(2)]:
            place = half * n + off[j] - begin

            @pl.when((place >= 0) & (place < count))
            def _():
                here = pl.ds(pl.multiple_of(place * unit, unit), unit)
                rows[:t, here] = pieces[j][:, half * unit : (half + 1) * unit]

        for j in range(chunks):
            here = slice(j * span, (j + 1) * span)

            @pl.when(off[n] == 1)
            def _():
                rows[t:, here] = inner[j][...]

            @pl.when(off[n] == 0)
            def _():
                rows[t:, here] = outer[j][...]

        if with_acc:
            total[...] = acc[...]

    forward_loop(
        g, rows, total, held, sems, lambda j: begin + j, unit, count, True, not with_acc, prepare
    )
    if with_acc:
        split_people(out, total, 0)


def wide_forward(pieces, inner, outer, places, begin, acc, genotypes, columns, name):
    people = genotypes.shape[0]
    n, t, unit = len(pieces), pieces[0].shape[0], pieces[0].shape[1] // 2
    r = t + inner[0].shape[0]
    pb, kb = block_of(people, 1024), block_of(unit, 2048)
    operands = [*pieces, *inner, *outer, *([] if acc is None else [acc]), genotypes]
    span = len(inner) * inner[0].shape[1]
    scratch = [pltpu.VMEM((r, span), BF16), *ring(pb, kb)]
    if acc is None:
        shape = jax.ShapeDtypeStruct((people, r), F32)
    else:
        shape = jax.ShapeDtypeStruct((columns, r, people // columns), BF16)
        scratch.append(pltpu.VMEM((people, r), F32))
    return pl.pallas_call(
        functools.partial(wide_body, n, begin, len(inner), acc is not None),
        grid_spec=pltpu.PrefetchScalarGridSpec(
            num_scalar_prefetch=1,
            grid=(),
            in_specs=[VMEM] * (len(operands) - 1) + [ANY],
            out_specs=VMEM,
            scratch_shapes=scratch,
        ),
        out_shape=shape,
        compiler_params=pltpu.CompilerParams(vmem_limit_bytes=LIMIT),
        cost_estimate=cost(r, people, span),
        name=name,
    )(places, *operands)


def backward_loop(g, rows, total, held, sems, off, span, pieces):
    people = g.shape[0]
    slots, pk, mb = held.shape
    steps, blocks = span // mb, people // pk

    def place(c):
        k, i = c // blocks, lax.rem(c, blocks)
        col = off[k // steps] * span + lax.rem(k, steps) * mb
        return g.at[pl.ds(pl.multiple_of(i * pk, pk), pk), pl.ds(pl.multiple_of(col, mb), mb)]

    def use(c, slot):
        k, i = c // blocks, lax.rem(c, blocks)
        here = pl.ds(pl.multiple_of(k * mb, mb), mb)
        d = rows[:, pl.ds(pl.multiple_of(i * pk, pk), pk)]
        value = jnp.dot(d, slot[...], preferred_element_type=F32)

        @pl.when(i == 0)
        def _():
            total[:, here] = value

        @pl.when(i > 0)
        def _():
            total[:, here] += value

    stream(place, held, sems, pieces * steps * blocks, lambda: None, use)


def back_body(n, unit, t, base, off, rows, g, *refs):
    refs = list(refs)
    held, sems = refs[-2:]
    if t == rows.shape[0]:
        outs, total = refs[:-3], refs[-3]
    else:
        outs, (lower, upper, total, made, sent) = refs[:-7], refs[-7:-2]
    backward_loop(g, rows, total, held, sems, off, unit, n)
    copies = []
    if t != rows.shape[0]:
        made[...] = total[t:, :].astype(BF16)
        for j in range(n):
            place = off[j] - base
            part = made.at[:, pl.ds(j * unit, unit)]

            def copy(whole, first):
                cols = pl.ds(pl.multiple_of((place - first) * unit, unit), unit)
                return pltpu.make_async_copy(part, whole.at[:, cols], sent.at[j])

            @pl.when(place < n // 2)
            def _():
                copy(lower, 0).start()

            @pl.when(place >= n // 2)
            def _():
                copy(upper, n // 2).start()

            copies.append(pltpu.make_async_copy(part, lower.at[:, pl.ds(0, unit)], sent.at[j]))
    span = outs[0].shape[1]
    for j, out in enumerate(outs):
        out[...] = total[:t, j * span : (j + 1) * span]
    for copy in copies:
        copy.wait()


def backward(rows, places, genotypes, unit, t, base, arrays, name):
    people = genotypes.shape[0]
    r, n = rows.shape[0], places.shape[0]
    pk, mb = block_of(people, 1024), block_of(unit, 2048)
    out_specs = [VMEM] * arrays
    out_shape = [jax.ShapeDtypeStruct((t, n * unit // arrays), F32)] * arrays
    scratch = [pltpu.VMEM((r, n * unit), F32)]
    if t != r:
        out_specs += [ANY] * 2
        out_shape += [jax.ShapeDtypeStruct((r - t, n * unit // 2), BF16)] * 2
        scratch += [pltpu.VMEM((r - t, n * unit), BF16), pltpu.SemaphoreType.DMA((n,))]
    return pl.pallas_call(
        functools.partial(back_body, n, unit, t, base),
        grid_spec=pltpu.PrefetchScalarGridSpec(
            num_scalar_prefetch=1,
            grid=(),
            in_specs=[VMEM, ANY],
            out_specs=out_specs,
            scratch_shapes=[*scratch, *ring(pk, mb)],
        ),
        out_shape=out_shape,
        compiler_params=pltpu.CompilerParams(vmem_limit_bytes=LIMIT),
        cost_estimate=cost(r, people, n * unit),
        name=name,
    )(places, rows, genotypes)


def finish_body(n, copies, off, sums, wide_cols, cols, centre, *refs):
    start_hi, back_hi, low = refs[:n], refs[n : 2 * n], refs[2 * n : 3 * n]
    estimate, lmmse = refs[3 * n :]
    t, unit = start_hi[0].shape[0], start_hi[0].shape[1] // 2
    norm_start, du, uu, xx, xw, ww = [sums[:, j : j + 1] for j in range(6)]
    tau, gamma = wide_cols[:, 0:1], wide_cols[:, 1:2]
    second_precision, slab_var, odds = [cols[:, j : j + 1] for j in range(3)]

    step_0 = norm_start / (tau * du + gamma * norm_start)
    left, b = 1.0 - step_0 * gamma, step_0 * tau
    norm_next = left * left * norm_start - 2.0 * left * b * du + b * b * uu
    a = left + norm_next / norm_start
    dir_norm = a * a * norm_start - 2.0 * a * b * du + b * b * uu
    dir_square = a * a * xx - 2.0 * a * b * xw + b * b * ww
    step_1 = norm_next / (tau * dir_square + gamma * dir_norm)

    start_coef = (step_0 + step_1 * a)[:t]
    back_coef = (step_1 * b)[:t]
    dots = step_0 * norm_start + step_1 * (a * norm_start - b * du)
    probe_dot = sum(dots[i * t : (i + 1) * t] for i in range(1, copies))
    probe_norm = sum(norm_start[i * t : (i + 1) * t] for i in range(1, copies))
    second_slope = second_precision * probe_dot / (probe_norm + 1e-06)
    next_precision = second_precision * (1.0 - second_slope) / second_slope
    next_shrink = slab_var * next_precision / (1.0 + slab_var * next_precision)
    next_base = odds + 0.5 * jnp.log(1.0 - next_shrink)
    for j, half in [(j, half) for j in range(n) for half in range(2)]:
        here = pl.ds(pl.multiple_of((half * n + off[j]) * unit, unit), unit)
        part = slice(half * unit, (half + 1) * unit)
        start = start_hi[j][:, part].astype(F32) + low[j][:t, part].astype(F32)
        back = back_hi[j][:, part].astype(F32) + low[j][t:, part].astype(F32)
        middle = centre[:, here]
        made = middle + start_coef * start - back_coef * back
        lmmse[:, here] = made
        next_message = (made - second_slope * middle) / (1.0 - second_slope)
        value, _ = denoise(next_message, next_precision, next_shrink, next_base)
        estimate[:, here] = value


def finish(places, sums, wide_cols, cols, centre, start_hi, back_hi, low):
    n = len(low)
    shape = jax.ShapeDtypeStruct(centre.shape, F32)
    copies = sums.shape[0] // centre.shape[0]
    operands = [sums, wide_cols, cols, centre, *start_hi, *back_hi, *low]
    return pl.pallas_call(
        functools.partial(finish_body, n, copies),
        grid_spec=pltpu.PrefetchScalarGridSpec(
            num_scalar_prefetch=1, grid=(), in_specs=[VMEM] * len(operands), out_specs=[VMEM, VMEM]
        ),
        out_shape=[shape, shape],
        compiler_params=pltpu.CompilerParams(vmem_limit_bytes=LIMIT),
        name="finish",
    )(places, *operands)


def per_device(
    genotypes, phenotypes, message, probes, inclusion, slab_ratio, input_precision, noise_precision
):
    samples, columns = lax.axis_size("sample"), lax.axis_size("marker")
    people_here, markers_here = genotypes.shape
    people, markers = people_here * samples, markers_here * columns
    traits = message.shape[0]
    copies = probes.shape[0] // traits + 1
    me, column = lax.axis_index("sample"), lax.axis_index("marker")
    unit, share = markers_here // (2 * samples), people_here // columns
    order = jnp.arange(samples, dtype=jnp.int32) ^ me
    some = samples // 2
    near, far = [jnp.stack([o, o + samples], axis=1).reshape(-1) for o in (order[:some], order[some:])]

    cols = jnp.stack([inclusion, slab_ratio, input_precision], axis=1)
    slopes = slope_sum(message, cols)
    slopes = slopes + swap(slopes, "marker", 1)
    probes_b = lax.optimization_barrier((probes, slopes))[0].astype(BF16)
    slopes = sum_direct(slopes, "marker", 2)
    value, centre = first_forward(message, cols, slopes, probes_b, genotypes, columns)
    kept_x = jnp.sum(lax.all_to_all(value, "marker", 0, 0).astype(F32), axis=0)
    kept_x, low_x = kept_x[: traits * copies], kept_x[traits * copies :]
    own = lax.dynamic_slice_in_dim(phenotypes, column * share, share, 1) - (kept_x[:traits] + low_x)
    rows = jnp.concatenate([own, kept_x[traits:]], axis=0).astype(BF16)
    pred_x = rows[traits:].astype(F32)
    rows = lax.all_gather(rows, "marker", axis=1, tiled=True)
    starts, chunks = [], []
    for half in range(2):
        *parts, lower, upper = backward(
            rows, order + half * samples, genotypes, unit, traits, half * samples, samples, f"first_back_{half}"
        )
        starts.append([swap(part, "sample", k) if k else part for k, part in enumerate(parts)])
        chunks += [lower, upper]
        rows, *_ = lax.optimization_barrier((rows, lower))

    def add(x, y):
        return (x.astype(F32) + y.astype(F32)).astype(BF16)

    def tie(values, *others):
        return lax.optimization_barrier((tuple(values), others))[0]

    def hop(x, pairs, *others):
        y = lax.ppermute(x, "sample", pairs)
        return add(*tie((x, y), *others))

    def inward(c, *others):
        return hop(chunks[c], [(0, 1), (3, 2)], *others)

    def across(x, *others):
        return hop(x, [(1, 2), (2, 1)], *others)

    def outward(x):
        return lax.ppermute(x, "sample", [(1, 0), (2, 3)])

    pair, full, ends = [None] * 4, [None] * 4, [None] * 4
    pair[0] = inward(0)
    scale = (noise_precision / people)[:, None]
    start = scale * jnp.concatenate([tree(parts) for parts in starts], axis=1)
    start_high = lax.reduce_precision(start, 8, 7)
    start_low = (start - start_high).astype(BF16)
    start_high = start_high.astype(BF16)

    start_pieces = [swap(start_high, "sample", k) if k else start_high for k in range(samples)]
    start_pieces[0], start_pieces[1], chunks[1] = tie(
        (start_pieces[0], start_pieces[1], chunks[1]), pair[0], start_high
    )
    value = narrow_forward(start_pieces[:some], near, None, genotypes, "second_forward_near")
    value, *start_pieces = tie((value, *start_pieces))
    full[0], pair[1] = across(pair[0], value), inward(1, value)
    value, chunks[2] = tie((value, chunks[2]), full[0], pair[1])
    ends[0], full[1], pair[2] = outward(full[0]), across(pair[1]), inward(2)
    value = narrow_forward(start_pieces[some:], far, value, genotypes, "second_forward_far")
    value, chunks[3] = tie((value, chunks[3]), full[1], pair[2], ends[0])
    ends[1], full[2], pair[3] = outward(full[1]), across(pair[2]), inward(3)
    value = sum_marker(value)
    kept_s = lax.dynamic_slice_in_dim(value, column * share, share, 1)
    rows = value.astype(BF16)
    parts = backward(rows, far, genotypes, unit, traits, 0, some, "second_back_far")
    sent = [swap(part, "sample", k + some) for k, part in enumerate(parts)]
    (rows,) = tie((rows,), full[2], pair[3], ends[1], *parts)
    ends[2] = outward(full[2])
    parts = backward(rows, near, genotypes, unit, traits, 0, some, "second_back_near")
    sent = [swap(part, "sample", k) if k else part for k, part in enumerate(parts)] + sent
    back = tree(list(tie(sent, ends[2])))
    back_high = lax.reduce_precision(back, 8, 7)
    back_low = (back - back_high).astype(BF16)
    back_high = back_high.astype(BF16)
    back_pieces = [swap(back_high, "sample", k) if k else back_high for k in range(samples)]
    full[3] = across(pair[3], *back_pieces)
    ends[3] = outward(full[3])

    inner = ((me == 1) | (me == 2)).astype(jnp.int32)
    places = jnp.concatenate([order, inner[None]])
    total = wide_forward(
        back_pieces, full[:3], ends[:3], places, 0, None, genotypes, columns, "third_forward_0"
    )
    total, low = tie((total, jnp.concatenate([start_low, back_low], axis=0)), ends[3])
    low_pieces = [swap(low, "sample", k) if k else low for k in range(samples)]
    value = wide_forward(
        back_pieces, full[3:], ends[3:], places, 3 * some, total, genotypes, columns, "third_forward_1"
    )
    (last,) = tie((lax.all_to_all(value, "marker", 0, 0),), *low_pieces)
    last = jnp.sum(last.astype(F32), axis=0)
    before = jnp.concatenate([kept_s, kept_x[traits:]], axis=0)

    def dot(x, y):
        return jnp.sum(x * y, axis=1)

    probes_here = [
        lax.dynamic_slice_in_dim(probes, (half * samples + me) * unit, unit, 1) for half in range(2)
    ]
    kept_p, last_p = kept_x[traits:], last[traits:]
    norms = jnp.concatenate(
        [
            jnp.stack([dot(start, start), dot(start, back), dot(back, back)], axis=1),
            jnp.stack(
                [sum(dot(p, p) for p in probes_here), dot(kept_p, pred_x), dot(last_p, pred_x)], axis=1
            ),
        ],
        axis=0,
    )
    squares = jnp.stack([dot(before, before), dot(before, last), dot(last, last)], axis=1)
    sums = sum_direct(sum_marker(jnp.concatenate([norms, squares], axis=1)), "sample")

    first_slope = slopes[:, 0] / markers
    second_precision = input_precision * (1.0 - first_slope) / first_slope
    odds = jnp.log(inclusion / (1.0 - inclusion))
    wide_cols = jnp.stack(
        [jnp.tile(noise_precision / people, copies), jnp.tile(second_precision, copies)], axis=1
    )
    cols = jnp.stack([second_precision, slab_ratio / input_precision, odds], axis=1)
    return tuple(
        finish(order, sums, wide_cols, cols, centre, start_pieces, back_pieces, low_pieces)
    )


def solution(mesh):
    return jax.shard_map(
        per_device,
        mesh=mesh,
        in_specs=(
            P("sample", "marker"),
            P(None, "sample"),
            P(None, "marker"),
            P(None, "marker"),
            P(),
            P(),
            P(),
            P(),
        ),
        out_specs=(P(None, "marker"), P(None, "marker")),
        check_vma=False,
    )
```

```python
import functools

import jax
import jax.numpy as jnp
from jax import lax
from jax.experimental import pallas as pl
from jax.experimental.pallas import tpu as pltpu
from jax.sharding import PartitionSpec as P

F32 = jnp.float32
BF16 = jnp.bfloat16
LIMIT = 44 << 20
SLOTS = 4
VMEM = pl.BlockSpec(memory_space=pltpu.VMEM)
ANY = pl.BlockSpec(memory_space=pl.ANY)


def block_of(size, most):
    while size % most:
        most //= 2
    return most


def swap(x, axis, bits):
    n = lax.axis_size(axis)
    return lax.ppermute(x, axis, [(i, i ^ bits) for i in range(n)])


def tree(parts):
    while len(parts) > 1:
        parts = [parts[i] + parts[i + 1] for i in range(0, len(parts), 2)]
    return parts[0]


def sum_direct(x, axis, unit=1):
    n = lax.axis_size(axis)
    return tree([x if k == 0 else swap(x, axis, k) for k in range(0, n, unit)])


def sum_marker(x):
    return sum_direct(x + swap(x, "marker", 1), "marker", 2)


def denoise(signal, precision, shrink, logit_base):
    energy = shrink * precision * signal * signal
    weight = jax.nn.sigmoid(logit_base + 0.5 * energy)
    return (shrink * weight * signal, shrink * weight * (1.0 + (1.0 - weight) * energy))


def stream(place, held, sems, total, prepare, use):
    slots = held.shape[0]

    def copy(c):
        slot = lax.rem(c, slots)
        return pltpu.make_async_copy(place(c), held.at[slot], sems.at[slot])

    for c in range(min(slots, total)):
        copy(c).start()
    prepare()

    def step(c, carry):
        copy(c).wait()
        use(c, held.at[lax.rem(c, slots)])

        @pl.when(c + slots < total)
        def _():
            copy(c + slots).start()

        return carry

    lax.fori_loop(0, total, step, 0)


def ring(rows, columns):
    return [pltpu.VMEM((SLOTS, rows, columns), BF16), pltpu.SemaphoreType.DMA((SLOTS,))]


def forward_loop(g, rows, total, held, sems, unit_at, span, pieces, wide, fresh, prepare):
    people = g.shape[0]
    slots, pb, kb = held.shape
    steps, blocks = span // kb, people // pb

    def place(c):
        k, i = c // blocks, lax.rem(c, blocks)
        col = unit_at(k // steps) * span + lax.rem(k, steps) * kb
        return g.at[pl.ds(pl.multiple_of(i * pb, pb), pb), pl.ds(pl.multiple_of(col, kb), kb)]

    def use(c, slot):
        k, i = c // blocks, lax.rem(c, blocks)
        d = rows[:, pl.ds(pl.multiple_of(k * kb, kb), kb)]
        here = pl.ds(pl.multiple_of(i * pb, pb), pb)
        across = (((1,), (1,)), ((), ()))
        if wide:
            at = (here, slice(None))
            value = lax.dot_general(slot[...], d, across, preferred_element_type=F32)
        else:
            at = (slice(None), here)
            value = lax.dot_general(d, slot[...], across, preferred_element_type=F32)
        if fresh:

            @pl.when(k == 0)
            def _():
                total[at] = value

            @pl.when(k > 0)
            def _():
                total[at] += value

        else:
            total[at] += value

    stream(place, held, sems, pieces * steps * blocks, prepare, use)


def split_people(out, total, t):
    n, r, share = out.shape
    for b in range(n):
        value = total[b * share : (b + 1) * share, :].T
        high = value.astype(BF16)
        out[b, : r - t, :] = high
        if t:
            out[b, r - t :, :] = (value[:t] - high[:t].astype(F32)).astype(BF16)


def prior(cols):
    inclusion, ratio, precision = [cols[:, j : j + 1] for j in range(3)]
    shrink = ratio / (1.0 + ratio)
    base = jnp.log(inclusion / (1.0 - inclusion)) + 0.5 * jnp.log(1.0 - shrink)
    return precision, shrink, base


def slope_body(message, cols, out):
    _, slopes = denoise(message[...], *prior(cols))
    out[...] = jnp.sum(slopes, axis=1, keepdims=True)


def slope_sum(message, cols):
    return pl.pallas_call(
        slope_body,
        in_specs=[VMEM, VMEM],
        out_specs=VMEM,
        out_shape=jax.ShapeDtypeStruct((message.shape[0], 1), F32),
        compiler_params=pltpu.CompilerParams(vmem_limit_bytes=LIMIT),
        name="slope_sum",
    )(message, cols)


def first_body(markers, off, message, cols, slopes, probes, g, out, centre, rows, held, sems, total):
    t = message.shape[0]

    def prepare():
        slope = slopes[...] / markers
        first, _ = denoise(message[...], *prior(cols))
        made = (first - slope * message[...]) / (1.0 - slope)
        centre[...] = made
        rows[:t, :] = made.astype(BF16)
        rows[t:, :] = probes[...]

    forward_loop(g, rows, total, held, sems, lambda j: j, g.shape[1], 1, True, True, prepare)
    split_people(out, total, t)


def cost(rows, people, markers):
    return pl.CostEstimate(
        flops=2 * rows * people * markers, transcendentals=0, bytes_accessed=2 * people * markers
    )


def first_forward(message, cols, slopes, probes, genotypes, columns):
    people, markers = genotypes.shape
    t = message.shape[0]
    r = t + probes.shape[0]
    pb, kb = block_of(people, 1024), block_of(markers, 2048)
    return pl.pallas_call(
        functools.partial(first_body, markers * columns),
        grid_spec=pltpu.PrefetchScalarGridSpec(
            num_scalar_prefetch=1,
            grid=(),
            in_specs=[VMEM, VMEM, VMEM, VMEM, ANY],
            out_specs=[VMEM, VMEM],
            scratch_shapes=[
                pltpu.VMEM((r, markers), BF16),
                *ring(pb, kb),
                pltpu.VMEM((people, r), F32),
            ],
        ),
        out_shape=[
            jax.ShapeDtypeStruct((columns, r + t, people // columns), BF16),
            jax.ShapeDtypeStruct(message.shape, F32),
        ],
        compiler_params=pltpu.CompilerParams(vmem_limit_bytes=LIMIT),
        cost_estimate=cost(r, people, markers),
        name="first_forward",
    )(jnp.zeros((1,), jnp.int32), message, cols, slopes, probes, genotypes)


def narrow_body(n, unit, with_acc, off, *refs):
    refs = list(refs)
    pieces = [refs.pop(0) for _ in range(n)]
    acc = refs.pop(0) if with_acc else None
    g, out, rows, held, sems = refs
    span = pieces[0].shape[1]

    def prepare():
        for j in range(n):
            rows[:, j * span : (j + 1) * span] = pieces[j][...]
        if with_acc:
            out[...] = acc[...]

    count = n * span // unit
    forward_loop(
        g, rows, out, held, sems, lambda j: off[j], unit, count, False, not with_acc, prepare
    )


def narrow_forward(pieces, places, acc, genotypes, name):
    people = genotypes.shape[0]
    n, (t, span) = len(pieces), pieces[0].shape
    unit = n * span // places.shape[0]
    pb, kb = block_of(people, 1024), block_of(unit, 2048)
    operands = [*pieces, *([] if acc is None else [acc]), genotypes]
    return pl.pallas_call(
        functools.partial(narrow_body, n, unit, acc is not None),
        grid_spec=pltpu.PrefetchScalarGridSpec(
            num_scalar_prefetch=1,
            grid=(),
            in_specs=[VMEM] * (len(operands) - 1) + [ANY],
            out_specs=VMEM,
            scratch_shapes=[pltpu.VMEM((t, n * span), BF16), *ring(pb, kb)],
        ),
        out_shape=jax.ShapeDtypeStruct((t, people), F32),
        compiler_params=pltpu.CompilerParams(vmem_limit_bytes=LIMIT),
        cost_estimate=cost(t, people, n * span),
        name=name,
    )(places, *operands)


def wide_body(n, begin, chunks, with_acc, off, *refs):
    refs = list(refs)
    pieces = [refs.pop(0) for _ in range(n)]
    inner = [refs.pop(0) for _ in range(chunks)]
    outer = [refs.pop(0) for _ in range(chunks)]
    acc = refs.pop(0) if with_acc else None
    if with_acc:
        g, out, rows, held, sems, total = refs
    else:
        g, total, rows, held, sems = refs
    t, unit = pieces[0].shape[0], pieces[0].shape[1] // 2
    ends = [0]
    for x in inner:
        ends.append(ends[-1] + x.shape[1])
    count = ends[-1] // unit

    def prepare():
        for j, half in [(j, half) for j in range(n) for half in range(2)]:
            place = half * n + off[j] - begin

            @pl.when((place >= 0) & (place < count))
            def _():
                here = pl.ds(pl.multiple_of(place * unit, unit), unit)
                rows[:t, here] = pieces[j][:, half * unit : (half + 1) * unit]

        for j in range(chunks):
            here = slice(ends[j], ends[j + 1])

            @pl.when(off[n] == 1)
            def _():
                rows[t:, here] = inner[j][...]

            @pl.when(off[n] == 0)
            def _():
                rows[t:, here] = outer[j][...]

        if with_acc:
            total[...] = acc[...]

    forward_loop(
        g, rows, total, held, sems, lambda j: begin + j, unit, count, True, not with_acc, prepare
    )
    if with_acc:
        split_people(out, total, 0)


def wide_forward(pieces, inner, outer, places, begin, acc, genotypes, columns, name):
    people = genotypes.shape[0]
    n, t, unit = len(pieces), pieces[0].shape[0], pieces[0].shape[1] // 2
    r = t + inner[0].shape[0]
    pb, kb = block_of(people, 1024), block_of(unit, 2048)
    operands = [*pieces, *inner, *outer, *([] if acc is None else [acc]), genotypes]
    span = sum(x.shape[1] for x in inner)
    scratch = [pltpu.VMEM((r, span), BF16), *ring(pb, kb)]
    if acc is None:
        shape = jax.ShapeDtypeStruct((people, r), F32)
    else:
        shape = jax.ShapeDtypeStruct((columns, r, people // columns), BF16)
        scratch.append(pltpu.VMEM((people, r), F32))
    return pl.pallas_call(
        functools.partial(wide_body, n, begin, len(inner), acc is not None),
        grid_spec=pltpu.PrefetchScalarGridSpec(
            num_scalar_prefetch=1,
            grid=(),
            in_specs=[VMEM] * (len(operands) - 1) + [ANY],
            out_specs=VMEM,
            scratch_shapes=scratch,
        ),
        out_shape=shape,
        compiler_params=pltpu.CompilerParams(vmem_limit_bytes=LIMIT),
        cost_estimate=cost(r, people, span),
        name=name,
    )(places, *operands)


def backward_loop(g, rows, total, held, sems, off, span, pieces):
    people = g.shape[0]
    slots, pk, mb = held.shape
    steps, blocks = span // mb, people // pk

    def place(c):
        k, i = c // blocks, lax.rem(c, blocks)
        col = off[k // steps] * span + lax.rem(k, steps) * mb
        return g.at[pl.ds(pl.multiple_of(i * pk, pk), pk), pl.ds(pl.multiple_of(col, mb), mb)]

    def use(c, slot):
        k, i = c // blocks, lax.rem(c, blocks)
        here = pl.ds(pl.multiple_of(k * mb, mb), mb)
        d = rows[:, pl.ds(pl.multiple_of(i * pk, pk), pk)]
        value = jnp.dot(d, slot[...], preferred_element_type=F32)

        @pl.when(i == 0)
        def _():
            total[:, here] = value

        @pl.when(i > 0)
        def _():
            total[:, here] += value

    stream(place, held, sems, pieces * steps * blocks, lambda: None, use)


def back_body(n, unit, t, base, cut, off, rows, g, *refs):
    refs = list(refs)
    held, sems = refs[-2:]
    if t == rows.shape[0]:
        outs, total = refs[:-3], refs[-3]
    else:
        outs, (lower, upper, total, made, sent) = refs[:-7], refs[-7:-2]
    backward_loop(g, rows, total, held, sems, off, unit, n)
    copies = []
    if t != rows.shape[0]:
        made[...] = total[t:, :].astype(BF16)
        for j in range(n):
            place = off[j] - base
            part = made.at[:, pl.ds(j * unit, unit)]

            def copy(whole, first):
                cols = pl.ds(pl.multiple_of((place - first) * unit, unit), unit)
                return pltpu.make_async_copy(part, whole.at[:, cols], sent.at[j])

            @pl.when(place < cut)
            def _():
                copy(lower, 0).start()

            @pl.when(place >= cut)
            def _():
                copy(upper, cut).start()

            copies.append(pltpu.make_async_copy(part, lower.at[:, pl.ds(0, unit)], sent.at[j]))
    span = outs[0].shape[1]
    for j, out in enumerate(outs):
        out[...] = total[:t, j * span : (j + 1) * span]
    for copy in copies:
        copy.wait()


def backward(rows, places, genotypes, unit, t, base, cut, arrays, name):
    people = genotypes.shape[0]
    r, n = rows.shape[0], places.shape[0]
    pk, mb = block_of(people, 1024), block_of(unit, 2048)
    out_specs = [VMEM] * arrays
    out_shape = [jax.ShapeDtypeStruct((t, n * unit // arrays), F32)] * arrays
    scratch = [pltpu.VMEM((r, n * unit), F32)]
    if t != r:
        out_specs += [ANY] * 2
        out_shape += [jax.ShapeDtypeStruct((r - t, c * unit), BF16) for c in (cut, n - cut)]
        scratch += [pltpu.VMEM((r - t, n * unit), BF16), pltpu.SemaphoreType.DMA((n,))]
    return pl.pallas_call(
        functools.partial(back_body, n, unit, t, base, cut),
        grid_spec=pltpu.PrefetchScalarGridSpec(
            num_scalar_prefetch=1,
            grid=(),
            in_specs=[VMEM, ANY],
            out_specs=out_specs,
            scratch_shapes=[*scratch, *ring(pk, mb)],
        ),
        out_shape=out_shape,
        compiler_params=pltpu.CompilerParams(vmem_limit_bytes=LIMIT),
        cost_estimate=cost(r, people, n * unit),
        name=name,
    )(places, rows, genotypes)


def finish_body(n, copies, off, sums, wide_cols, cols, centre, *refs):
    start_hi, back_hi, low = refs[:n], refs[n : 2 * n], refs[2 * n : 3 * n]
    estimate, lmmse = refs[3 * n :]
    t, unit = start_hi[0].shape[0], start_hi[0].shape[1] // 2
    norm_start, du, uu, xx, xw, ww = [sums[:, j : j + 1] for j in range(6)]
    tau, gamma = wide_cols[:, 0:1], wide_cols[:, 1:2]
    second_precision, slab_var, odds = [cols[:, j : j + 1] for j in range(3)]

    step_0 = norm_start / (tau * du + gamma * norm_start)
    left, b = 1.0 - step_0 * gamma, step_0 * tau
    norm_next = left * left * norm_start - 2.0 * left * b * du + b * b * uu
    a = left + norm_next / norm_start
    dir_norm = a * a * norm_start - 2.0 * a * b * du + b * b * uu
    dir_square = a * a * xx - 2.0 * a * b * xw + b * b * ww
    step_1 = norm_next / (tau * dir_square + gamma * dir_norm)

    start_coef = (step_0 + step_1 * a)[:t]
    back_coef = (step_1 * b)[:t]
    dots = step_0 * norm_start + step_1 * (a * norm_start - b * du)
    probe_dot = sum(dots[i * t : (i + 1) * t] for i in range(1, copies))
    probe_norm = sum(norm_start[i * t : (i + 1) * t] for i in range(1, copies))
    second_slope = second_precision * probe_dot / (probe_norm + 1e-06)
    next_precision = second_precision * (1.0 - second_slope) / second_slope
    next_shrink = slab_var * next_precision / (1.0 + slab_var * next_precision)
    next_base = odds + 0.5 * jnp.log(1.0 - next_shrink)
    for j, half in [(j, half) for j in range(n) for half in range(2)]:
        here = pl.ds(pl.multiple_of((half * n + off[j]) * unit, unit), unit)
        part = slice(half * unit, (half + 1) * unit)
        start = start_hi[j][:, part].astype(F32) + low[j][:, part].astype(F32)
        back = back_hi[j][:, part].astype(F32)
        middle = centre[:, here]
        made = middle + start_coef * start - back_coef * back
        lmmse[:, here] = made
        next_message = (made - second_slope * middle) / (1.0 - second_slope)
        value, _ = denoise(next_message, next_precision, next_shrink, next_base)
        estimate[:, here] = value


def finish(places, sums, wide_cols, cols, centre, start_hi, back_hi, low):
    n = len(low)
    shape = jax.ShapeDtypeStruct(centre.shape, F32)
    copies = sums.shape[0] // centre.shape[0]
    operands = [sums, wide_cols, cols, centre, *start_hi, *back_hi, *low]
    return pl.pallas_call(
        functools.partial(finish_body, n, copies),
        grid_spec=pltpu.PrefetchScalarGridSpec(
            num_scalar_prefetch=1, grid=(), in_specs=[VMEM] * len(operands), out_specs=[VMEM, VMEM]
        ),
        out_shape=[shape, shape],
        compiler_params=pltpu.CompilerParams(vmem_limit_bytes=LIMIT),
        name="finish",
    )(places, *operands)


def per_device(
    genotypes, phenotypes, message, probes, inclusion, slab_ratio, input_precision, noise_precision
):
    samples, columns = lax.axis_size("sample"), lax.axis_size("marker")
    people_here, markers_here = genotypes.shape
    people, markers = people_here * samples, markers_here * columns
    traits = message.shape[0]
    copies = probes.shape[0] // traits + 1
    me, column = lax.axis_index("sample"), lax.axis_index("marker")
    unit, share = markers_here // (2 * samples), people_here // columns
    order = jnp.arange(samples, dtype=jnp.int32) ^ me
    some = samples // 2
    near, far = [jnp.stack([o, o + samples], axis=1).reshape(-1) for o in (order[:some], order[some:])]

    cols = jnp.stack([inclusion, slab_ratio, input_precision], axis=1)
    slopes = slope_sum(message, cols)
    slopes = slopes + swap(slopes, "marker", 1)
    probes_b = lax.optimization_barrier((probes, slopes))[0].astype(BF16)
    slopes = sum_direct(slopes, "marker", 2)
    value, centre = first_forward(message, cols, slopes, probes_b, genotypes, columns)
    kept_x = jnp.sum(lax.all_to_all(value, "marker", 0, 0).astype(F32), axis=0)
    kept_x, low_x = kept_x[: traits * copies], kept_x[traits * copies :]
    own = lax.dynamic_slice_in_dim(phenotypes, column * share, share, 1) - (kept_x[:traits] + low_x)
    rows = jnp.concatenate([own, kept_x[traits:]], axis=0).astype(BF16)
    pred_x = rows[traits:].astype(F32)
    rows = lax.all_gather(rows, "marker", axis=1, tiled=True)
    starts, chunks = [], []
    for half, cut in enumerate((samples - 1, some)):
        base = half * samples
        *parts, lower, upper = backward(
            rows, order + base, genotypes, unit, traits, base, cut, samples, f"first_back_{half}"
        )
        starts.append([swap(part, "sample", k) if k else part for k, part in enumerate(parts)])
        chunks += [lower, upper]
        rows, *_ = lax.optimization_barrier((rows, lower))
    chunks = [chunks[0], jnp.concatenate(chunks[1:3], axis=1), chunks[3]]

    def add(x, y):
        return (x.astype(F32) + y.astype(F32)).astype(BF16)

    def tie(values, *others):
        return lax.optimization_barrier((tuple(values), others))[0]

    def hop(x, pairs, *others):
        y = lax.ppermute(x, "sample", pairs)
        return add(*tie((x, y), *others))

    def inward(c, *others):
        return hop(chunks[c], [(0, 1), (3, 2)], *others)

    def across(x, *others):
        return hop(x, [(1, 2), (2, 1)], *others)

    def outward(x):
        return lax.ppermute(x, "sample", [(1, 0), (2, 3)])

    pair, full, ends = [None] * 3, [None] * 3, [None] * 3
    pair[0] = inward(0)
    scale = (noise_precision / people)[:, None]
    start = scale * jnp.concatenate([tree(parts) for parts in starts], axis=1)
    start_high = lax.reduce_precision(start, 8, 7)
    start_low = (start - start_high).astype(BF16)
    start_high = start_high.astype(BF16)

    start_pieces = [swap(start_high, "sample", k) if k else start_high for k in range(samples)]
    *start_pieces, pair[0], chunks[1] = tie((*start_pieces, pair[0], chunks[1]))
    full[0], pair[1] = across(pair[0]), inward(1)
    both = jnp.concatenate([near, far])
    value = narrow_forward(start_pieces, both, None, genotypes, "second_forward")
    value, chunks[2] = tie((value, chunks[2]), full[0], pair[1])
    ends[0], full[1], pair[2] = outward(full[0]), across(pair[1]), inward(2)
    value = sum_marker(value)
    kept_s = lax.dynamic_slice_in_dim(value, column * share, share, 1)
    rows = value.astype(BF16)
    parts = backward(rows, far, genotypes, unit, traits, 0, 0, some, "second_back_far")
    sent = [swap(part, "sample", k + some) for k, part in enumerate(parts)]
    (rows,) = tie((rows,), full[1], pair[2], ends[0], *parts)
    ends[1] = outward(full[1])
    parts = backward(rows, near, genotypes, unit, traits, 0, 0, some, "second_back_near")
    sent = [swap(part, "sample", k) if k else part for k, part in enumerate(parts)] + sent
    back_high = tree(list(tie(sent, ends[1]))).astype(BF16)
    back = back_high.astype(F32)
    back_pieces = [swap(back_high, "sample", k) if k else back_high for k in range(samples)]
    full[2] = across(pair[2], *back_pieces)
    ends[2] = outward(full[2])

    inner = ((me == 1) | (me == 2)).astype(jnp.int32)
    places = jnp.concatenate([order, inner[None]])
    total = wide_forward(
        back_pieces, full[:2], ends[:2], places, 0, None, genotypes, columns, "third_forward_0"
    )
    (start_low,) = tie((start_low,), total)
    low_pieces = [swap(start_low, "sample", k) if k else start_low for k in range(samples)]
    value = wide_forward(
        back_pieces, full[2:], ends[2:], places, 3 * some, total, genotypes, columns, "third_forward_1"
    )
    (last,) = tie((lax.all_to_all(value, "marker", 0, 0),), *low_pieces)
    last = jnp.sum(last.astype(F32), axis=0)
    before = jnp.concatenate([kept_s, kept_x[traits:]], axis=0)

    def dot(x, y):
        return jnp.sum(x * y, axis=1)

    probes_here = [
        lax.dynamic_slice_in_dim(probes, (half * samples + me) * unit, unit, 1) for half in range(2)
    ]
    kept_p, last_p = kept_x[traits:], last[traits:]
    norms = jnp.concatenate(
        [
            jnp.stack([dot(start, start), dot(start, back), dot(back, back)], axis=1),
            jnp.stack(
                [sum(dot(p, p) for p in probes_here), dot(kept_p, pred_x), dot(last_p, pred_x)], axis=1
            ),
        ],
        axis=0,
    )
    squares = jnp.stack([dot(before, before), dot(before, last), dot(last, last)], axis=1)
    sums = sum_direct(sum_marker(jnp.concatenate([norms, squares], axis=1)), "sample")

    first_slope = slopes[:, 0] / markers
    second_precision = input_precision * (1.0 - first_slope) / first_slope
    odds = jnp.log(inclusion / (1.0 - inclusion))
    wide_cols = jnp.stack(
        [jnp.tile(noise_precision / people, copies), jnp.tile(second_precision, copies)], axis=1
    )
    cols = jnp.stack([second_precision, slab_ratio / input_precision, odds], axis=1)
    return tuple(
        finish(order, sums, wide_cols, cols, centre, start_pieces, back_pieces, low_pieces)
    )


def solution(mesh):
    return jax.shard_map(
        per_device,
        mesh=mesh,
        in_specs=(
            P("sample", "marker"),
            P(None, "sample"),
            P(None, "marker"),
            P(None, "marker"),
            P(),
            P(),
            P(),
            P(),
        ),
        out_specs=(P(None, "marker"), P(None, "marker")),
        check_vma=False,
    )
```

```python
import functools

import jax
import jax.numpy as jnp
from jax import lax
from jax.experimental import pallas as pl
from jax.experimental.pallas import tpu as pltpu
from jax.sharding import PartitionSpec as P

F32 = jnp.float32
BF16 = jnp.bfloat16
LIMIT = 44 << 20
SLOTS = 4
VMEM = pl.BlockSpec(memory_space=pltpu.VMEM)
ANY = pl.BlockSpec(memory_space=pl.ANY)


def block_of(size, most):
    while size % most:
        most //= 2
    return most


def swap(x, axis, bits):
    n = lax.axis_size(axis)
    return lax.ppermute(x, axis, [(i, i ^ bits) for i in range(n)])


def tree(parts):
    while len(parts) > 1:
        parts = [parts[i] + parts[i + 1] for i in range(0, len(parts), 2)]
    return parts[0]


def sum_direct(x, axis, unit=1):
    n = lax.axis_size(axis)
    return tree([x if k == 0 else swap(x, axis, k) for k in range(0, n, unit)])


def sum_marker(x):
    return sum_direct(x + swap(x, "marker", 1), "marker", 2)


def denoise(signal, precision, shrink, logit_base):
    energy = shrink * precision * signal * signal
    weight = jax.nn.sigmoid(logit_base + 0.5 * energy)
    return (shrink * weight * signal, shrink * weight * (1.0 + (1.0 - weight) * energy))


def stream(place, held, sems, total, prepare, use):
    slots = held.shape[0]

    def copy(c):
        slot = lax.rem(c, slots)
        return pltpu.make_async_copy(place(c), held.at[slot], sems.at[slot])

    for c in range(min(slots, total)):
        copy(c).start()
    prepare()

    def step(c, carry):
        copy(c).wait()
        use(c, held.at[lax.rem(c, slots)])

        @pl.when(c + slots < total)
        def _():
            copy(c + slots).start()

        return carry

    lax.fori_loop(0, total, step, 0)


def ring(rows, columns):
    return [pltpu.VMEM((SLOTS, rows, columns), BF16), pltpu.SemaphoreType.DMA((SLOTS,))]


def forward_loop(g, rows, total, held, sems, unit_at, span, pieces, wide, fresh, prepare):
    people = g.shape[0]
    slots, pb, kb = held.shape
    steps, blocks = span // kb, people // pb

    def place(c):
        k, i = c // blocks, lax.rem(c, blocks)
        col = unit_at(k // steps) * span + lax.rem(k, steps) * kb
        return g.at[pl.ds(pl.multiple_of(i * pb, pb), pb), pl.ds(pl.multiple_of(col, kb), kb)]

    def use(c, slot):
        k, i = c // blocks, lax.rem(c, blocks)
        d = rows[:, pl.ds(pl.multiple_of(k * kb, kb), kb)]
        here = pl.ds(pl.multiple_of(i * pb, pb), pb)
        across = (((1,), (1,)), ((), ()))
        if wide:
            at = (here, slice(None))
            value = lax.dot_general(slot[...], d, across, preferred_element_type=F32)
        else:
            at = (slice(None), here)
            value = lax.dot_general(d, slot[...], across, preferred_element_type=F32)
        if fresh:

            @pl.when(k == 0)
            def _():
                total[at] = value

            @pl.when(k > 0)
            def _():
                total[at] += value

        else:
            total[at] += value

    stream(place, held, sems, pieces * steps * blocks, prepare, use)


def split_people(out, total, t):
    n, r, share = out.shape
    for b in range(n):
        value = total[b * share : (b + 1) * share, :].T
        high = value.astype(BF16)
        out[b, : r - t, :] = high
        if t:
            out[b, r - t :, :] = (value[:t] - high[:t].astype(F32)).astype(BF16)


def prior(cols):
    inclusion, ratio, precision = [cols[:, j : j + 1] for j in range(3)]
    shrink = ratio / (1.0 + ratio)
    base = jnp.log(inclusion / (1.0 - inclusion)) + 0.5 * jnp.log(1.0 - shrink)
    return precision, shrink, base


def slope_body(message, cols, out):
    _, slopes = denoise(message[...], *prior(cols))
    out[...] = jnp.sum(slopes, axis=1, keepdims=True)


def slope_sum(message, cols):
    return pl.pallas_call(
        slope_body,
        in_specs=[VMEM, VMEM],
        out_specs=VMEM,
        out_shape=jax.ShapeDtypeStruct((message.shape[0], 1), F32),
        compiler_params=pltpu.CompilerParams(vmem_limit_bytes=LIMIT),
        name="slope_sum",
    )(message, cols)


def first_body(markers, off, message, cols, slopes, probes, g, out, centre, rows, held, sems, total):
    t = message.shape[0]

    def prepare():
        slope = slopes[...] / markers
        first, _ = denoise(message[...], *prior(cols))
        made = (first - slope * message[...]) / (1.0 - slope)
        centre[...] = made
        rows[:t, :] = made.astype(BF16)
        rows[t:, :] = probes[...]

    forward_loop(g, rows, total, held, sems, lambda j: j, g.shape[1], 1, True, True, prepare)
    split_people(out, total, t)


def cost(rows, people, markers):
    return pl.CostEstimate(
        flops=2 * rows * people * markers, transcendentals=0, bytes_accessed=2 * people * markers
    )


def first_forward(message, cols, slopes, probes, genotypes, columns):
    people, markers = genotypes.shape
    t = message.shape[0]
    r = t + probes.shape[0]
    pb, kb = block_of(people, 1024), block_of(markers, 2048)
    return pl.pallas_call(
        functools.partial(first_body, markers * columns),
        grid_spec=pltpu.PrefetchScalarGridSpec(
            num_scalar_prefetch=1,
            grid=(),
            in_specs=[VMEM, VMEM, VMEM, VMEM, ANY],
            out_specs=[VMEM, VMEM],
            scratch_shapes=[
                pltpu.VMEM((r, markers), BF16),
                *ring(pb, kb),
                pltpu.VMEM((people, r), F32),
            ],
        ),
        out_shape=[
            jax.ShapeDtypeStruct((columns, r + t, people // columns), BF16),
            jax.ShapeDtypeStruct(message.shape, F32),
        ],
        compiler_params=pltpu.CompilerParams(vmem_limit_bytes=LIMIT),
        cost_estimate=cost(r, people, markers),
        name="first_forward",
    )(jnp.zeros((1,), jnp.int32), message, cols, slopes, probes, genotypes)


def narrow_body(n, unit, with_acc, off, *refs):
    refs = list(refs)
    pieces = [refs.pop(0) for _ in range(n)]
    acc = refs.pop(0) if with_acc else None
    g, out, rows, held, sems = refs
    span = pieces[0].shape[1]

    def prepare():
        for j in range(n):
            rows[:, j * span : (j + 1) * span] = pieces[j][...]
        if with_acc:
            out[...] = acc[...]

    count = n * span // unit
    forward_loop(
        g, rows, out, held, sems, lambda j: off[j], unit, count, False, not with_acc, prepare
    )


def narrow_forward(pieces, places, acc, genotypes, name):
    people = genotypes.shape[0]
    n, (t, span) = len(pieces), pieces[0].shape
    unit = n * span // places.shape[0]
    pb, kb = block_of(people, 1024), block_of(unit, 2048)
    operands = [*pieces, *([] if acc is None else [acc]), genotypes]
    return pl.pallas_call(
        functools.partial(narrow_body, n, unit, acc is not None),
        grid_spec=pltpu.PrefetchScalarGridSpec(
            num_scalar_prefetch=1,
            grid=(),
            in_specs=[VMEM] * (len(operands) - 1) + [ANY],
            out_specs=VMEM,
            scratch_shapes=[pltpu.VMEM((t, n * span), BF16), *ring(pb, kb)],
        ),
        out_shape=jax.ShapeDtypeStruct((t, people), F32),
        compiler_params=pltpu.CompilerParams(vmem_limit_bytes=LIMIT),
        cost_estimate=cost(t, people, n * span),
        name=name,
    )(places, *operands)


def wide_body(n, begin, chunks, chosen, with_acc, off, *refs):
    refs = list(refs)
    pieces = [refs.pop(0) for _ in range(n)]
    inner = [refs.pop(0) for _ in range(chunks)]
    outer = [refs.pop(0) if j in chosen else None for j in range(chunks)]
    acc = refs.pop(0) if with_acc else None
    if with_acc:
        g, out, rows, held, sems, total = refs
    else:
        g, total, rows, held, sems = refs
    t, unit = pieces[0].shape[0], pieces[0].shape[1] // 2
    ends = [0]
    for x in inner:
        ends.append(ends[-1] + x.shape[1])
    count = ends[-1] // unit

    def prepare():
        for j, half in [(j, half) for j in range(n) for half in range(2)]:
            place = half * n + off[j] - begin

            @pl.when((place >= 0) & (place < count))
            def _():
                here = pl.ds(pl.multiple_of(place * unit, unit), unit)
                rows[:t, here] = pieces[j][:, half * unit : (half + 1) * unit]

        for j in range(chunks):
            here = slice(ends[j], ends[j + 1])
            if outer[j] is None:
                rows[t:, here] = inner[j][...]
                continue

            @pl.when(off[n] == 1)
            def _():
                rows[t:, here] = inner[j][...]

            @pl.when(off[n] == 0)
            def _():
                rows[t:, here] = outer[j][...]

        if with_acc:
            total[...] = acc[...]

    forward_loop(
        g, rows, total, held, sems, lambda j: begin + j, unit, count, True, not with_acc, prepare
    )
    if with_acc:
        split_people(out, total, 0)


def wide_forward(pieces, inner, outer, places, begin, acc, genotypes, columns, name):
    people = genotypes.shape[0]
    n, t, unit = len(pieces), pieces[0].shape[0], pieces[0].shape[1] // 2
    r = t + inner[0].shape[0]
    pb, kb = block_of(people, 1024), block_of(unit, 2048)
    chosen = [j for j, x in enumerate(outer) if x is not None]
    outer = [outer[j] for j in chosen]
    operands = [*pieces, *inner, *outer, *([] if acc is None else [acc]), genotypes]
    span = sum(x.shape[1] for x in inner)
    scratch = [pltpu.VMEM((r, span), BF16), *ring(pb, kb)]
    if acc is None:
        shape = jax.ShapeDtypeStruct((people, r), F32)
    else:
        shape = jax.ShapeDtypeStruct((columns, r, people // columns), BF16)
        scratch.append(pltpu.VMEM((people, r), F32))
    return pl.pallas_call(
        functools.partial(wide_body, n, begin, len(inner), chosen, acc is not None),
        grid_spec=pltpu.PrefetchScalarGridSpec(
            num_scalar_prefetch=1,
            grid=(),
            in_specs=[VMEM] * (len(operands) - 1) + [ANY],
            out_specs=VMEM,
            scratch_shapes=scratch,
        ),
        out_shape=shape,
        compiler_params=pltpu.CompilerParams(vmem_limit_bytes=LIMIT),
        cost_estimate=cost(r, people, span),
        name=name,
    )(places, *operands)


def backward_loop(g, rows, total, held, sems, off, span, pieces):
    people = g.shape[0]
    slots, pk, mb = held.shape
    steps, blocks = span // mb, people // pk

    def place(c):
        k, i = c // blocks, lax.rem(c, blocks)
        col = off[k // steps] * span + lax.rem(k, steps) * mb
        return g.at[pl.ds(pl.multiple_of(i * pk, pk), pk), pl.ds(pl.multiple_of(col, mb), mb)]

    def use(c, slot):
        k, i = c // blocks, lax.rem(c, blocks)
        here = pl.ds(pl.multiple_of(k * mb, mb), mb)
        d = rows[:, pl.ds(pl.multiple_of(i * pk, pk), pk)]
        value = jnp.dot(d, slot[...], preferred_element_type=F32)

        @pl.when(i == 0)
        def _():
            total[:, here] = value

        @pl.when(i > 0)
        def _():
            total[:, here] += value

    stream(place, held, sems, pieces * steps * blocks, lambda: None, use)


def back_body(n, unit, t, base, cut, off, rows, g, *refs):
    refs = list(refs)
    held, sems = refs[-2:]
    if t == rows.shape[0]:
        outs, total = refs[:-3], refs[-3]
    else:
        total, made, sent = refs[-5:-2]
        outs, (lower, upper) = (refs[:-7], refs[-7:-5]) if cut < n else (refs[:-6], [refs[-6]] * 2)
    backward_loop(g, rows, total, held, sems, off, unit, n)
    copies = []
    if t != rows.shape[0]:
        made[...] = total[t:, :].astype(BF16)
        for j in range(n):
            place = off[j] - base
            part = made.at[:, pl.ds(j * unit, unit)]

            def copy(whole, first):
                cols = pl.ds(pl.multiple_of((place - first) * unit, unit), unit)
                return pltpu.make_async_copy(part, whole.at[:, cols], sent.at[j])

            @pl.when(place < cut)
            def _():
                copy(lower, 0).start()

            @pl.when(place >= cut)
            def _():
                copy(upper, cut).start()

            copies.append(pltpu.make_async_copy(part, lower.at[:, pl.ds(0, unit)], sent.at[j]))
    span = outs[0].shape[1]
    for j, out in enumerate(outs):
        out[...] = total[:t, j * span : (j + 1) * span]
    for copy in copies:
        copy.wait()


def backward(rows, places, genotypes, unit, t, base, cut, arrays, name):
    people = genotypes.shape[0]
    r, n = rows.shape[0], places.shape[0]
    pk, mb = block_of(people, 1024), block_of(unit, 2048)
    out_specs = [VMEM] * arrays
    out_shape = [jax.ShapeDtypeStruct((t, n * unit // arrays), F32)] * arrays
    scratch = [pltpu.VMEM((r, n * unit), F32)]
    if t != r:
        sizes = [c for c in (cut, n - cut) if c]
        out_specs += [ANY] * len(sizes)
        out_shape += [jax.ShapeDtypeStruct((r - t, c * unit), BF16) for c in sizes]
        scratch += [pltpu.VMEM((r - t, n * unit), BF16), pltpu.SemaphoreType.DMA((n,))]
    return pl.pallas_call(
        functools.partial(back_body, n, unit, t, base, cut),
        grid_spec=pltpu.PrefetchScalarGridSpec(
            num_scalar_prefetch=1,
            grid=(),
            in_specs=[VMEM, ANY],
            out_specs=out_specs,
            scratch_shapes=[*scratch, *ring(pk, mb)],
        ),
        out_shape=out_shape,
        compiler_params=pltpu.CompilerParams(vmem_limit_bytes=LIMIT),
        cost_estimate=cost(r, people, n * unit),
        name=name,
    )(places, rows, genotypes)


def finish_body(n, copies, off, sums, wide_cols, cols, centre, *refs):
    start_hi, back_hi, low = refs[:n], refs[n : 2 * n], refs[2 * n : 3 * n]
    estimate, lmmse = refs[3 * n :]
    t, unit = start_hi[0].shape[0], start_hi[0].shape[1] // 2
    sums = sums[...].T
    norm_start, du, uu, xx, xw, ww = [sums[:, j : j + 1] for j in range(6)]
    tau, gamma = wide_cols[:, 0:1], wide_cols[:, 1:2]
    second_precision, slab_var, odds = [cols[:, j : j + 1] for j in range(3)]

    step_0 = norm_start / (tau * du + gamma * norm_start)
    left, b = 1.0 - step_0 * gamma, step_0 * tau
    norm_next = left * left * norm_start - 2.0 * left * b * du + b * b * uu
    a = left + norm_next / norm_start
    dir_norm = a * a * norm_start - 2.0 * a * b * du + b * b * uu
    dir_square = a * a * xx - 2.0 * a * b * xw + b * b * ww
    step_1 = norm_next / (tau * dir_square + gamma * dir_norm)

    start_coef = (step_0 + step_1 * a)[:t]
    back_coef = (step_1 * b)[:t]
    dots = step_0 * norm_start + step_1 * (a * norm_start - b * du)
    probe_dot = sum(dots[i * t : (i + 1) * t] for i in range(1, copies))
    probe_norm = sum(norm_start[i * t : (i + 1) * t] for i in range(1, copies))
    second_slope = second_precision * probe_dot / (probe_norm + 1e-06)
    next_precision = second_precision * (1.0 - second_slope) / second_slope
    next_shrink = slab_var * next_precision / (1.0 + slab_var * next_precision)
    next_base = odds + 0.5 * jnp.log(1.0 - next_shrink)
    for j, half in [(j, half) for j in range(n) for half in range(2)]:
        here = pl.ds(pl.multiple_of((half * n + off[j]) * unit, unit), unit)
        part = slice(half * unit, (half + 1) * unit)
        start = start_hi[j][:, part].astype(F32) + low[j][:, part].astype(F32)
        back = back_hi[j][:, part].astype(F32)
        middle = centre[:, here]
        made = middle + start_coef * start - back_coef * back
        lmmse[:, here] = made
        next_message = (made - second_slope * middle) / (1.0 - second_slope)
        value, _ = denoise(next_message, next_precision, next_shrink, next_base)
        estimate[:, here] = value


def finish(places, sums, wide_cols, cols, centre, start_hi, back_hi, low):
    n = len(low)
    shape = jax.ShapeDtypeStruct(centre.shape, F32)
    copies = sums.shape[1] // centre.shape[0]
    operands = [sums, wide_cols, cols, centre, *start_hi, *back_hi, *low]
    return pl.pallas_call(
        functools.partial(finish_body, n, copies),
        grid_spec=pltpu.PrefetchScalarGridSpec(
            num_scalar_prefetch=1, grid=(), in_specs=[VMEM] * len(operands), out_specs=[VMEM, VMEM]
        ),
        out_shape=[shape, shape],
        compiler_params=pltpu.CompilerParams(vmem_limit_bytes=LIMIT),
        name="finish",
    )(places, *operands)


def per_device(
    genotypes, phenotypes, message, probes, inclusion, slab_ratio, input_precision, noise_precision
):
    samples, columns = lax.axis_size("sample"), lax.axis_size("marker")
    people_here, markers_here = genotypes.shape
    people, markers = people_here * samples, markers_here * columns
    traits = message.shape[0]
    copies = probes.shape[0] // traits + 1
    me, column = lax.axis_index("sample"), lax.axis_index("marker")
    unit, share = markers_here // (2 * samples), people_here // columns
    order = jnp.arange(samples, dtype=jnp.int32) ^ me
    some = samples // 2
    near, far = [jnp.stack([o, o + samples], axis=1).reshape(-1) for o in (order[:some], order[some:])]

    cols = jnp.stack([inclusion, slab_ratio, input_precision], axis=1)
    slopes = slope_sum(message, cols)
    slopes = slopes + swap(slopes, "marker", 1)
    probes_b = lax.optimization_barrier((probes, slopes))[0].astype(BF16)
    slopes = sum_direct(slopes, "marker", 2)
    value, centre = first_forward(message, cols, slopes, probes_b, genotypes, columns)
    kept_x = jnp.sum(lax.all_to_all(value, "marker", 0, 0).astype(F32), axis=0)
    kept_x, low_x = kept_x[: traits * copies], kept_x[traits * copies :]
    own = lax.dynamic_slice_in_dim(phenotypes, column * share, share, 1) - (kept_x[:traits] + low_x)
    rows = jnp.concatenate([own, kept_x[traits:]], axis=0).astype(BF16)
    pred_x = rows[traits:].astype(F32)
    rows = lax.all_gather(rows, "marker", axis=1, tiled=True)
    starts, chunks = [], []
    for half, cut in enumerate((samples, some)):
        base = half * samples
        outs = backward(
            rows, order + base, genotypes, unit, traits, base, cut, samples, f"first_back_{half}"
        )
        parts = outs[:samples]
        starts.append([swap(part, "sample", k) if k else part for k, part in enumerate(parts)])
        chunks += outs[samples:]
        rows, *_ = lax.optimization_barrier((rows, outs[-1]))

    first_half = lax.psum_scatter(chunks[0], "sample", scatter_dimension=1, tiled=True)

    def add(x, y):
        return (x.astype(F32) + y.astype(F32)).astype(BF16)

    def tie(values, *others):
        return lax.optimization_barrier((tuple(values), others))[0]

    def hop(x, pairs, *others):
        y = lax.ppermute(x, "sample", pairs)
        return add(*tie((x, y), *others))

    def inward(c, *others):
        return hop(chunks[c], [(0, 1), (3, 2)], *others)

    def across(x, *others):
        return hop(x, [(1, 2), (2, 1)], *others)

    def outward(x):
        return lax.ppermute(x, "sample", [(1, 0), (2, 3)])

    pair, full, ends = [None] * 3, [None] * 3, [None] * 3
    scale = (noise_precision / people)[:, None]
    start = scale * jnp.concatenate([tree(parts) for parts in starts], axis=1)
    start_high = lax.reduce_precision(start, 8, 7)
    start_low = (start - start_high).astype(BF16)
    start_high = start_high.astype(BF16)

    start_pieces = [swap(start_high, "sample", k) if k else start_high for k in range(samples)]
    *start_pieces, chunks[1], chunks[2], first_half = tie((*start_pieces, chunks[1], chunks[2], first_half))
    first_half = lax.all_gather(first_half, "sample", axis=1, tiled=True)
    pair[1] = inward(1)
    both = jnp.concatenate([near, far])
    value = narrow_forward(start_pieces, both, None, genotypes, "second_forward")
    value, pair[1], chunks[2], start_low = tie((value, pair[1], chunks[2], start_low))
    full[1], pair[2] = across(pair[1]), inward(2)
    low_pieces = [swap(start_low, "sample", k) if k else start_low for k in range(samples)]
    value = sum_marker(value)
    kept_s = lax.dynamic_slice_in_dim(value, column * share, share, 1)
    rows = value.astype(BF16)
    parts = backward(rows, far, genotypes, unit, traits, 0, 0, some, "second_back_far")
    sent = [swap(part, "sample", k + some) for k, part in enumerate(parts)]
    (rows,) = tie((rows,), full[1], pair[2], *low_pieces, first_half, *parts)
    ends[1] = outward(full[1])
    parts = backward(rows, near, genotypes, unit, traits, 0, 0, some, "second_back_near")
    sent = [swap(part, "sample", k) if k else part for k, part in enumerate(parts)] + sent
    back_high = tree(list(tie(sent, ends[1]))).astype(BF16)
    back = back_high.astype(F32)
    back_pieces = [swap(back_high, "sample", k) if k else back_high for k in range(samples)]
    full[2] = across(pair[2], *back_pieces)
    ends[2] = outward(full[2])

    inner = ((me == 1) | (me == 2)).astype(jnp.int32)
    places = jnp.concatenate([order, inner[None]])
    total = wide_forward(
        back_pieces, [first_half, full[1]], [None, ends[1]], places, 0, None, genotypes, columns, "third_forward_0"
    )
    value = wide_forward(
        back_pieces, full[2:], ends[2:], places, 3 * some, total, genotypes, columns, "third_forward_1"
    )
    last = lax.all_to_all(value, "marker", 0, 0)
    last = jnp.sum(last.astype(F32), axis=0)
    before = jnp.concatenate([kept_s, kept_x[traits:]], axis=0)

    def dot(x, y):
        return jnp.sum(x * y, axis=1)

    probes_here = [
        lax.dynamic_slice_in_dim(probes, (half * samples + me) * unit, unit, 1) for half in range(2)
    ]
    kept_p, last_p = kept_x[traits:], last[traits:]
    norms = jnp.concatenate(
        [
            jnp.stack([dot(start, start), dot(start, back), dot(back, back)]),
            jnp.stack([sum(dot(p, p) for p in probes_here), dot(kept_p, pred_x), dot(last_p, pred_x)]),
        ],
        axis=1,
    )
    squares = jnp.stack([dot(before, before), dot(before, last), dot(last, last)])
    sums = jnp.concatenate([norms, squares, jnp.zeros((2, norms.shape[1]), F32)], axis=0)
    sums = sum_direct(sum_marker(sums), "sample")

    first_slope = slopes[:, 0] / markers
    second_precision = input_precision * (1.0 - first_slope) / first_slope
    odds = jnp.log(inclusion / (1.0 - inclusion))
    wide_cols = jnp.stack(
        [jnp.tile(noise_precision / people, copies), jnp.tile(second_precision, copies)], axis=1
    )
    cols = jnp.stack([second_precision, slab_ratio / input_precision, odds], axis=1)
    return tuple(
        finish(order, sums, wide_cols, cols, centre, start_pieces, back_pieces, low_pieces)
    )


def solution(mesh):
    return jax.shard_map(
        per_device,
        mesh=mesh,
        in_specs=(
            P("sample", "marker"),
            P(None, "sample"),
            P(None, "marker"),
            P(None, "marker"),
            P(),
            P(),
            P(),
            P(),
        ),
        out_specs=(P(None, "marker"), P(None, "marker")),
        check_vma=False,
    )
```

```python
import functools

import jax
import jax.numpy as jnp
from jax import lax
from jax.experimental import pallas as pl
from jax.experimental.pallas import tpu as pltpu
from jax.sharding import PartitionSpec as P

F32 = jnp.float32
BF16 = jnp.bfloat16
LIMIT = 44 << 20
SLOTS = 4
VMEM = pl.BlockSpec(memory_space=pltpu.VMEM)
ANY = pl.BlockSpec(memory_space=pl.ANY)


def block_of(size, most):
    while size % most:
        most //= 2
    return most


def swap(x, axis, bits):
    n = lax.axis_size(axis)
    return lax.ppermute(x, axis, [(i, i ^ bits) for i in range(n)])


def tree(parts):
    while len(parts) > 1:
        parts = [parts[i] + parts[i + 1] for i in range(0, len(parts), 2)]
    return parts[0]


def sum_direct(x, axis, unit=1):
    n = lax.axis_size(axis)
    return tree([x if k == 0 else swap(x, axis, k) for k in range(0, n, unit)])


def sum_marker(x):
    return sum_direct(x + swap(x, "marker", 1), "marker", 2)


def denoise(signal, precision, shrink, logit_base):
    energy = shrink * precision * signal * signal
    weight = jax.nn.sigmoid(logit_base + 0.5 * energy)
    return (shrink * weight * signal, shrink * weight * (1.0 + (1.0 - weight) * energy))


def stream(place, held, sems, total, prepare, use):
    slots = held.shape[0]

    def copy(c):
        slot = lax.rem(c, slots)
        return pltpu.make_async_copy(place(c), held.at[slot], sems.at[slot])

    for c in range(min(slots, total)):
        copy(c).start()
    prepare()

    def step(c, carry):
        copy(c).wait()
        use(c, held.at[lax.rem(c, slots)])

        @pl.when(c + slots < total)
        def _():
            copy(c + slots).start()

        return carry

    lax.fori_loop(0, total, step, 0)


def ring(rows, columns):
    return [pltpu.VMEM((SLOTS, rows, columns), BF16), pltpu.SemaphoreType.DMA((SLOTS,))]


def forward_loop(g, rows, total, held, sems, unit_at, span, pieces, wide, fresh, prepare):
    people = g.shape[0]
    slots, pb, kb = held.shape
    steps, blocks = span // kb, people // pb

    def place(c):
        k, i = c // blocks, lax.rem(c, blocks)
        col = unit_at(k // steps) * span + lax.rem(k, steps) * kb
        return g.at[pl.ds(pl.multiple_of(i * pb, pb), pb), pl.ds(pl.multiple_of(col, kb), kb)]

    def use(c, slot):
        k, i = c // blocks, lax.rem(c, blocks)
        d = rows[:, pl.ds(pl.multiple_of(k * kb, kb), kb)]
        here = pl.ds(pl.multiple_of(i * pb, pb), pb)
        across = (((1,), (1,)), ((), ()))
        if wide:
            at = (here, slice(None))
            value = lax.dot_general(slot[...], d, across, preferred_element_type=F32)
        else:
            at = (slice(None), here)
            value = lax.dot_general(d, slot[...], across, preferred_element_type=F32)
        if fresh:

            @pl.when(k == 0)
            def _():
                total[at] = value

            @pl.when(k > 0)
            def _():
                total[at] += value

        else:
            total[at] += value

    stream(place, held, sems, pieces * steps * blocks, prepare, use)


def split_people(out, total, t):
    n, r, share = out.shape
    for b in range(n):
        value = total[b * share : (b + 1) * share, :].T
        high = value.astype(BF16)
        out[b, : r - t, :] = high
        if t:
            out[b, r - t :, :] = (value[:t] - high[:t].astype(F32)).astype(BF16)


def prior(cols):
    inclusion, ratio, precision = [cols[:, j : j + 1] for j in range(3)]
    shrink = ratio / (1.0 + ratio)
    base = jnp.log(inclusion / (1.0 - inclusion)) + 0.5 * jnp.log(1.0 - shrink)
    return precision, shrink, base


def slope_body(message, cols, out):
    _, slopes = denoise(message[...], *prior(cols))
    out[...] = jnp.sum(slopes, axis=1, keepdims=True)


def slope_sum(message, cols):
    return pl.pallas_call(
        slope_body,
        in_specs=[VMEM, VMEM],
        out_specs=VMEM,
        out_shape=jax.ShapeDtypeStruct((message.shape[0], 1), F32),
        compiler_params=pltpu.CompilerParams(vmem_limit_bytes=LIMIT),
        name="slope_sum",
    )(message, cols)


def first_body(markers, off, message, cols, slopes, probes, g, out, centre, rows, held, sems, total):
    t = message.shape[0]

    def prepare():
        slope = slopes[...] / markers
        first, _ = denoise(message[...], *prior(cols))
        made = (first - slope * message[...]) / (1.0 - slope)
        centre[...] = made
        rows[:t, :] = made.astype(BF16)
        rows[t:, :] = probes[...]

    forward_loop(g, rows, total, held, sems, lambda j: j, g.shape[1], 1, True, True, prepare)
    split_people(out, total, t)


def cost(rows, people, markers):
    return pl.CostEstimate(
        flops=2 * rows * people * markers, transcendentals=0, bytes_accessed=2 * people * markers
    )


def first_forward(message, cols, slopes, probes, genotypes, columns):
    people, markers = genotypes.shape
    t = message.shape[0]
    r = t + probes.shape[0]
    pb, kb = block_of(people, 1024), block_of(markers, 2048)
    return pl.pallas_call(
        functools.partial(first_body, markers * columns),
        grid_spec=pltpu.PrefetchScalarGridSpec(
            num_scalar_prefetch=1,
            grid=(),
            in_specs=[VMEM, VMEM, VMEM, VMEM, ANY],
            out_specs=[VMEM, VMEM],
            scratch_shapes=[
                pltpu.VMEM((r, markers), BF16),
                *ring(pb, kb),
                pltpu.VMEM((people, r), F32),
            ],
        ),
        out_shape=[
            jax.ShapeDtypeStruct((columns, r + t, people // columns), BF16),
            jax.ShapeDtypeStruct(message.shape, F32),
        ],
        compiler_params=pltpu.CompilerParams(vmem_limit_bytes=LIMIT),
        cost_estimate=cost(r, people, markers),
        name="first_forward",
    )(jnp.zeros((1,), jnp.int32), message, cols, slopes, probes, genotypes)


def narrow_body(n, unit, with_acc, off, *refs):
    refs = list(refs)
    pieces = [refs.pop(0) for _ in range(n)]
    acc = refs.pop(0) if with_acc else None
    g, out, rows, held, sems = refs
    span = pieces[0].shape[1]

    def prepare():
        for j in range(n):
            rows[:, j * span : (j + 1) * span] = pieces[j][...]
        if with_acc:
            out[...] = acc[...]

    count = n * span // unit
    forward_loop(
        g, rows, out, held, sems, lambda j: off[j], unit, count, False, not with_acc, prepare
    )


def narrow_forward(pieces, places, acc, genotypes, name):
    people = genotypes.shape[0]
    n, (t, span) = len(pieces), pieces[0].shape
    unit = n * span // places.shape[0]
    pb, kb = block_of(people, 1024), block_of(unit, 2048)
    operands = [*pieces, *([] if acc is None else [acc]), genotypes]
    return pl.pallas_call(
        functools.partial(narrow_body, n, unit, acc is not None),
        grid_spec=pltpu.PrefetchScalarGridSpec(
            num_scalar_prefetch=1,
            grid=(),
            in_specs=[VMEM] * (len(operands) - 1) + [ANY],
            out_specs=VMEM,
            scratch_shapes=[pltpu.VMEM((t, n * span), BF16), *ring(pb, kb)],
        ),
        out_shape=jax.ShapeDtypeStruct((t, people), F32),
        compiler_params=pltpu.CompilerParams(vmem_limit_bytes=LIMIT),
        cost_estimate=cost(t, people, n * span),
        name=name,
    )(places, *operands)


def wide_body(n, begin, chunks, chosen, with_acc, off, *refs):
    refs = list(refs)
    pieces = [refs.pop(0) for _ in range(n)]
    inner = [refs.pop(0) for _ in range(chunks)]
    outer = [refs.pop(0) if j in chosen else None for j in range(chunks)]
    acc = refs.pop(0) if with_acc else None
    if with_acc:
        g, out, rows, held, sems, total = refs
    else:
        g, total, rows, held, sems = refs
    t, unit = pieces[0].shape[0], pieces[0].shape[1] // 2
    ends = [0]
    for x in inner:
        ends.append(ends[-1] + x.shape[1])
    count = ends[-1] // unit

    def prepare():
        for j, half in [(j, half) for j in range(n) for half in range(2)]:
            place = half * n + off[j] - begin

            @pl.when((place >= 0) & (place < count))
            def _():
                here = pl.ds(pl.multiple_of(place * unit, unit), unit)
                rows[:t, here] = pieces[j][:, half * unit : (half + 1) * unit]

        for j in range(chunks):
            here = slice(ends[j], ends[j + 1])
            if outer[j] is None:
                rows[t:, here] = inner[j][...]
                continue

            @pl.when(off[n] == 1)
            def _():
                rows[t:, here] = inner[j][...]

            @pl.when(off[n] == 0)
            def _():
                rows[t:, here] = outer[j][...]

        if with_acc:
            total[...] = acc[...]

    forward_loop(
        g, rows, total, held, sems, lambda j: begin + j, unit, count, True, not with_acc, prepare
    )
    if with_acc:
        split_people(out, total, 0)


def wide_forward(pieces, inner, outer, places, begin, acc, genotypes, columns, name):
    people = genotypes.shape[0]
    n, t, unit = len(pieces), pieces[0].shape[0], pieces[0].shape[1] // 2
    r = t + inner[0].shape[0]
    pb, kb = block_of(people, 1024), block_of(unit, 2048)
    chosen = [j for j, x in enumerate(outer) if x is not None]
    outer = [outer[j] for j in chosen]
    operands = [*pieces, *inner, *outer, *([] if acc is None else [acc]), genotypes]
    span = sum(x.shape[1] for x in inner)
    scratch = [pltpu.VMEM((r, span), BF16), *ring(pb, kb)]
    if acc is None:
        shape = jax.ShapeDtypeStruct((people, r), F32)
    else:
        shape = jax.ShapeDtypeStruct((columns, r, people // columns), BF16)
        scratch.append(pltpu.VMEM((people, r), F32))
    return pl.pallas_call(
        functools.partial(wide_body, n, begin, len(inner), chosen, acc is not None),
        grid_spec=pltpu.PrefetchScalarGridSpec(
            num_scalar_prefetch=1,
            grid=(),
            in_specs=[VMEM] * (len(operands) - 1) + [ANY],
            out_specs=VMEM,
            scratch_shapes=scratch,
        ),
        out_shape=shape,
        compiler_params=pltpu.CompilerParams(vmem_limit_bytes=LIMIT),
        cost_estimate=cost(r, people, span),
        name=name,
    )(places, *operands)


def backward_loop(g, rows, total, held, sems, off, span, pieces):
    people = g.shape[0]
    slots, pk, mb = held.shape
    steps, blocks = span // mb, people // pk

    def place(c):
        k, i = c // blocks, lax.rem(c, blocks)
        col = off[k // steps] * span + lax.rem(k, steps) * mb
        return g.at[pl.ds(pl.multiple_of(i * pk, pk), pk), pl.ds(pl.multiple_of(col, mb), mb)]

    def use(c, slot):
        k, i = c // blocks, lax.rem(c, blocks)
        here = pl.ds(pl.multiple_of(k * mb, mb), mb)
        d = rows[:, pl.ds(pl.multiple_of(i * pk, pk), pk)]
        value = jnp.dot(d, slot[...], preferred_element_type=F32)

        @pl.when(i == 0)
        def _():
            total[:, here] = value

        @pl.when(i > 0)
        def _():
            total[:, here] += value

    stream(place, held, sems, pieces * steps * blocks, lambda: None, use)


def back_body(n, unit, t, base, cut, off, rows, g, *refs):
    refs = list(refs)
    held, sems = refs[-2:]
    if t == rows.shape[0]:
        outs, total = refs[:-3], refs[-3]
    else:
        total, made, sent = refs[-5:-2]
        outs, (lower, upper) = (refs[:-7], refs[-7:-5]) if cut < n else (refs[:-6], [refs[-6]] * 2)
    backward_loop(g, rows, total, held, sems, off, unit, n)
    copies = []
    if t != rows.shape[0]:
        made[...] = total[t:, :].astype(BF16)
        for j in range(n):
            place = off[j] - base
            part = made.at[:, pl.ds(j * unit, unit)]

            def copy(whole, first):
                cols = pl.ds(pl.multiple_of((place - first) * unit, unit), unit)
                return pltpu.make_async_copy(part, whole.at[:, cols], sent.at[j])

            @pl.when(place < cut)
            def _():
                copy(lower, 0).start()

            @pl.when(place >= cut)
            def _():
                copy(upper, cut).start()

            copies.append(pltpu.make_async_copy(part, lower.at[:, pl.ds(0, unit)], sent.at[j]))
    span = outs[0].shape[1]
    for j, out in enumerate(outs):
        out[...] = total[:t, j * span : (j + 1) * span]
    for copy in copies:
        copy.wait()


def backward(rows, places, genotypes, unit, t, base, cut, arrays, name):
    people = genotypes.shape[0]
    r, n = rows.shape[0], places.shape[0]
    pk, mb = block_of(people, 1024), block_of(unit, 2048)
    out_specs = [VMEM] * arrays
    out_shape = [jax.ShapeDtypeStruct((t, n * unit // arrays), F32)] * arrays
    scratch = [pltpu.VMEM((r, n * unit), F32)]
    if t != r:
        sizes = [c for c in (cut, n - cut) if c]
        out_specs += [ANY] * len(sizes)
        out_shape += [jax.ShapeDtypeStruct((r - t, c * unit), BF16) for c in sizes]
        scratch += [pltpu.VMEM((r - t, n * unit), BF16), pltpu.SemaphoreType.DMA((n,))]
    return pl.pallas_call(
        functools.partial(back_body, n, unit, t, base, cut),
        grid_spec=pltpu.PrefetchScalarGridSpec(
            num_scalar_prefetch=1,
            grid=(),
            in_specs=[VMEM, ANY],
            out_specs=out_specs,
            scratch_shapes=[*scratch, *ring(pk, mb)],
        ),
        out_shape=out_shape,
        compiler_params=pltpu.CompilerParams(vmem_limit_bytes=LIMIT),
        cost_estimate=cost(r, people, n * unit),
        name=name,
    )(places, rows, genotypes)


def finish_body(n, copies, off, sums, wide_cols, cols, centre, *refs):
    start_hi, back_hi, low = refs[:n], refs[n : 2 * n], refs[2 * n : 3 * n]
    estimate, lmmse = refs[3 * n :]
    t, unit = start_hi[0].shape[0], start_hi[0].shape[1] // 2
    sums = sums[...].T
    norm_start, du, uu, xx, xw, ww = [sums[:, j : j + 1] for j in range(6)]
    tau, gamma = wide_cols[:, 0:1], wide_cols[:, 1:2]
    second_precision, slab_var, odds = [cols[:, j : j + 1] for j in range(3)]

    step_0 = norm_start / (tau * du + gamma * norm_start)
    left, b = 1.0 - step_0 * gamma, step_0 * tau
    norm_next = left * left * norm_start - 2.0 * left * b * du + b * b * uu
    a = left + norm_next / norm_start
    dir_norm = a * a * norm_start - 2.0 * a * b * du + b * b * uu
    dir_square = a * a * xx - 2.0 * a * b * xw + b * b * ww
    step_1 = norm_next / (tau * dir_square + gamma * dir_norm)

    start_coef = (step_0 + step_1 * a)[:t]
    back_coef = (step_1 * b)[:t]
    dots = step_0 * norm_start + step_1 * (a * norm_start - b * du)
    probe_dot = sum(dots[i * t : (i + 1) * t] for i in range(1, copies))
    probe_norm = sum(norm_start[i * t : (i + 1) * t] for i in range(1, copies))
    second_slope = second_precision * probe_dot / (probe_norm + 1e-06)
    next_precision = second_precision * (1.0 - second_slope) / second_slope
    next_shrink = slab_var * next_precision / (1.0 + slab_var * next_precision)
    next_base = odds + 0.5 * jnp.log(1.0 - next_shrink)
    for j, half in [(j, half) for j in range(n) for half in range(2)]:
        here = pl.ds(pl.multiple_of((half * n + off[j]) * unit, unit), unit)
        part = slice(half * unit, (half + 1) * unit)
        start = start_hi[j][:, part].astype(F32) + low[j][:, part].astype(F32)
        back = back_hi[j][:, part].astype(F32)
        middle = centre[:, here]
        made = middle + start_coef * start - back_coef * back
        lmmse[:, here] = made
        next_message = (made - second_slope * middle) / (1.0 - second_slope)
        value, _ = denoise(next_message, next_precision, next_shrink, next_base)
        estimate[:, here] = value


def finish(places, sums, wide_cols, cols, centre, start_hi, back_hi, low):
    n = len(low)
    shape = jax.ShapeDtypeStruct(centre.shape, F32)
    copies = sums.shape[1] // centre.shape[0]
    operands = [sums, wide_cols, cols, centre, *start_hi, *back_hi, *low]
    return pl.pallas_call(
        functools.partial(finish_body, n, copies),
        grid_spec=pltpu.PrefetchScalarGridSpec(
            num_scalar_prefetch=1, grid=(), in_specs=[VMEM] * len(operands), out_specs=[VMEM, VMEM]
        ),
        out_shape=[shape, shape],
        compiler_params=pltpu.CompilerParams(vmem_limit_bytes=LIMIT),
        name="finish",
    )(places, *operands)


def per_device(
    genotypes, phenotypes, message, probes, inclusion, slab_ratio, input_precision, noise_precision
):
    samples, columns = lax.axis_size("sample"), lax.axis_size("marker")
    people_here, markers_here = genotypes.shape
    people, markers = people_here * samples, markers_here * columns
    traits = message.shape[0]
    copies = probes.shape[0] // traits + 1
    me, column = lax.axis_index("sample"), lax.axis_index("marker")
    unit, share = markers_here // (2 * samples), people_here // columns
    order = jnp.arange(samples, dtype=jnp.int32) ^ me
    some = samples // 2
    near, far = [jnp.stack([o, o + samples], axis=1).reshape(-1) for o in (order[:some], order[some:])]

    cols = jnp.stack([inclusion, slab_ratio, input_precision], axis=1)
    slopes = slope_sum(message, cols)
    slopes = slopes + swap(slopes, "marker", 1)
    probes_b = lax.optimization_barrier((probes, slopes))[0].astype(BF16)
    slopes = sum_direct(slopes, "marker", 2)
    value, centre = first_forward(message, cols, slopes, probes_b, genotypes, columns)
    kept_x = jnp.sum(lax.all_to_all(value, "marker", 0, 0).astype(F32), axis=0)
    kept_x, low_x = kept_x[: traits * copies], kept_x[traits * copies :]
    own = lax.dynamic_slice_in_dim(phenotypes, column * share, share, 1) - (kept_x[:traits] + low_x)
    rows = jnp.concatenate([own, kept_x[traits:]], axis=0).astype(BF16)
    pred_x = rows[traits:].astype(F32)
    rows = lax.all_gather(rows, "marker", axis=1, tiled=True)
    starts, chunks = [], []
    for half, cut in enumerate((samples, some)):
        base = half * samples
        outs = backward(
            rows, order + base, genotypes, unit, traits, base, cut, samples, f"first_back_{half}"
        )
        parts = outs[:samples]
        starts.append([swap(part, "sample", k) if k else part for k, part in enumerate(parts)])
        chunks += outs[samples:]
        rows, *_ = lax.optimization_barrier((rows, outs[-1]))

    first_half = lax.psum_scatter(chunks[0], "sample", scatter_dimension=1, tiled=True)

    def add(x, y):
        return (x.astype(F32) + y.astype(F32)).astype(BF16)

    def tie(values, *others):
        return lax.optimization_barrier((tuple(values), others))[0]

    def hop(x, pairs, *others):
        y = lax.ppermute(x, "sample", pairs)
        return add(*tie((x, y), *others))

    def inward(c, *others):
        return hop(chunks[c], [(0, 1), (3, 2)], *others)

    def across(x, *others):
        return hop(x, [(1, 2), (2, 1)], *others)

    def outward(x):
        return lax.ppermute(x, "sample", [(1, 0), (2, 3)])

    pair, full, ends = [None] * 3, [None] * 3, [None] * 3
    scale = (noise_precision / people)[:, None]
    start = scale * jnp.concatenate([tree(parts) for parts in starts], axis=1)
    start_high = lax.reduce_precision(start, 8, 7)
    start_low = (start - start_high).astype(BF16)
    start_high = start_high.astype(BF16)

    start_pieces = [swap(start_high, "sample", k) if k else start_high for k in range(samples)]
    *start_pieces, chunks[1], chunks[2], start_low, first_half = tie(
        (*start_pieces, chunks[1], chunks[2], start_low, first_half)
    )
    first_half = lax.all_gather(first_half, "sample", axis=1, tiled=True)
    pair[1] = inward(1)
    low_pieces = [swap(start_low, "sample", k) if k else start_low for k in range(samples)]
    both = jnp.concatenate([near, far])
    value = narrow_forward(start_pieces, both, None, genotypes, "second_forward")
    value, pair[1], chunks[2], *low_pieces = tie((value, pair[1], chunks[2], *low_pieces))
    value = sum_marker(value)
    kept_s = lax.dynamic_slice_in_dim(value, column * share, share, 1)
    rows = value.astype(BF16)
    (rows,) = tie((rows,), first_half)
    parts = backward(rows, far, genotypes, unit, traits, 0, 0, some, "second_back_far")
    sent = [swap(part, "sample", k + some) for k, part in enumerate(parts)]
    full[1], pair[2] = across(pair[1], *parts), inward(2, *parts)
    (rows,) = tie((rows,), full[1], pair[2], *parts)
    ends[1] = outward(full[1])
    parts = backward(rows, near, genotypes, unit, traits, 0, 0, some, "second_back_near")
    sent = [swap(part, "sample", k) if k else part for k, part in enumerate(parts)] + sent
    back_high = tree(list(tie(sent, ends[1]))).astype(BF16)
    back = back_high.astype(F32)
    back_pieces = [swap(back_high, "sample", k) if k else back_high for k in range(samples)]
    full[2] = across(pair[2], *back_pieces)
    ends[2] = outward(full[2])

    inner = ((me == 1) | (me == 2)).astype(jnp.int32)
    places = jnp.concatenate([order, inner[None]])
    total = wide_forward(
        back_pieces, [first_half, full[1]], [None, ends[1]], places, 0, None, genotypes, columns, "third_forward_0"
    )
    value = wide_forward(
        back_pieces, full[2:], ends[2:], places, 3 * some, total, genotypes, columns, "third_forward_1"
    )
    last = lax.all_to_all(value, "marker", 0, 0)
    last = jnp.sum(last.astype(F32), axis=0)
    before = jnp.concatenate([kept_s, kept_x[traits:]], axis=0)

    def dot(x, y):
        return jnp.sum(x * y, axis=1)

    probes_here = [
        lax.dynamic_slice_in_dim(probes, (half * samples + me) * unit, unit, 1) for half in range(2)
    ]
    kept_p, last_p = kept_x[traits:], last[traits:]
    norms = jnp.concatenate(
        [
            jnp.stack([dot(start, start), dot(start, back), dot(back, back)]),
            jnp.stack([sum(dot(p, p) for p in probes_here), dot(kept_p, pred_x), dot(last_p, pred_x)]),
        ],
        axis=1,
    )
    squares = jnp.stack([dot(before, before), dot(before, last), dot(last, last)])
    sums = jnp.concatenate([norms, squares, jnp.zeros((2, norms.shape[1]), F32)], axis=0)
    sums = sum_direct(sum_marker(sums), "sample")

    first_slope = slopes[:, 0] / markers
    second_precision = input_precision * (1.0 - first_slope) / first_slope
    odds = jnp.log(inclusion / (1.0 - inclusion))
    wide_cols = jnp.stack(
        [jnp.tile(noise_precision / people, copies), jnp.tile(second_precision, copies)], axis=1
    )
    cols = jnp.stack([second_precision, slab_ratio / input_precision, odds], axis=1)
    return tuple(
        finish(order, sums, wide_cols, cols, centre, start_pieces, back_pieces, low_pieces)
    )


def solution(mesh):
    return jax.shard_map(
        per_device,
        mesh=mesh,
        in_specs=(
            P("sample", "marker"),
            P(None, "sample"),
            P(None, "marker"),
            P(None, "marker"),
            P(),
            P(),
            P(),
            P(),
        ),
        out_specs=(P(None, "marker"), P(None, "marker")),
        check_vma=False,
    )
```

```python
import functools

import jax
import jax.numpy as jnp
from jax import lax
from jax.experimental import pallas as pl
from jax.experimental.pallas import tpu as pltpu
from jax.sharding import PartitionSpec as P

F32 = jnp.float32
BF16 = jnp.bfloat16
LIMIT = 44 << 20
SLOTS = 4
VMEM = pl.BlockSpec(memory_space=pltpu.VMEM)
ANY = pl.BlockSpec(memory_space=pl.ANY)


def block_of(size, most):
    while size % most:
        most //= 2
    return most


def swap(x, axis, bits):
    n = lax.axis_size(axis)
    return lax.ppermute(x, axis, [(i, i ^ bits) for i in range(n)])


def tree(parts):
    while len(parts) > 1:
        parts = [parts[i] + parts[i + 1] for i in range(0, len(parts), 2)]
    return parts[0]


def sum_direct(x, axis, unit=1):
    n = lax.axis_size(axis)
    return tree([x if k == 0 else swap(x, axis, k) for k in range(0, n, unit)])


def sum_marker(x):
    return sum_direct(x + swap(x, "marker", 1), "marker", 2)


def denoise(signal, precision, shrink, logit_base):
    energy = shrink * precision * signal * signal
    weight = jax.nn.sigmoid(logit_base + 0.5 * energy)
    return (shrink * weight * signal, shrink * weight * (1.0 + (1.0 - weight) * energy))


def stream(place, held, sems, total, prepare, use):
    slots = held.shape[0]

    def copy(c):
        slot = lax.rem(c, slots)
        return pltpu.make_async_copy(place(c), held.at[slot], sems.at[slot])

    for c in range(min(slots, total)):
        copy(c).start()
    prepare()

    def step(c, carry):
        copy(c).wait()
        use(c, held.at[lax.rem(c, slots)])

        @pl.when(c + slots < total)
        def _():
            copy(c + slots).start()

        return carry

    lax.fori_loop(0, total, step, 0)


def ring(rows, columns):
    return [pltpu.VMEM((SLOTS, rows, columns), BF16), pltpu.SemaphoreType.DMA((SLOTS,))]


def forward_loop(g, rows, total, held, sems, unit_at, span, pieces, wide, fresh, prepare):
    people = g.shape[0]
    slots, pb, kb = held.shape
    steps, blocks = span // kb, people // pb

    def place(c):
        k, i = c // blocks, lax.rem(c, blocks)
        col = unit_at(k // steps) * span + lax.rem(k, steps) * kb
        return g.at[pl.ds(pl.multiple_of(i * pb, pb), pb), pl.ds(pl.multiple_of(col, kb), kb)]

    def use(c, slot):
        k, i = c // blocks, lax.rem(c, blocks)
        d = rows[:, pl.ds(pl.multiple_of(k * kb, kb), kb)]
        here = pl.ds(pl.multiple_of(i * pb, pb), pb)
        across = (((1,), (1,)), ((), ()))
        if wide:
            at = (here, slice(None))
            value = lax.dot_general(slot[...], d, across, preferred_element_type=F32)
        else:
            at = (slice(None), here)
            value = lax.dot_general(d, slot[...], across, preferred_element_type=F32)
        if fresh:

            @pl.when(k == 0)
            def _():
                total[at] = value

            @pl.when(k > 0)
            def _():
                total[at] += value

        else:
            total[at] += value

    stream(place, held, sems, pieces * steps * blocks, prepare, use)


def split_people(out, total, t):
    n, r, share = out.shape
    for b in range(n):
        value = total[b * share : (b + 1) * share, :].T
        high = value.astype(BF16)
        out[b, : r - t, :] = high
        if t:
            out[b, r - t :, :] = (value[:t] - high[:t].astype(F32)).astype(BF16)


def prior(cols):
    inclusion, ratio, precision = [cols[:, j : j + 1] for j in range(3)]
    shrink = ratio / (1.0 + ratio)
    base = jnp.log(inclusion / (1.0 - inclusion)) + 0.5 * jnp.log(1.0 - shrink)
    return precision, shrink, base


def slope_body(message, cols, out):
    _, slopes = denoise(message[...], *prior(cols))
    out[...] = jnp.sum(slopes, axis=1, keepdims=True)


def slope_sum(message, cols):
    return pl.pallas_call(
        slope_body,
        in_specs=[VMEM, VMEM],
        out_specs=VMEM,
        out_shape=jax.ShapeDtypeStruct((message.shape[0], 1), F32),
        compiler_params=pltpu.CompilerParams(vmem_limit_bytes=LIMIT),
        name="slope_sum",
    )(message, cols)


def first_body(markers, off, message, cols, slopes, probes, g, out, centre, rows, held, sems, total):
    t = message.shape[0]

    def prepare():
        slope = slopes[...] / markers
        first, _ = denoise(message[...], *prior(cols))
        made = (first - slope * message[...]) / (1.0 - slope)
        centre[...] = made
        rows[:t, :] = made.astype(BF16)
        rows[t:, :] = probes[...]

    forward_loop(g, rows, total, held, sems, lambda j: j, g.shape[1], 1, True, True, prepare)
    split_people(out, total, t)


def cost(rows, people, markers):
    return pl.CostEstimate(
        flops=2 * rows * people * markers, transcendentals=0, bytes_accessed=2 * people * markers
    )


def first_forward(message, cols, slopes, probes, genotypes, columns):
    people, markers = genotypes.shape
    t = message.shape[0]
    r = t + probes.shape[0]
    pb, kb = block_of(people, 1024), block_of(markers, 2048)
    return pl.pallas_call(
        functools.partial(first_body, markers * columns),
        grid_spec=pltpu.PrefetchScalarGridSpec(
            num_scalar_prefetch=1,
            grid=(),
            in_specs=[VMEM, VMEM, VMEM, VMEM, ANY],
            out_specs=[VMEM, VMEM],
            scratch_shapes=[
                pltpu.VMEM((r, markers), BF16),
                *ring(pb, kb),
                pltpu.VMEM((people, r), F32),
            ],
        ),
        out_shape=[
            jax.ShapeDtypeStruct((columns, r + t, people // columns), BF16),
            jax.ShapeDtypeStruct(message.shape, F32),
        ],
        compiler_params=pltpu.CompilerParams(vmem_limit_bytes=LIMIT),
        cost_estimate=cost(r, people, markers),
        name="first_forward",
    )(jnp.zeros((1,), jnp.int32), message, cols, slopes, probes, genotypes)


def narrow_body(n, unit, with_acc, off, *refs):
    refs = list(refs)
    pieces = [refs.pop(0) for _ in range(n)]
    acc = refs.pop(0) if with_acc else None
    g, out, rows, held, sems = refs
    span = pieces[0].shape[1]

    def prepare():
        for j in range(n):
            rows[:, j * span : (j + 1) * span] = pieces[j][...]
        if with_acc:
            out[...] = acc[...]

    count = n * span // unit
    forward_loop(
        g, rows, out, held, sems, lambda j: off[j], unit, count, False, not with_acc, prepare
    )


def narrow_forward(pieces, places, acc, genotypes, name):
    people = genotypes.shape[0]
    n, (t, span) = len(pieces), pieces[0].shape
    unit = n * span // places.shape[0]
    pb, kb = block_of(people, 1024), block_of(unit, 2048)
    operands = [*pieces, *([] if acc is None else [acc]), genotypes]
    return pl.pallas_call(
        functools.partial(narrow_body, n, unit, acc is not None),
        grid_spec=pltpu.PrefetchScalarGridSpec(
            num_scalar_prefetch=1,
            grid=(),
            in_specs=[VMEM] * (len(operands) - 1) + [ANY],
            out_specs=VMEM,
            scratch_shapes=[pltpu.VMEM((t, n * span), BF16), *ring(pb, kb)],
        ),
        out_shape=jax.ShapeDtypeStruct((t, people), F32),
        compiler_params=pltpu.CompilerParams(vmem_limit_bytes=LIMIT),
        cost_estimate=cost(t, people, n * span),
        name=name,
    )(places, *operands)


def wide_body(n, begin, chunks, with_acc, off, *refs):
    refs = list(refs)
    pieces = [refs.pop(0) for _ in range(n)]
    inner = [refs.pop(0) for _ in range(chunks)]
    outer = [refs.pop(0) for _ in range(chunks)]
    acc = refs.pop(0) if with_acc else None
    if with_acc:
        g, out, rows, held, sems, total = refs
    else:
        g, total, rows, held, sems = refs
    t, unit = pieces[0].shape[0], pieces[0].shape[1] // 2
    ends = [0]
    for x in inner:
        ends.append(ends[-1] + x.shape[1])
    count = ends[-1] // unit

    def prepare():
        for j, half in [(j, half) for j in range(n) for half in range(2)]:
            place = half * n + off[j] - begin

            @pl.when((place >= 0) & (place < count))
            def _():
                here = pl.ds(pl.multiple_of(place * unit, unit), unit)
                rows[:t, here] = pieces[j][:, half * unit : (half + 1) * unit]

        for j in range(chunks):
            here = slice(ends[j], ends[j + 1])

            @pl.when(off[n] == 1)
            def _():
                rows[t:, here] = inner[j][...]

            @pl.when(off[n] == 0)
            def _():
                rows[t:, here] = outer[j][...]

        if with_acc:
            total[...] = acc[...]

    forward_loop(
        g, rows, total, held, sems, lambda j: begin + j, unit, count, True, not with_acc, prepare
    )
    if with_acc:
        split_people(out, total, 0)


def wide_forward(pieces, inner, outer, places, begin, acc, genotypes, columns, name):
    people = genotypes.shape[0]
    n, t, unit = len(pieces), pieces[0].shape[0], pieces[0].shape[1] // 2
    r = t + inner[0].shape[0]
    pb, kb = block_of(people, 1024), block_of(unit, 2048)
    operands = [*pieces, *inner, *outer, *([] if acc is None else [acc]), genotypes]
    span = sum(x.shape[1] for x in inner)
    scratch = [pltpu.VMEM((r, span), BF16), *ring(pb, kb)]
    if acc is None:
        shape = jax.ShapeDtypeStruct((people, r), F32)
    else:
        shape = jax.ShapeDtypeStruct((columns, r, people // columns), BF16)
        scratch.append(pltpu.VMEM((people, r), F32))
    return pl.pallas_call(
        functools.partial(wide_body, n, begin, len(inner), acc is not None),
        grid_spec=pltpu.PrefetchScalarGridSpec(
            num_scalar_prefetch=1,
            grid=(),
            in_specs=[VMEM] * (len(operands) - 1) + [ANY],
            out_specs=VMEM,
            scratch_shapes=scratch,
        ),
        out_shape=shape,
        compiler_params=pltpu.CompilerParams(vmem_limit_bytes=LIMIT),
        cost_estimate=cost(r, people, span),
        name=name,
    )(places, *operands)


def backward_loop(g, rows, total, held, sems, off, span, pieces):
    people = g.shape[0]
    slots, pk, mb = held.shape
    steps, blocks = span // mb, people // pk

    def place(c):
        k, i = c // blocks, lax.rem(c, blocks)
        col = off[k // steps] * span + lax.rem(k, steps) * mb
        return g.at[pl.ds(pl.multiple_of(i * pk, pk), pk), pl.ds(pl.multiple_of(col, mb), mb)]

    def use(c, slot):
        k, i = c // blocks, lax.rem(c, blocks)
        here = pl.ds(pl.multiple_of(k * mb, mb), mb)
        d = rows[:, pl.ds(pl.multiple_of(i * pk, pk), pk)]
        value = jnp.dot(d, slot[...], preferred_element_type=F32)

        @pl.when(i == 0)
        def _():
            total[:, here] = value

        @pl.when(i > 0)
        def _():
            total[:, here] += value

    stream(place, held, sems, pieces * steps * blocks, lambda: None, use)


def back_body(n, unit, t, base, cut, off, rows, g, *refs):
    refs = list(refs)
    held, sems = refs[-2:]
    if t == rows.shape[0]:
        outs, total = refs[:-3], refs[-3]
    else:
        outs, (lower, upper, total, made, sent) = refs[:-7], refs[-7:-2]
    backward_loop(g, rows, total, held, sems, off, unit, n)
    copies = []
    if t != rows.shape[0]:
        made[...] = total[t:, :].astype(BF16)
        for j in range(n):
            place = off[j] - base
            part = made.at[:, pl.ds(j * unit, unit)]

            def copy(whole, first):
                cols = pl.ds(pl.multiple_of((place - first) * unit, unit), unit)
                return pltpu.make_async_copy(part, whole.at[:, cols], sent.at[j])

            @pl.when(place < cut)
            def _():
                copy(lower, 0).start()

            @pl.when(place >= cut)
            def _():
                copy(upper, cut).start()

            copies.append(pltpu.make_async_copy(part, lower.at[:, pl.ds(0, unit)], sent.at[j]))
    span = outs[0].shape[1]
    for j, out in enumerate(outs):
        out[...] = total[:t, j * span : (j + 1) * span].astype(out.dtype)
    for copy in copies:
        copy.wait()


def backward(rows, places, genotypes, unit, t, base, cut, types, name):
    people = genotypes.shape[0]
    r, n = rows.shape[0], places.shape[0]
    pk, mb = block_of(people, 1024), block_of(unit, 2048)
    out_specs = [VMEM] * len(types)
    out_shape = [jax.ShapeDtypeStruct((t, n * unit // len(types)), kind) for kind in types]
    scratch = [pltpu.VMEM((r, n * unit), F32)]
    if t != r:
        out_specs += [ANY] * 2
        out_shape += [jax.ShapeDtypeStruct((r - t, c * unit), BF16) for c in (cut, n - cut)]
        scratch += [pltpu.VMEM((r - t, n * unit), BF16), pltpu.SemaphoreType.DMA((n,))]
    return pl.pallas_call(
        functools.partial(back_body, n, unit, t, base, cut),
        grid_spec=pltpu.PrefetchScalarGridSpec(
            num_scalar_prefetch=1,
            grid=(),
            in_specs=[VMEM, ANY],
            out_specs=out_specs,
            scratch_shapes=[*scratch, *ring(pk, mb)],
        ),
        out_shape=out_shape,
        compiler_params=pltpu.CompilerParams(vmem_limit_bytes=LIMIT),
        cost_estimate=cost(r, people, n * unit),
        name=name,
    )(places, rows, genotypes)


def finish_body(n, copies, off, sums, wide_cols, cols, centre, *refs):
    start_hi, back_hi, low = refs[:n], refs[n : 2 * n], refs[2 * n : 3 * n]
    estimate, lmmse = refs[3 * n :]
    t, unit = start_hi[0].shape[0], start_hi[0].shape[1] // 2
    sums = sums[...].T
    norm_start, du, uu, xx, xw, ww = [sums[:, j : j + 1] for j in range(6)]
    tau, gamma = wide_cols[:, 0:1], wide_cols[:, 1:2]
    second_precision, slab_var, odds = [cols[:, j : j + 1] for j in range(3)]

    step_0 = norm_start / (tau * du + gamma * norm_start)
    left, b = 1.0 - step_0 * gamma, step_0 * tau
    norm_next = left * left * norm_start - 2.0 * left * b * du + b * b * uu
    a = left + norm_next / norm_start
    dir_norm = a * a * norm_start - 2.0 * a * b * du + b * b * uu
    dir_square = a * a * xx - 2.0 * a * b * xw + b * b * ww
    step_1 = norm_next / (tau * dir_square + gamma * dir_norm)

    start_coef = (step_0 + step_1 * a)[:t]
    back_coef = (step_1 * b)[:t]
    dots = step_0 * norm_start + step_1 * (a * norm_start - b * du)
    probe_dot = sum(dots[i * t : (i + 1) * t] for i in range(1, copies))
    probe_norm = sum(norm_start[i * t : (i + 1) * t] for i in range(1, copies))
    second_slope = second_precision * probe_dot / (probe_norm + 1e-06)
    next_precision = second_precision * (1.0 - second_slope) / second_slope
    next_shrink = slab_var * next_precision / (1.0 + slab_var * next_precision)
    next_base = odds + 0.5 * jnp.log(1.0 - next_shrink)
    for j, half in [(j, half) for j in range(n) for half in range(2)]:
        here = pl.ds(pl.multiple_of((half * n + off[j]) * unit, unit), unit)
        part = slice(half * unit, (half + 1) * unit)
        start = start_hi[j][:, part].astype(F32) + low[j][:, part].astype(F32)
        back = back_hi[j][:, part].astype(F32)
        middle = centre[:, here]
        made = middle + start_coef * start - back_coef * back
        lmmse[:, here] = made
        next_message = (made - second_slope * middle) / (1.0 - second_slope)
        value, _ = denoise(next_message, next_precision, next_shrink, next_base)
        estimate[:, here] = value


def finish(places, sums, wide_cols, cols, centre, start_hi, back_hi, low):
    n = len(low)
    shape = jax.ShapeDtypeStruct(centre.shape, F32)
    copies = sums.shape[1] // centre.shape[0]
    operands = [sums, wide_cols, cols, centre, *start_hi, *back_hi, *low]
    return pl.pallas_call(
        functools.partial(finish_body, n, copies),
        grid_spec=pltpu.PrefetchScalarGridSpec(
            num_scalar_prefetch=1, grid=(), in_specs=[VMEM] * len(operands), out_specs=[VMEM, VMEM]
        ),
        out_shape=[shape, shape],
        compiler_params=pltpu.CompilerParams(vmem_limit_bytes=LIMIT),
        name="finish",
    )(places, *operands)


def per_device(
    genotypes, phenotypes, message, probes, inclusion, slab_ratio, input_precision, noise_precision
):
    samples, columns = lax.axis_size("sample"), lax.axis_size("marker")
    people_here, markers_here = genotypes.shape
    people, markers = people_here * samples, markers_here * columns
    traits = message.shape[0]
    copies = probes.shape[0] // traits + 1
    me, column = lax.axis_index("sample"), lax.axis_index("marker")
    unit, share = markers_here // (2 * samples), people_here // columns
    order = jnp.arange(samples, dtype=jnp.int32) ^ me
    some = samples // 2
    near, far = [jnp.stack([o, o + samples], axis=1).reshape(-1) for o in (order[:some], order[some:])]

    cols = jnp.stack([inclusion, slab_ratio, input_precision], axis=1)
    slopes = slope_sum(message, cols)
    slopes = slopes + swap(slopes, "marker", 1)
    probes_b = lax.optimization_barrier((probes, slopes))[0].astype(BF16)
    slopes = sum_direct(slopes, "marker", 2)
    value, centre = first_forward(message, cols, slopes, probes_b, genotypes, columns)
    kept_x = jnp.sum(lax.all_to_all(value, "marker", 0, 0).astype(F32), axis=0)
    kept_x, low_x = kept_x[: traits * copies], kept_x[traits * copies :]
    own = lax.dynamic_slice_in_dim(phenotypes, column * share, share, 1) - (kept_x[:traits] + low_x)
    rows = jnp.concatenate([own, kept_x[traits:]], axis=0).astype(BF16)
    pred_x = rows[traits:].astype(F32)
    rows = lax.all_gather(rows, "marker", axis=1, tiled=True)
    starts, chunks = [], []
    for half, cut in enumerate((samples - 1, some)):
        base = half * samples
        *parts, lower, upper = backward(
            rows, order + base, genotypes, unit, traits, base, cut, [F32] * samples, f"first_back_{half}"
        )
        starts.append([swap(part, "sample", k) if k else part for k, part in enumerate(parts)])
        chunks += [lower, upper]
        rows, *_ = lax.optimization_barrier((rows, lower))
    chunks = [chunks[0], jnp.concatenate(chunks[1:3], axis=1), chunks[3]]

    def add(x, y):
        return (x.astype(F32) + y.astype(F32)).astype(BF16)

    def tie(values, *others):
        return lax.optimization_barrier((tuple(values), others))[0]

    def hop(x, pairs, *others):
        y = lax.ppermute(x, "sample", pairs)
        return add(*tie((x, y), *others))

    def inward(c, *others):
        return hop(chunks[c], [(0, 1), (3, 2)], *others)

    def across(x, *others):
        return hop(x, [(1, 2), (2, 1)], *others)

    def outward(x):
        return lax.ppermute(x, "sample", [(1, 0), (2, 3)])

    pair, full, ends = [None] * 3, [None] * 3, [None] * 3
    pair[0] = inward(0)
    scale = (noise_precision / people)[:, None]
    start = scale * jnp.concatenate([tree(parts) for parts in starts], axis=1)
    start_high = lax.reduce_precision(start, 8, 7)
    start_low = (start - start_high).astype(BF16)
    start_high = start_high.astype(BF16)

    start_pieces = [swap(start_high, "sample", k) if k else start_high for k in range(samples)]
    *start_pieces, pair[0], chunks[1] = tie((*start_pieces, pair[0], chunks[1]))
    both = jnp.concatenate([near, far])
    value = narrow_forward(start_pieces, both, None, genotypes, "second_forward")
    full[0], pair[1] = across(pair[0], value), inward(1, value)
    value, pair[1], chunks[2] = tie((value, pair[1], chunks[2]), full[0])
    ends[0] = outward(full[0])
    value = sum_marker(value)
    kept_s = lax.dynamic_slice_in_dim(value, column * share, share, 1)
    rows = value.astype(BF16)
    parts = backward(rows, far, genotypes, unit, traits, 0, 0, [BF16] * some, "second_back_far")
    sent = [swap(part, "sample", k + some) for k, part in enumerate(parts)]
    full[1], pair[2] = across(pair[1], *parts), inward(2, *parts)
    (rows,) = tie((rows,), full[1], pair[2], ends[0], *parts)
    ends[1] = outward(full[1])
    parts = backward(rows, near, genotypes, unit, traits, 0, 0, [F32] + [BF16] * (some - 1), "second_back_near")
    sent = [swap(part, "sample", k) if k else part for k, part in enumerate(parts)] + sent
    back_high = tree([part.astype(F32) for part in tie(sent, ends[1])]).astype(BF16)
    back = back_high.astype(F32)
    back_pieces = [swap(back_high, "sample", k) if k else back_high for k in range(samples)]
    full[2] = across(pair[2], *back_pieces)
    ends[2] = outward(full[2])

    inner = ((me == 1) | (me == 2)).astype(jnp.int32)
    places = jnp.concatenate([order, inner[None]])
    total = wide_forward(
        back_pieces, full[:2], ends[:2], places, 0, None, genotypes, columns, "third_forward_0"
    )
    (start_low,) = tie((start_low,), total)
    low_pieces = [swap(start_low, "sample", k) if k else start_low for k in range(samples)]
    value = wide_forward(
        back_pieces, full[2:], ends[2:], places, 3 * some, total, genotypes, columns, "third_forward_1"
    )
    (last,) = tie((lax.all_to_all(value, "marker", 0, 0),), *low_pieces)
    last = jnp.sum(last.astype(F32), axis=0)
    before = jnp.concatenate([kept_s, kept_x[traits:]], axis=0)

    def dot(x, y):
        return jnp.sum(x * y, axis=1)

    probes_here = [
        lax.dynamic_slice_in_dim(probes, (half * samples + me) * unit, unit, 1) for half in range(2)
    ]
    kept_p, last_p = kept_x[traits:], last[traits:]
    norms = jnp.concatenate(
        [
            jnp.stack([dot(start, start), dot(start, back), dot(back, back)]),
            jnp.stack([sum(dot(p, p) for p in probes_here), dot(kept_p, pred_x), dot(last_p, pred_x)]),
        ],
        axis=1,
    )
    squares = jnp.stack([dot(before, before), dot(before, last), dot(last, last)])
    sums = jnp.concatenate([norms, squares, jnp.zeros((2, norms.shape[1]), F32)], axis=0)
    sums = sum_direct(sum_marker(sums), "sample")

    first_slope = slopes[:, 0] / markers
    second_precision = input_precision * (1.0 - first_slope) / first_slope
    odds = jnp.log(inclusion / (1.0 - inclusion))
    wide_cols = jnp.stack(
        [jnp.tile(noise_precision / people, copies), jnp.tile(second_precision, copies)], axis=1
    )
    cols = jnp.stack([second_precision, slab_ratio / input_precision, odds], axis=1)
    return tuple(
        finish(order, sums, wide_cols, cols, centre, start_pieces, back_pieces, low_pieces)
    )


def solution(mesh):
    return jax.shard_map(
        per_device,
        mesh=mesh,
        in_specs=(
            P("sample", "marker"),
            P(None, "sample"),
            P(None, "marker"),
            P(None, "marker"),
            P(),
            P(),
            P(),
            P(),
        ),
        out_specs=(P(None, "marker"), P(None, "marker")),
        check_vma=False,
    )
```

```python
import functools

import jax
import jax.numpy as jnp
from jax import lax
from jax.experimental import pallas as pl
from jax.experimental.pallas import tpu as pltpu
from jax.sharding import PartitionSpec as P

F32 = jnp.float32
BF16 = jnp.bfloat16
LIMIT = 44 << 20
SLOTS = 4
VMEM = pl.BlockSpec(memory_space=pltpu.VMEM)
ANY = pl.BlockSpec(memory_space=pl.ANY)


def block_of(size, most):
    while size % most:
        most //= 2
    return most


def swap(x, axis, bits):
    n = lax.axis_size(axis)
    return lax.ppermute(x, axis, [(i, i ^ bits) for i in range(n)])


def tree(parts):
    while len(parts) > 1:
        parts = [parts[i] + parts[i + 1] for i in range(0, len(parts), 2)]
    return parts[0]


def sum_direct(x, axis, unit=1):
    n = lax.axis_size(axis)
    return tree([x if k == 0 else swap(x, axis, k) for k in range(0, n, unit)])


def sum_marker(x):
    return sum_direct(x + swap(x, "marker", 1), "marker", 2)


def denoise(signal, precision, shrink, logit_base):
    energy = shrink * precision * signal * signal
    weight = jax.nn.sigmoid(logit_base + 0.5 * energy)
    return (shrink * weight * signal, shrink * weight * (1.0 + (1.0 - weight) * energy))


def stream(place, held, sems, total, prepare, use):
    slots = held.shape[0]

    def copy(c):
        slot = lax.rem(c, slots)
        return pltpu.make_async_copy(place(c), held.at[slot], sems.at[slot])

    for c in range(min(slots, total)):
        copy(c).start()
    prepare()

    def step(c, carry):
        copy(c).wait()
        use(c, held.at[lax.rem(c, slots)])

        @pl.when(c + slots < total)
        def _():
            copy(c + slots).start()

        return carry

    lax.fori_loop(0, total, step, 0)


def ring(rows, columns):
    return [pltpu.VMEM((SLOTS, rows, columns), BF16), pltpu.SemaphoreType.DMA((SLOTS,))]


def forward_loop(g, rows, total, held, sems, unit_at, span, pieces, wide, fresh, prepare):
    people = g.shape[0]
    slots, pb, kb = held.shape
    steps, blocks = span // kb, people // pb

    def place(c):
        k, i = c // blocks, lax.rem(c, blocks)
        col = unit_at(k // steps) * span + lax.rem(k, steps) * kb
        return g.at[pl.ds(pl.multiple_of(i * pb, pb), pb), pl.ds(pl.multiple_of(col, kb), kb)]

    def use(c, slot):
        k, i = c // blocks, lax.rem(c, blocks)
        d = rows[:, pl.ds(pl.multiple_of(k * kb, kb), kb)]
        here = pl.ds(pl.multiple_of(i * pb, pb), pb)
        across = (((1,), (1,)), ((), ()))
        if wide:
            at = (here, slice(None))
            value = lax.dot_general(slot[...], d, across, preferred_element_type=F32)
        else:
            at = (slice(None), here)
            value = lax.dot_general(d, slot[...], across, preferred_element_type=F32)
        if fresh:

            @pl.when(k == 0)
            def _():
                total[at] = value

            @pl.when(k > 0)
            def _():
                total[at] += value

        else:
            total[at] += value

    stream(place, held, sems, pieces * steps * blocks, prepare, use)


def split_people(out, total, t):
    n, r, share = out.shape
    for b in range(n):
        value = total[b * share : (b + 1) * share, :].T
        high = value.astype(BF16)
        out[b, : r - t, :] = high
        if t:
            out[b, r - t :, :] = (value[:t] - high[:t].astype(F32)).astype(BF16)


def prior(cols):
    inclusion, ratio, precision = [cols[:, j : j + 1] for j in range(3)]
    shrink = ratio / (1.0 + ratio)
    base = jnp.log(inclusion / (1.0 - inclusion)) + 0.5 * jnp.log(1.0 - shrink)
    return precision, shrink, base


def slope_body(message, cols, out):
    _, slopes = denoise(message[...], *prior(cols))
    out[...] = jnp.sum(slopes, axis=1, keepdims=True)


def slope_sum(message, cols):
    return pl.pallas_call(
        slope_body,
        in_specs=[VMEM, VMEM],
        out_specs=VMEM,
        out_shape=jax.ShapeDtypeStruct((message.shape[0], 1), F32),
        compiler_params=pltpu.CompilerParams(vmem_limit_bytes=LIMIT),
        name="slope_sum",
    )(message, cols)


def first_body(markers, off, message, cols, slopes, probes, g, out, centre, rows, held, sems, total):
    t = message.shape[0]

    def prepare():
        slope = slopes[...] / markers
        first, _ = denoise(message[...], *prior(cols))
        made = (first - slope * message[...]) / (1.0 - slope)
        centre[...] = made
        rows[:t, :] = made.astype(BF16)
        rows[t:, :] = probes[...]

    forward_loop(g, rows, total, held, sems, lambda j: j, g.shape[1], 1, True, True, prepare)
    split_people(out, total, t)


def cost(rows, people, markers):
    return pl.CostEstimate(
        flops=2 * rows * people * markers, transcendentals=0, bytes_accessed=2 * people * markers
    )


def first_forward(message, cols, slopes, probes, genotypes, columns):
    people, markers = genotypes.shape
    t = message.shape[0]
    r = t + probes.shape[0]
    pb, kb = block_of(people, 1024), block_of(markers, 2048)
    return pl.pallas_call(
        functools.partial(first_body, markers * columns),
        grid_spec=pltpu.PrefetchScalarGridSpec(
            num_scalar_prefetch=1,
            grid=(),
            in_specs=[VMEM, VMEM, VMEM, VMEM, ANY],
            out_specs=[VMEM, VMEM],
            scratch_shapes=[
                pltpu.VMEM((r, markers), BF16),
                *ring(pb, kb),
                pltpu.VMEM((people, r), F32),
            ],
        ),
        out_shape=[
            jax.ShapeDtypeStruct((columns, r + t, people // columns), BF16),
            jax.ShapeDtypeStruct(message.shape, F32),
        ],
        compiler_params=pltpu.CompilerParams(vmem_limit_bytes=LIMIT),
        cost_estimate=cost(r, people, markers),
        name="first_forward",
    )(jnp.zeros((1,), jnp.int32), message, cols, slopes, probes, genotypes)


def narrow_body(n, unit, with_acc, off, *refs):
    refs = list(refs)
    pieces = [refs.pop(0) for _ in range(n)]
    acc = refs.pop(0) if with_acc else None
    g, out, rows, held, sems = refs
    span = pieces[0].shape[1]

    def prepare():
        for j in range(n):
            rows[:, j * span : (j + 1) * span] = pieces[j][...]
        if with_acc:
            out[...] = acc[...]

    count = n * span // unit
    forward_loop(
        g, rows, out, held, sems, lambda j: off[j], unit, count, False, not with_acc, prepare
    )


def narrow_forward(pieces, places, acc, genotypes, name):
    people = genotypes.shape[0]
    n, (t, span) = len(pieces), pieces[0].shape
    unit = n * span // places.shape[0]
    pb, kb = block_of(people, 1024), block_of(unit, 2048)
    operands = [*pieces, *([] if acc is None else [acc]), genotypes]
    return pl.pallas_call(
        functools.partial(narrow_body, n, unit, acc is not None),
        grid_spec=pltpu.PrefetchScalarGridSpec(
            num_scalar_prefetch=1,
            grid=(),
            in_specs=[VMEM] * (len(operands) - 1) + [ANY],
            out_specs=VMEM,
            scratch_shapes=[pltpu.VMEM((t, n * span), BF16), *ring(pb, kb)],
        ),
        out_shape=jax.ShapeDtypeStruct((t, people), F32),
        compiler_params=pltpu.CompilerParams(vmem_limit_bytes=LIMIT),
        cost_estimate=cost(t, people, n * span),
        name=name,
    )(places, *operands)


def wide_body(n, begin, chunks, with_acc, off, *refs):
    refs = list(refs)
    pieces = [refs.pop(0) for _ in range(n)]
    inner = [refs.pop(0) for _ in range(chunks)]
    outer = [refs.pop(0) for _ in range(chunks)]
    acc = refs.pop(0) if with_acc else None
    if with_acc:
        g, out, rows, held, sems, total = refs
    else:
        g, total, rows, held, sems = refs
    t, unit = pieces[0].shape[0], pieces[0].shape[1] // 2
    ends = [0]
    for x in inner:
        ends.append(ends[-1] + x.shape[1])
    count = ends[-1] // unit

    def prepare():
        for j, half in [(j, half) for j in range(n) for half in range(2)]:
            place = 2 * off[j] + half - begin

            @pl.when((place >= 0) & (place < count))
            def _():
                here = pl.ds(pl.multiple_of(place * unit, unit), unit)
                rows[:t, here] = pieces[j][:, half * unit : (half + 1) * unit]

        for j in range(chunks):
            here = slice(ends[j], ends[j + 1])

            @pl.when(off[n] == 1)
            def _():
                rows[t:, here] = inner[j][...]

            @pl.when(off[n] == 0)
            def _():
                rows[t:, here] = outer[j][...]

        if with_acc:
            total[...] = acc[...]

    forward_loop(
        g, rows, total, held, sems, lambda j: begin + j, unit, count, True, not with_acc, prepare
    )
    if with_acc:
        split_people(out, total, 0)


def wide_forward(pieces, inner, outer, places, begin, acc, genotypes, columns, name):
    people = genotypes.shape[0]
    n, t, unit = len(pieces), pieces[0].shape[0], pieces[0].shape[1] // 2
    r = t + inner[0].shape[0]
    pb, kb = block_of(people, 1024), block_of(unit, 2048)
    operands = [*pieces, *inner, *outer, *([] if acc is None else [acc]), genotypes]
    span = sum(x.shape[1] for x in inner)
    scratch = [pltpu.VMEM((r, span), BF16), *ring(pb, kb)]
    if acc is None:
        shape = jax.ShapeDtypeStruct((people, r), F32)
    else:
        shape = jax.ShapeDtypeStruct((columns, r, people // columns), BF16)
        scratch.append(pltpu.VMEM((people, r), F32))
    return pl.pallas_call(
        functools.partial(wide_body, n, begin, len(inner), acc is not None),
        grid_spec=pltpu.PrefetchScalarGridSpec(
            num_scalar_prefetch=1,
            grid=(),
            in_specs=[VMEM] * (len(operands) - 1) + [ANY],
            out_specs=VMEM,
            scratch_shapes=scratch,
        ),
        out_shape=shape,
        compiler_params=pltpu.CompilerParams(vmem_limit_bytes=LIMIT),
        cost_estimate=cost(r, people, span),
        name=name,
    )(places, *operands)


def backward_loop(g, rows, total, held, sems, unit_at, span, pieces):
    people = g.shape[0]
    slots, pk, mb = held.shape
    steps, blocks = span // mb, people // pk

    def place(c):
        k, i = c // blocks, lax.rem(c, blocks)
        col = unit_at(k // steps) * span + lax.rem(k, steps) * mb
        return g.at[pl.ds(pl.multiple_of(i * pk, pk), pk), pl.ds(pl.multiple_of(col, mb), mb)]

    def use(c, slot):
        k, i = c // blocks, lax.rem(c, blocks)
        here = pl.ds(pl.multiple_of(k * mb, mb), mb)
        d = rows[:, pl.ds(pl.multiple_of(i * pk, pk), pk)]
        value = jnp.dot(d, slot[...], preferred_element_type=F32)

        @pl.when(i == 0)
        def _():
            total[:, here] = value

        @pl.when(i > 0)
        def _():
            total[:, here] += value

    stream(place, held, sems, pieces * steps * blocks, lambda: None, use)


def first_back_body(unit, begin, t, arrays, off, rows, g, *refs):
    refs = list(refs)
    before = refs.pop(0) if begin else None
    total, held, sems = refs[-3:]
    count = total.shape[1] // unit
    backward_loop(g, rows, total, held, sems, lambda j: begin + j, unit, count)
    if not begin:
        refs[0][...] = total[:t, :]
        chunks = refs[1:-3]
    else:
        whole = refs[-4]
        first = begin * unit
        whole[:, :first] = before[...]
        whole[:, first:] = total[:t, :]
        for k in range(arrays):
            out = refs[k]
            span = out.shape[1]
            out[...] = whole[:, pl.ds(pl.multiple_of(off[k] * span, span), span)]
        chunks = refs[arrays:-4]
    at = 0
    for chunk in chunks:
        chunk[...] = total[t:, at : at + chunk.shape[1]].astype(BF16)
        at += chunk.shape[1]


def first_back(rows, order, genotypes, unit, t, begin, before, sizes, name):
    people, markers = genotypes.shape
    r, n = rows.shape[0], sum(sizes)
    pk, mb = block_of(people, 1024), block_of(unit, 2048)
    arrays = order.shape[0]
    operands = [rows, genotypes]
    scratch = [pltpu.VMEM((r, n * unit), F32)]
    if begin:
        operands.append(before)
        out_shape = [jax.ShapeDtypeStruct((t, markers // arrays), F32)] * arrays
        scratch.insert(0, pltpu.VMEM((t, markers), F32))
    else:
        out_shape = [jax.ShapeDtypeStruct((t, n * unit), F32)]
    out_shape += [jax.ShapeDtypeStruct((r - t, c * unit), BF16) for c in sizes]
    return pl.pallas_call(
        functools.partial(first_back_body, unit, begin, t, arrays),
        grid_spec=pltpu.PrefetchScalarGridSpec(
            num_scalar_prefetch=1,
            grid=(),
            in_specs=[VMEM, ANY] + [VMEM] * (len(operands) - 2),
            out_specs=[VMEM] * len(out_shape),
            scratch_shapes=[*scratch, *ring(pk, mb)],
        ),
        out_shape=out_shape,
        compiler_params=pltpu.CompilerParams(vmem_limit_bytes=LIMIT),
        cost_estimate=cost(r, people, n * unit),
        name=name,
    )(order, *operands)


def second_back_body(n, unit, off, rows, g, *refs):
    outs, (total, held, sems) = refs[:-3], refs[-3:]
    backward_loop(g, rows, total, held, sems, lambda j: off[j], unit, n)
    span = outs[0].shape[1]
    for j, out in enumerate(outs):
        out[...] = total[:, j * span : (j + 1) * span].astype(out.dtype)


def second_back(rows, places, genotypes, unit, types):
    people = genotypes.shape[0]
    r, n = rows.shape[0], places.shape[0]
    pk, mb = block_of(people, 1024), block_of(unit, 2048)
    return pl.pallas_call(
        functools.partial(second_back_body, n, unit),
        grid_spec=pltpu.PrefetchScalarGridSpec(
            num_scalar_prefetch=1,
            grid=(),
            in_specs=[VMEM, ANY],
            out_specs=[VMEM] * len(types),
            scratch_shapes=[pltpu.VMEM((r, n * unit), F32), *ring(pk, mb)],
        ),
        out_shape=[jax.ShapeDtypeStruct((r, n * unit // len(types)), kind) for kind in types],
        compiler_params=pltpu.CompilerParams(vmem_limit_bytes=LIMIT),
        cost_estimate=cost(r, people, n * unit),
        name="second_back",
    )(places, rows, genotypes)


def finish_body(n, copies, off, sums, wide_cols, cols, centre, *refs):
    start_hi, back_hi, low = refs[:n], refs[n : 2 * n], refs[2 * n : 3 * n]
    estimate, lmmse = refs[3 * n :]
    t, unit = start_hi[0].shape[0], start_hi[0].shape[1] // 2
    sums = sums[...].T
    norm_start, du, uu, xx, xw, ww = [sums[:, j : j + 1] for j in range(6)]
    tau, gamma = wide_cols[:, 0:1], wide_cols[:, 1:2]
    second_precision, slab_var, odds = [cols[:, j : j + 1] for j in range(3)]

    step_0 = norm_start / (tau * du + gamma * norm_start)
    left, b = 1.0 - step_0 * gamma, step_0 * tau
    norm_next = left * left * norm_start - 2.0 * left * b * du + b * b * uu
    a = left + norm_next / norm_start
    dir_norm = a * a * norm_start - 2.0 * a * b * du + b * b * uu
    dir_square = a * a * xx - 2.0 * a * b * xw + b * b * ww
    step_1 = norm_next / (tau * dir_square + gamma * dir_norm)

    start_coef = (step_0 + step_1 * a)[:t]
    back_coef = (step_1 * b)[:t]
    dots = step_0 * norm_start + step_1 * (a * norm_start - b * du)
    probe_dot = sum(dots[i * t : (i + 1) * t] for i in range(1, copies))
    probe_norm = sum(norm_start[i * t : (i + 1) * t] for i in range(1, copies))
    second_slope = second_precision * probe_dot / (probe_norm + 1e-06)
    next_precision = second_precision * (1.0 - second_slope) / second_slope
    next_shrink = slab_var * next_precision / (1.0 + slab_var * next_precision)
    next_base = odds + 0.5 * jnp.log(1.0 - next_shrink)
    for j, half in [(j, half) for j in range(n) for half in range(2)]:
        here = pl.ds(pl.multiple_of((2 * off[j] + half) * unit, unit), unit)
        part = slice(half * unit, (half + 1) * unit)
        start = start_hi[j][:, part].astype(F32) + low[j][:, part].astype(F32)
        back = back_hi[j][:, part].astype(F32)
        middle = centre[:, here]
        made = middle + start_coef * start - back_coef * back
        lmmse[:, here] = made
        next_message = (made - second_slope * middle) / (1.0 - second_slope)
        value, _ = denoise(next_message, next_precision, next_shrink, next_base)
        estimate[:, here] = value


def finish(places, sums, wide_cols, cols, centre, start_hi, back_hi, low):
    n = len(low)
    shape = jax.ShapeDtypeStruct(centre.shape, F32)
    copies = sums.shape[1] // centre.shape[0]
    operands = [sums, wide_cols, cols, centre, *start_hi, *back_hi, *low]
    return pl.pallas_call(
        functools.partial(finish_body, n, copies),
        grid_spec=pltpu.PrefetchScalarGridSpec(
            num_scalar_prefetch=1, grid=(), in_specs=[VMEM] * len(operands), out_specs=[VMEM, VMEM]
        ),
        out_shape=[shape, shape],
        compiler_params=pltpu.CompilerParams(vmem_limit_bytes=LIMIT),
        name="finish",
    )(places, *operands)


def per_device(
    genotypes, phenotypes, message, probes, inclusion, slab_ratio, input_precision, noise_precision
):
    samples, columns = lax.axis_size("sample"), lax.axis_size("marker")
    people_here, markers_here = genotypes.shape
    people, markers = people_here * samples, markers_here * columns
    traits = message.shape[0]
    copies = probes.shape[0] // traits + 1
    me, column = lax.axis_index("sample"), lax.axis_index("marker")
    unit, share = markers_here // (2 * samples), people_here // columns
    order = jnp.arange(samples, dtype=jnp.int32) ^ me
    some = samples // 2
    owned = jnp.stack([2 * order, 2 * order + 1], axis=1).reshape(-1)

    cols = jnp.stack([inclusion, slab_ratio, input_precision], axis=1)
    slopes = slope_sum(message, cols)
    slopes = slopes + swap(slopes, "marker", 1)
    probes_b = lax.optimization_barrier((probes, slopes))[0].astype(BF16)
    slopes = sum_direct(slopes, "marker", 2)
    value, centre = first_forward(message, cols, slopes, probes_b, genotypes, columns)
    kept_x = jnp.sum(lax.all_to_all(value, "marker", 0, 0).astype(F32), axis=0)
    kept_x, low_x = kept_x[: traits * copies], kept_x[traits * copies :]
    own = lax.dynamic_slice_in_dim(phenotypes, column * share, share, 1) - (kept_x[:traits] + low_x)
    rows = jnp.concatenate([own, kept_x[traits:]], axis=0).astype(BF16)
    pred_x = rows[traits:].astype(F32)
    rows = lax.all_gather(rows, "marker", axis=1, tiled=True)
    sizes = (some, samples - 1, samples - 1)
    before, *chunks = first_back(
        rows, order, genotypes, unit, traits, 0, None, sizes[:1], "first_back_0"
    )
    rows, before, chunks[0] = lax.optimization_barrier((rows, before, chunks[0]))
    outs = first_back(
        rows, order, genotypes, unit, traits, sizes[0], before, sizes[1:], "first_back_1"
    )
    chunks += outs[samples:]

    def add(x, y):
        return (x.astype(F32) + y.astype(F32)).astype(BF16)

    def tie(values, *others):
        return lax.optimization_barrier((tuple(values), others))[0]

    def inward(c):
        return lax.ppermute(chunks[c], "sample", [(0, 1), (3, 2)])

    def across(x):
        return lax.ppermute(x, "sample", [(1, 2), (2, 1)])

    def outward(x):
        return lax.ppermute(x, "sample", [(1, 0), (2, 3)])

    pair, full, ends = [None] * 3, [None] * 3, [None] * 3
    *parts, pair[0] = tie((*outs[:samples], inward(0)))
    sent = [swap(part, "sample", k) if k else part for k, part in enumerate(parts)]
    pair[0] = add(chunks[0], pair[0])
    scale = (noise_precision / people)[:, None]
    start = scale * tree(sent)
    start_high = lax.reduce_precision(start, 8, 7)
    start_low = (start - start_high).astype(BF16)
    start_high = start_high.astype(BF16)

    start_pieces = [swap(start_high, "sample", k) if k else start_high for k in range(samples)]
    *start_pieces, pair[0], chunks[1] = tie((*start_pieces, pair[0], chunks[1]))
    full[0], pair[1] = across(pair[0]), inward(1)
    value = narrow_forward(start_pieces, owned, None, genotypes, "second_forward")
    value, full[0], pair[1] = tie((value, full[0], pair[1]))
    value = sum_marker(value)
    kept_s = lax.dynamic_slice_in_dim(value, column * share, share, 1)
    full[0], pair[1] = tie((add(pair[0], full[0]), add(chunks[1], pair[1])))
    rows, full[0], pair[1], chunks[2] = tie((value.astype(BF16), full[0], pair[1], chunks[2]))
    ends[0], full[1], pair[2] = outward(full[0]), across(pair[1]), inward(2)
    parts = second_back(rows, owned, genotypes, unit, [F32] + [BF16] * (samples - 1))
    *parts, ends[0] = tie((*parts, ends[0]))
    sent = [swap(part, "sample", k) if k else part for k, part in enumerate(parts)]
    full[1], pair[2] = tie((full[1], pair[2]), *parts)
    full[1], pair[2] = add(pair[1], full[1]), add(chunks[2], pair[2])
    ends[1] = outward(full[1])
    back_high = tree([part.astype(F32) for part in sent]).astype(BF16)
    back = back_high.astype(F32)
    back_pieces = [swap(back_high, "sample", k) if k else back_high for k in range(samples)]
    full[2] = add(*tie((pair[2], across(pair[2])), *back_pieces))
    ends[2] = outward(full[2])

    inner = ((me == 1) | (me == 2)).astype(jnp.int32)
    places = jnp.concatenate([order, inner[None]])
    total = wide_forward(
        back_pieces, full[:2], ends[:2], places, 0, None, genotypes, columns, "third_forward_0"
    )
    (start_low,) = tie((start_low,), total)
    low_pieces = [swap(start_low, "sample", k) if k else start_low for k in range(samples)]
    value = wide_forward(
        back_pieces, full[2:], ends[2:], places, sum(sizes[:2]), total, genotypes, columns, "third_forward_1"
    )
    (last,) = tie((lax.all_to_all(value, "marker", 0, 0),), *low_pieces)
    last = jnp.sum(last.astype(F32), axis=0)
    before = jnp.concatenate([kept_s, kept_x[traits:]], axis=0)

    def dot(x, y):
        return jnp.sum(x * y, axis=1)

    probes_here = lax.dynamic_slice_in_dim(probes, 2 * me * unit, 2 * unit, 1)
    kept_p, last_p = kept_x[traits:], last[traits:]
    norms = jnp.concatenate(
        [
            jnp.stack([dot(start, start), dot(start, back), dot(back, back)]),
            jnp.stack([dot(probes_here, probes_here), dot(kept_p, pred_x), dot(last_p, pred_x)]),
        ],
        axis=1,
    )
    squares = jnp.stack([dot(before, before), dot(before, last), dot(last, last)])
    sums = jnp.concatenate([norms, squares, jnp.zeros((2, norms.shape[1]), F32)], axis=0)
    sums = sum_direct(sum_marker(sums), "sample")

    first_slope = slopes[:, 0] / markers
    second_precision = input_precision * (1.0 - first_slope) / first_slope
    odds = jnp.log(inclusion / (1.0 - inclusion))
    wide_cols = jnp.stack(
        [jnp.tile(noise_precision / people, copies), jnp.tile(second_precision, copies)], axis=1
    )
    cols = jnp.stack([second_precision, slab_ratio / input_precision, odds], axis=1)
    return tuple(
        finish(order, sums, wide_cols, cols, centre, start_pieces, back_pieces, low_pieces)
    )


def solution(mesh):
    return jax.shard_map(
        per_device,
        mesh=mesh,
        in_specs=(
            P("sample", "marker"),
            P(None, "sample"),
            P(None, "marker"),
            P(None, "marker"),
            P(),
            P(),
            P(),
            P(),
        ),
        out_specs=(P(None, "marker"), P(None, "marker")),
        check_vma=False,
    )
```

```python
import functools

import jax
import jax.numpy as jnp
from jax import lax
from jax.experimental import pallas as pl
from jax.experimental.pallas import tpu as pltpu
from jax.sharding import PartitionSpec as P

F32 = jnp.float32
BF16 = jnp.bfloat16
LIMIT = 44 << 20
SLOTS = 4
VMEM = pl.BlockSpec(memory_space=pltpu.VMEM)
ANY = pl.BlockSpec(memory_space=pl.ANY)


def block_of(size, most):
    while size % most:
        most //= 2
    return most


def swap(x, axis, bits):
    n = lax.axis_size(axis)
    return lax.ppermute(x, axis, [(i, i ^ bits) for i in range(n)])


def tree(parts):
    while len(parts) > 1:
        parts = [parts[i] + parts[i + 1] for i in range(0, len(parts), 2)]
    return parts[0]


def sum_direct(x, axis, unit=1):
    n = lax.axis_size(axis)
    return tree([x if k == 0 else swap(x, axis, k) for k in range(0, n, unit)])


def sum_marker(x):
    return sum_direct(x + swap(x, "marker", 1), "marker", 2)


def denoise(signal, precision, shrink, logit_base):
    energy = shrink * precision * signal * signal
    weight = jax.nn.sigmoid(logit_base + 0.5 * energy)
    return (shrink * weight * signal, shrink * weight * (1.0 + (1.0 - weight) * energy))


def stream(place, held, sems, total, prepare, use):
    slots = held.shape[0]

    def copy(c):
        slot = lax.rem(c, slots)
        return pltpu.make_async_copy(place(c), held.at[slot], sems.at[slot])

    for c in range(min(slots, total)):
        copy(c).start()
    prepare()

    def step(c, carry):
        copy(c).wait()
        use(c, held.at[lax.rem(c, slots)])

        @pl.when(c + slots < total)
        def _():
            copy(c + slots).start()

        return carry

    lax.fori_loop(0, total, step, 0)


def ring(rows, columns):
    return [pltpu.VMEM((SLOTS, rows, columns), BF16), pltpu.SemaphoreType.DMA((SLOTS,))]


def forward_loop(g, rows, total, held, sems, unit_at, span, pieces, wide, fresh, prepare):
    people = g.shape[0]
    slots, pb, kb = held.shape
    steps, blocks = span // kb, people // pb

    def place(c):
        k, i = c // blocks, lax.rem(c, blocks)
        col = unit_at(k // steps) * span + lax.rem(k, steps) * kb
        return g.at[pl.ds(pl.multiple_of(i * pb, pb), pb), pl.ds(pl.multiple_of(col, kb), kb)]

    def use(c, slot):
        k, i = c // blocks, lax.rem(c, blocks)
        d = rows[:, pl.ds(pl.multiple_of(k * kb, kb), kb)]
        here = pl.ds(pl.multiple_of(i * pb, pb), pb)
        across = (((1,), (1,)), ((), ()))
        if wide:
            at = (here, slice(None))
            value = lax.dot_general(slot[...], d, across, preferred_element_type=F32)
        else:
            at = (slice(None), here)
            value = lax.dot_general(d, slot[...], across, preferred_element_type=F32)
        if fresh:

            @pl.when(k == 0)
            def _():
                total[at] = value

            @pl.when(k > 0)
            def _():
                total[at] += value

        else:
            total[at] += value

    stream(place, held, sems, pieces * steps * blocks, prepare, use)


def split_people(out, total, t):
    n, r, share = out.shape
    for b in range(n):
        value = total[b * share : (b + 1) * share, :].T
        high = value.astype(BF16)
        out[b, : r - t, :] = high
        if t:
            out[b, r - t :, :] = (value[:t] - high[:t].astype(F32)).astype(BF16)


def prior(cols):
    inclusion, ratio, precision = [cols[:, j : j + 1] for j in range(3)]
    shrink = ratio / (1.0 + ratio)
    base = jnp.log(inclusion / (1.0 - inclusion)) + 0.5 * jnp.log(1.0 - shrink)
    return precision, shrink, base


def slope_body(message, cols, out):
    _, slopes = denoise(message[...], *prior(cols))
    out[...] = jnp.sum(slopes, axis=1, keepdims=True)


def slope_sum(message, cols):
    return pl.pallas_call(
        slope_body,
        in_specs=[VMEM, VMEM],
        out_specs=VMEM,
        out_shape=jax.ShapeDtypeStruct((message.shape[0], 1), F32),
        compiler_params=pltpu.CompilerParams(vmem_limit_bytes=LIMIT),
        name="slope_sum",
    )(message, cols)


def first_body(markers, off, message, cols, slopes, probes, g, out, centre, rows, held, sems, total):
    t = message.shape[0]

    def prepare():
        slope = slopes[...] / markers
        first, _ = denoise(message[...], *prior(cols))
        made = (first - slope * message[...]) / (1.0 - slope)
        centre[...] = made
        rows[:t, :] = made.astype(BF16)
        rows[t:, :] = probes[...]

    forward_loop(g, rows, total, held, sems, lambda j: j, g.shape[1], 1, True, True, prepare)
    split_people(out, total, t)


def cost(rows, people, markers):
    return pl.CostEstimate(
        flops=2 * rows * people * markers, transcendentals=0, bytes_accessed=2 * people * markers
    )


def first_forward(message, cols, slopes, probes, genotypes, columns):
    people, markers = genotypes.shape
    t = message.shape[0]
    r = t + probes.shape[0]
    pb, kb = block_of(people, 1024), block_of(markers, 2048)
    return pl.pallas_call(
        functools.partial(first_body, markers * columns),
        grid_spec=pltpu.PrefetchScalarGridSpec(
            num_scalar_prefetch=1,
            grid=(),
            in_specs=[VMEM, VMEM, VMEM, VMEM, ANY],
            out_specs=[VMEM, VMEM],
            scratch_shapes=[
                pltpu.VMEM((r, markers), BF16),
                *ring(pb, kb),
                pltpu.VMEM((people, r), F32),
            ],
        ),
        out_shape=[
            jax.ShapeDtypeStruct((columns, r + t, people // columns), BF16),
            jax.ShapeDtypeStruct(message.shape, F32),
        ],
        compiler_params=pltpu.CompilerParams(vmem_limit_bytes=LIMIT),
        cost_estimate=cost(r, people, markers),
        name="first_forward",
    )(jnp.zeros((1,), jnp.int32), message, cols, slopes, probes, genotypes)


def narrow_body(n, unit, with_acc, off, *refs):
    refs = list(refs)
    pieces = [refs.pop(0) for _ in range(n)]
    acc = refs.pop(0) if with_acc else None
    g, out, rows, held, sems = refs
    span = pieces[0].shape[1]

    def prepare():
        for j in range(n):
            rows[:, j * span : (j + 1) * span] = pieces[j][...]
        if with_acc:
            out[...] = acc[...]

    count = n * span // unit
    forward_loop(
        g, rows, out, held, sems, lambda j: off[j], unit, count, False, not with_acc, prepare
    )


def narrow_forward(pieces, places, acc, genotypes, name):
    people = genotypes.shape[0]
    n, (t, span) = len(pieces), pieces[0].shape
    unit = n * span // places.shape[0]
    pb, kb = block_of(people, 1024), block_of(unit, 2048)
    operands = [*pieces, *([] if acc is None else [acc]), genotypes]
    return pl.pallas_call(
        functools.partial(narrow_body, n, unit, acc is not None),
        grid_spec=pltpu.PrefetchScalarGridSpec(
            num_scalar_prefetch=1,
            grid=(),
            in_specs=[VMEM] * (len(operands) - 1) + [ANY],
            out_specs=VMEM,
            scratch_shapes=[pltpu.VMEM((t, n * span), BF16), *ring(pb, kb)],
        ),
        out_shape=jax.ShapeDtypeStruct((t, people), F32),
        compiler_params=pltpu.CompilerParams(vmem_limit_bytes=LIMIT),
        cost_estimate=cost(t, people, n * span),
        name=name,
    )(places, *operands)


def wide_body(n, begin, chunks, with_acc, off, *refs):
    refs = list(refs)
    pieces = [refs.pop(0) for _ in range(n)]
    inner = [refs.pop(0) for _ in range(chunks)]
    outer = [refs.pop(0) for _ in range(chunks)]
    acc = refs.pop(0) if with_acc else None
    if with_acc:
        g, out, rows, held, sems, total = refs
    else:
        g, total, rows, held, sems = refs
    t, unit = pieces[0].shape[0], pieces[0].shape[1] // 2
    ends = [0]
    for x in inner:
        ends.append(ends[-1] + x.shape[1])
    count = ends[-1] // unit

    def prepare():
        for j, half in [(j, half) for j in range(n) for half in range(2)]:
            place = 2 * off[j] + half - begin

            @pl.when((place >= 0) & (place < count))
            def _():
                here = pl.ds(pl.multiple_of(place * unit, unit), unit)
                rows[:t, here] = pieces[j][:, half * unit : (half + 1) * unit]

        for j in range(chunks):
            here = slice(ends[j], ends[j + 1])

            @pl.when(off[n] == 1)
            def _():
                rows[t:, here] = inner[j][...]

            @pl.when(off[n] == 0)
            def _():
                rows[t:, here] = outer[j][...]

        if with_acc:
            total[...] = acc[...]

    forward_loop(
        g, rows, total, held, sems, lambda j: begin + j, unit, count, True, not with_acc, prepare
    )
    if with_acc:
        split_people(out, total, 0)


def wide_forward(pieces, inner, outer, places, begin, acc, genotypes, columns, name):
    people = genotypes.shape[0]
    n, t, unit = len(pieces), pieces[0].shape[0], pieces[0].shape[1] // 2
    r = t + inner[0].shape[0]
    pb, kb = block_of(people, 1024), block_of(unit, 2048)
    operands = [*pieces, *inner, *outer, *([] if acc is None else [acc]), genotypes]
    span = sum(x.shape[1] for x in inner)
    scratch = [pltpu.VMEM((r, span), BF16), *ring(pb, kb)]
    if acc is None:
        shape = jax.ShapeDtypeStruct((people, r), F32)
    else:
        shape = jax.ShapeDtypeStruct((columns, r, people // columns), BF16)
        scratch.append(pltpu.VMEM((people, r), F32))
    return pl.pallas_call(
        functools.partial(wide_body, n, begin, len(inner), acc is not None),
        grid_spec=pltpu.PrefetchScalarGridSpec(
            num_scalar_prefetch=1,
            grid=(),
            in_specs=[VMEM] * (len(operands) - 1) + [ANY],
            out_specs=VMEM,
            scratch_shapes=scratch,
        ),
        out_shape=shape,
        compiler_params=pltpu.CompilerParams(vmem_limit_bytes=LIMIT),
        cost_estimate=cost(r, people, span),
        name=name,
    )(places, *operands)


def backward_loop(g, rows, total, held, sems, unit_at, span, pieces):
    people = g.shape[0]
    slots, pk, mb = held.shape
    steps, blocks = span // mb, people // pk

    def place(c):
        k, i = c // blocks, lax.rem(c, blocks)
        col = unit_at(k // steps) * span + lax.rem(k, steps) * mb
        return g.at[pl.ds(pl.multiple_of(i * pk, pk), pk), pl.ds(pl.multiple_of(col, mb), mb)]

    def use(c, slot):
        k, i = c // blocks, lax.rem(c, blocks)
        here = pl.ds(pl.multiple_of(k * mb, mb), mb)
        d = rows[:, pl.ds(pl.multiple_of(i * pk, pk), pk)]
        value = jnp.dot(d, slot[...], preferred_element_type=F32)

        @pl.when(i == 0)
        def _():
            total[:, here] = value

        @pl.when(i > 0)
        def _():
            total[:, here] += value

    stream(place, held, sems, pieces * steps * blocks, lambda: None, use)


def first_back_body(unit, begin, t, arrays, off, rows, g, *refs):
    refs = list(refs)
    before = refs.pop(0) if begin else None
    total, held, sems = refs[-3:]
    count = total.shape[1] // unit
    backward_loop(g, rows, total, held, sems, lambda j: begin + j, unit, count)
    if not begin:
        refs[0][...] = total[:t, :]
        chunks = refs[1:-3]
    else:
        whole = refs[-4]
        first = begin * unit
        whole[:, :first] = before[...]
        whole[:, first:] = total[:t, :]
        for k in range(arrays):
            out = refs[k]
            span = out.shape[1]
            out[...] = whole[:, pl.ds(pl.multiple_of(off[k] * span, span), span)]
        chunks = refs[arrays:-4]
    at = 0
    for chunk in chunks:
        chunk[...] = total[t:, at : at + chunk.shape[1]].astype(BF16)
        at += chunk.shape[1]


def first_back(rows, order, genotypes, unit, t, begin, before, sizes, name):
    people, markers = genotypes.shape
    r, n = rows.shape[0], sum(sizes)
    pk, mb = block_of(people, 1024), block_of(unit, 2048)
    arrays = order.shape[0]
    operands = [rows, genotypes]
    scratch = [pltpu.VMEM((r, n * unit), F32)]
    if begin:
        operands.append(before)
        out_shape = [jax.ShapeDtypeStruct((t, markers // arrays), F32)] * arrays
        scratch.insert(0, pltpu.VMEM((t, markers), F32))
    else:
        out_shape = [jax.ShapeDtypeStruct((t, n * unit), F32)]
    out_shape += [jax.ShapeDtypeStruct((r - t, c * unit), BF16) for c in sizes]
    return pl.pallas_call(
        functools.partial(first_back_body, unit, begin, t, arrays),
        grid_spec=pltpu.PrefetchScalarGridSpec(
            num_scalar_prefetch=1,
            grid=(),
            in_specs=[VMEM, ANY] + [VMEM] * (len(operands) - 2),
            out_specs=[VMEM] * len(out_shape),
            scratch_shapes=[*scratch, *ring(pk, mb)],
        ),
        out_shape=out_shape,
        compiler_params=pltpu.CompilerParams(vmem_limit_bytes=LIMIT),
        cost_estimate=cost(r, people, n * unit),
        name=name,
    )(order, *operands)


def second_back_body(n, unit, off, rows, g, *refs):
    outs, (total, held, sems) = refs[:-3], refs[-3:]
    backward_loop(g, rows, total, held, sems, lambda j: off[j], unit, n)
    span = outs[0].shape[1]
    for j, out in enumerate(outs):
        out[...] = total[:, j * span : (j + 1) * span].astype(out.dtype)


def second_back(rows, places, genotypes, unit, types):
    people = genotypes.shape[0]
    r, n = rows.shape[0], places.shape[0]
    pk, mb = block_of(people, 1024), block_of(unit, 2048)
    return pl.pallas_call(
        functools.partial(second_back_body, n, unit),
        grid_spec=pltpu.PrefetchScalarGridSpec(
            num_scalar_prefetch=1,
            grid=(),
            in_specs=[VMEM, ANY],
            out_specs=[VMEM] * len(types),
            scratch_shapes=[pltpu.VMEM((r, n * unit), F32), *ring(pk, mb)],
        ),
        out_shape=[jax.ShapeDtypeStruct((r, n * unit // len(types)), kind) for kind in types],
        compiler_params=pltpu.CompilerParams(vmem_limit_bytes=LIMIT),
        cost_estimate=cost(r, people, n * unit),
        name="second_back",
    )(places, rows, genotypes)


def finish_body(n, copies, off, sums, wide_cols, cols, centre, *refs):
    start_hi, back_hi, low = refs[:n], refs[n : 2 * n], refs[2 * n : 3 * n]
    estimate, lmmse = refs[3 * n :]
    t, unit = start_hi[0].shape[0], start_hi[0].shape[1] // 2
    sums = sums[...].T
    norm_start, du, uu, xx, xw, ww = [sums[:, j : j + 1] for j in range(6)]
    tau, gamma = wide_cols[:, 0:1], wide_cols[:, 1:2]
    second_precision, slab_var, odds = [cols[:, j : j + 1] for j in range(3)]

    step_0 = norm_start / (tau * du + gamma * norm_start)
    left, b = 1.0 - step_0 * gamma, step_0 * tau
    norm_next = left * left * norm_start - 2.0 * left * b * du + b * b * uu
    a = left + norm_next / norm_start
    dir_norm = a * a * norm_start - 2.0 * a * b * du + b * b * uu
    dir_square = a * a * xx - 2.0 * a * b * xw + b * b * ww
    step_1 = norm_next / (tau * dir_square + gamma * dir_norm)

    start_coef = (step_0 + step_1 * a)[:t]
    back_coef = (step_1 * b)[:t]
    dots = step_0 * norm_start + step_1 * (a * norm_start - b * du)
    probe_dot = sum(dots[i * t : (i + 1) * t] for i in range(1, copies))
    probe_norm = sum(norm_start[i * t : (i + 1) * t] for i in range(1, copies))
    second_slope = second_precision * probe_dot / (probe_norm + 1e-06)
    next_precision = second_precision * (1.0 - second_slope) / second_slope
    next_shrink = slab_var * next_precision / (1.0 + slab_var * next_precision)
    next_base = odds + 0.5 * jnp.log(1.0 - next_shrink)
    for j, half in [(j, half) for j in range(n) for half in range(2)]:
        here = pl.ds(pl.multiple_of((2 * off[j] + half) * unit, unit), unit)
        part = slice(half * unit, (half + 1) * unit)
        start = start_hi[j][:, part].astype(F32) + low[j][:, part].astype(F32)
        back = back_hi[j][:, part].astype(F32)
        middle = centre[:, here]
        made = middle + start_coef * start - back_coef * back
        lmmse[:, here] = made
        next_message = (made - second_slope * middle) / (1.0 - second_slope)
        value, _ = denoise(next_message, next_precision, next_shrink, next_base)
        estimate[:, here] = value


def finish(places, sums, wide_cols, cols, centre, start_hi, back_hi, low):
    n = len(low)
    shape = jax.ShapeDtypeStruct(centre.shape, F32)
    copies = sums.shape[1] // centre.shape[0]
    operands = [sums, wide_cols, cols, centre, *start_hi, *back_hi, *low]
    return pl.pallas_call(
        functools.partial(finish_body, n, copies),
        grid_spec=pltpu.PrefetchScalarGridSpec(
            num_scalar_prefetch=1, grid=(), in_specs=[VMEM] * len(operands), out_specs=[VMEM, VMEM]
        ),
        out_shape=[shape, shape],
        compiler_params=pltpu.CompilerParams(vmem_limit_bytes=LIMIT),
        name="finish",
    )(places, *operands)


def per_device(
    genotypes, phenotypes, message, probes, inclusion, slab_ratio, input_precision, noise_precision
):
    samples, columns = lax.axis_size("sample"), lax.axis_size("marker")
    people_here, markers_here = genotypes.shape
    people, markers = people_here * samples, markers_here * columns
    traits = message.shape[0]
    copies = probes.shape[0] // traits + 1
    me, column = lax.axis_index("sample"), lax.axis_index("marker")
    unit, share = markers_here // (2 * samples), people_here // columns
    order = jnp.arange(samples, dtype=jnp.int32) ^ me
    some = samples // 2
    owned = jnp.stack([2 * order, 2 * order + 1], axis=1).reshape(-1)

    cols = jnp.stack([inclusion, slab_ratio, input_precision], axis=1)
    slopes = slope_sum(message, cols)
    slopes = slopes + swap(slopes, "marker", 1)
    probes_b = lax.optimization_barrier((probes, slopes))[0].astype(BF16)
    slopes = sum_direct(slopes, "marker", 2)
    value, centre = first_forward(message, cols, slopes, probes_b, genotypes, columns)
    kept_x = jnp.sum(lax.all_to_all(value, "marker", 0, 0).astype(F32), axis=0)
    kept_x, low_x = kept_x[: traits * copies], kept_x[traits * copies :]
    own = lax.dynamic_slice_in_dim(phenotypes, column * share, share, 1) - (kept_x[:traits] + low_x)
    rows = jnp.concatenate([own, kept_x[traits:]], axis=0).astype(BF16)
    pred_x = rows[traits:].astype(F32)
    rows = lax.all_gather(rows, "marker", axis=1, tiled=True)
    sizes = (samples - 1, samples - 1, some)
    before, *chunks = first_back(
        rows, order, genotypes, unit, traits, 0, None, sizes[:1], "first_back_0"
    )
    rows, before, chunks[0] = lax.optimization_barrier((rows, before, chunks[0]))
    outs = first_back(
        rows, order, genotypes, unit, traits, sizes[0], before, sizes[1:], "first_back_1"
    )
    chunks += outs[samples:]

    def add(x, y):
        return (x.astype(F32) + y.astype(F32)).astype(BF16)

    def tie(values, *others):
        return lax.optimization_barrier((tuple(values), others))[0]

    def inward(c):
        return lax.ppermute(chunks[c], "sample", [(0, 1), (3, 2)])

    def across(x):
        return lax.ppermute(x, "sample", [(1, 2), (2, 1)])

    def outward(x):
        return lax.ppermute(x, "sample", [(1, 0), (2, 3)])

    pair, full, ends = [None] * 3, [None] * 3, [None] * 3
    *parts, pair[0] = tie((*outs[:samples], inward(0)))
    sent = [swap(part, "sample", k) if k else part for k, part in enumerate(parts)]
    pair[0] = add(chunks[0], pair[0])
    scale = (noise_precision / people)[:, None]
    start = scale * tree(sent)
    start_high = lax.reduce_precision(start, 8, 7)
    start_low = (start - start_high).astype(BF16)
    start_high = start_high.astype(BF16)

    start_pieces = [swap(start_high, "sample", k) if k else start_high for k in range(samples)]
    *start_pieces, pair[0], chunks[1] = tie((*start_pieces, pair[0], chunks[1]))
    full[0], pair[1] = across(pair[0]), inward(1)
    value = narrow_forward(start_pieces, owned, None, genotypes, "second_forward")
    value, full[0], pair[1] = tie((value, full[0], pair[1]))
    value = sum_marker(value)
    kept_s = lax.dynamic_slice_in_dim(value, column * share, share, 1)
    full[0], pair[1] = tie((add(pair[0], full[0]), add(chunks[1], pair[1])))
    rows, full[0], pair[1], chunks[2] = tie((value.astype(BF16), full[0], pair[1], chunks[2]))
    ends[0], full[1], pair[2] = outward(full[0]), across(pair[1]), inward(2)
    parts = second_back(rows, owned, genotypes, unit, [F32] + [BF16] * (samples - 1))
    *parts, ends[0] = tie((*parts, ends[0]))
    sent = [swap(part, "sample", k) if k else part for k, part in enumerate(parts)]
    full[1], pair[2] = tie((full[1], pair[2]), *parts)
    full[1], pair[2] = add(pair[1], full[1]), add(chunks[2], pair[2])
    ends[1] = outward(full[1])
    back_high = tree([part.astype(F32) for part in sent]).astype(BF16)
    back = back_high.astype(F32)
    back_pieces = [swap(back_high, "sample", k) if k else back_high for k in range(samples)]
    full[2] = add(*tie((pair[2], across(pair[2])), *back_pieces))
    ends[2] = outward(full[2])

    inner = ((me == 1) | (me == 2)).astype(jnp.int32)
    places = jnp.concatenate([order, inner[None]])
    total = wide_forward(
        back_pieces, full[:2], ends[:2], places, 0, None, genotypes, columns, "third_forward_0"
    )
    (start_low,) = tie((start_low,), total)
    low_pieces = [swap(start_low, "sample", k) if k else start_low for k in range(samples)]
    value = wide_forward(
        back_pieces, full[2:], ends[2:], places, sum(sizes[:2]), total, genotypes, columns, "third_forward_1"
    )
    (last,) = tie((lax.all_to_all(value, "marker", 0, 0),), *low_pieces)
    last = jnp.sum(last.astype(F32), axis=0)
    before = jnp.concatenate([kept_s, kept_x[traits:]], axis=0)

    def dot(x, y):
        return jnp.sum(x * y, axis=1)

    probes_here = lax.dynamic_slice_in_dim(probes, 2 * me * unit, 2 * unit, 1)
    kept_p, last_p = kept_x[traits:], last[traits:]
    norms = jnp.concatenate(
        [
            jnp.stack([dot(start, start), dot(start, back), dot(back, back)]),
            jnp.stack([dot(probes_here, probes_here), dot(kept_p, pred_x), dot(last_p, pred_x)]),
        ],
        axis=1,
    )
    squares = jnp.stack([dot(before, before), dot(before, last), dot(last, last)])
    sums = jnp.concatenate([norms, squares, jnp.zeros((2, norms.shape[1]), F32)], axis=0)
    sums = sum_direct(sum_marker(sums), "sample")

    first_slope = slopes[:, 0] / markers
    second_precision = input_precision * (1.0 - first_slope) / first_slope
    odds = jnp.log(inclusion / (1.0 - inclusion))
    wide_cols = jnp.stack(
        [jnp.tile(noise_precision / people, copies), jnp.tile(second_precision, copies)], axis=1
    )
    cols = jnp.stack([second_precision, slab_ratio / input_precision, odds], axis=1)
    return tuple(
        finish(order, sums, wide_cols, cols, centre, start_pieces, back_pieces, low_pieces)
    )


def solution(mesh):
    return jax.shard_map(
        per_device,
        mesh=mesh,
        in_specs=(
            P("sample", "marker"),
            P(None, "sample"),
            P(None, "marker"),
            P(None, "marker"),
            P(),
            P(),
            P(),
            P(),
        ),
        out_specs=(P(None, "marker"), P(None, "marker")),
        check_vma=False,
    )
```

```python
import functools

import jax
import jax.numpy as jnp
from jax import lax
from jax.experimental import pallas as pl
from jax.experimental.pallas import tpu as pltpu
from jax.sharding import PartitionSpec as P

F32 = jnp.float32
BF16 = jnp.bfloat16
LIMIT = 44 << 20
SLOTS = 4
VMEM = pl.BlockSpec(memory_space=pltpu.VMEM)
ANY = pl.BlockSpec(memory_space=pl.ANY)


def block_of(size, most):
    while size % most:
        most //= 2
    return most


def swap(x, axis, bits):
    n = lax.axis_size(axis)
    return lax.ppermute(x, axis, [(i, i ^ bits) for i in range(n)])


def tree(parts):
    while len(parts) > 1:
        parts = [parts[i] + parts[i + 1] for i in range(0, len(parts), 2)]
    return parts[0]


def sum_direct(x, axis, unit=1):
    n = lax.axis_size(axis)
    return tree([x if k == 0 else swap(x, axis, k) for k in range(0, n, unit)])


def sum_marker(x):
    return sum_direct(x + swap(x, "marker", 1), "marker", 2)


def denoise(signal, precision, shrink, logit_base):
    energy = shrink * precision * signal * signal
    weight = jax.nn.sigmoid(logit_base + 0.5 * energy)
    return (shrink * weight * signal, shrink * weight * (1.0 + (1.0 - weight) * energy))


def stream(place, held, sems, total, prepare, use):
    slots = held.shape[0]

    def copy(c):
        slot = lax.rem(c, slots)
        return pltpu.make_async_copy(place(c), held.at[slot], sems.at[slot])

    for c in range(min(slots, total)):
        copy(c).start()
    prepare()

    def step(c, carry):
        copy(c).wait()
        use(c, held.at[lax.rem(c, slots)])

        @pl.when(c + slots < total)
        def _():
            copy(c + slots).start()

        return carry

    lax.fori_loop(0, total, step, 0)


def ring(rows, columns):
    return [pltpu.VMEM((SLOTS, rows, columns), BF16), pltpu.SemaphoreType.DMA((SLOTS,))]


def forward_loop(g, rows, total, held, sems, unit_at, span, pieces, wide, fresh, prepare):
    people = g.shape[0]
    slots, pb, kb = held.shape
    steps, blocks = span // kb, people // pb

    def place(c):
        k, i = c // blocks, lax.rem(c, blocks)
        col = unit_at(k // steps) * span + lax.rem(k, steps) * kb
        return g.at[pl.ds(pl.multiple_of(i * pb, pb), pb), pl.ds(pl.multiple_of(col, kb), kb)]

    def use(c, slot):
        k, i = c // blocks, lax.rem(c, blocks)
        d = rows[:, pl.ds(pl.multiple_of(k * kb, kb), kb)]
        here = pl.ds(pl.multiple_of(i * pb, pb), pb)
        across = (((1,), (1,)), ((), ()))
        if wide:
            at = (here, slice(None))
            value = lax.dot_general(slot[...], d, across, preferred_element_type=F32)
        else:
            at = (slice(None), here)
            value = lax.dot_general(d, slot[...], across, preferred_element_type=F32)
        if fresh:

            @pl.when(k == 0)
            def _():
                total[at] = value

            @pl.when(k > 0)
            def _():
                total[at] += value

        else:
            total[at] += value

    stream(place, held, sems, pieces * steps * blocks, prepare, use)


def split_people(out, total, t):
    n, r, share = out.shape
    for b in range(n):
        value = total[b * share : (b + 1) * share, :].T
        high = value.astype(BF16)
        out[b, : r - t, :] = high
        if t:
            out[b, r - t :, :] = (value[:t] - high[:t].astype(F32)).astype(BF16)


def prior(cols):
    inclusion, ratio, precision = [cols[:, j : j + 1] for j in range(3)]
    shrink = ratio / (1.0 + ratio)
    base = jnp.log(inclusion / (1.0 - inclusion)) + 0.5 * jnp.log(1.0 - shrink)
    return precision, shrink, base


def slope_body(message, cols, out):
    _, slopes = denoise(message[...], *prior(cols))
    out[...] = jnp.sum(slopes, axis=1, keepdims=True)


def slope_sum(message, cols):
    return pl.pallas_call(
        slope_body,
        in_specs=[VMEM, VMEM],
        out_specs=VMEM,
        out_shape=jax.ShapeDtypeStruct((message.shape[0], 1), F32),
        compiler_params=pltpu.CompilerParams(vmem_limit_bytes=LIMIT),
        name="slope_sum",
    )(message, cols)


def first_body(markers, off, message, cols, slopes, probes, g, out, centre, rows, held, sems, total):
    t = message.shape[0]

    def prepare():
        slope = slopes[...] / markers
        first, _ = denoise(message[...], *prior(cols))
        made = (first - slope * message[...]) / (1.0 - slope)
        centre[...] = made
        rows[:t, :] = made.astype(BF16)
        rows[t:, :] = probes[...]

    forward_loop(g, rows, total, held, sems, lambda j: j, g.shape[1], 1, True, True, prepare)
    split_people(out, total, t)


def cost(rows, people, markers):
    return pl.CostEstimate(
        flops=2 * rows * people * markers, transcendentals=0, bytes_accessed=2 * people * markers
    )


def first_forward(message, cols, slopes, probes, genotypes, columns):
    people, markers = genotypes.shape
    t = message.shape[0]
    r = t + probes.shape[0]
    pb, kb = block_of(people, 1024), block_of(markers, 2048)
    return pl.pallas_call(
        functools.partial(first_body, markers * columns),
        grid_spec=pltpu.PrefetchScalarGridSpec(
            num_scalar_prefetch=1,
            grid=(),
            in_specs=[VMEM, VMEM, VMEM, VMEM, ANY],
            out_specs=[VMEM, VMEM],
            scratch_shapes=[
                pltpu.VMEM((r, markers), BF16),
                *ring(pb, kb),
                pltpu.VMEM((people, r), F32),
            ],
        ),
        out_shape=[
            jax.ShapeDtypeStruct((columns, r + t, people // columns), BF16),
            jax.ShapeDtypeStruct(message.shape, F32),
        ],
        compiler_params=pltpu.CompilerParams(vmem_limit_bytes=LIMIT),
        cost_estimate=cost(r, people, markers),
        name="first_forward",
    )(jnp.zeros((1,), jnp.int32), message, cols, slopes, probes, genotypes)


def narrow_body(n, unit, with_acc, off, *refs):
    refs = list(refs)
    pieces = [refs.pop(0) for _ in range(n)]
    acc = refs.pop(0) if with_acc else None
    g, out, rows, held, sems = refs
    span = pieces[0].shape[1]

    def prepare():
        for j in range(n):
            rows[:, j * span : (j + 1) * span] = pieces[j][...]
        if with_acc:
            out[...] = acc[...]

    count = n * span // unit
    forward_loop(
        g, rows, out, held, sems, lambda j: off[j], unit, count, False, not with_acc, prepare
    )


def narrow_forward(pieces, places, acc, genotypes, name):
    people = genotypes.shape[0]
    n, (t, span) = len(pieces), pieces[0].shape
    unit = n * span // places.shape[0]
    pb, kb = block_of(people, 1024), block_of(unit, 2048)
    operands = [*pieces, *([] if acc is None else [acc]), genotypes]
    return pl.pallas_call(
        functools.partial(narrow_body, n, unit, acc is not None),
        grid_spec=pltpu.PrefetchScalarGridSpec(
            num_scalar_prefetch=1,
            grid=(),
            in_specs=[VMEM] * (len(operands) - 1) + [ANY],
            out_specs=VMEM,
            scratch_shapes=[pltpu.VMEM((t, n * span), BF16), *ring(pb, kb)],
        ),
        out_shape=jax.ShapeDtypeStruct((t, people), F32),
        compiler_params=pltpu.CompilerParams(vmem_limit_bytes=LIMIT),
        cost_estimate=cost(t, people, n * span),
        name=name,
    )(places, *operands)


def wide_body(n, begin, chunks, with_acc, off, *refs):
    refs = list(refs)
    pieces = [refs.pop(0) for _ in range(n)]
    inner = [refs.pop(0) for _ in range(chunks)]
    outer = [refs.pop(0) for _ in range(chunks)]
    acc = refs.pop(0) if with_acc else None
    if with_acc:
        g, out, rows, held, sems, total = refs
    else:
        g, total, rows, held, sems = refs
    t, unit = pieces[0].shape[0], pieces[0].shape[1] // 2
    ends = [0]
    for x in inner:
        ends.append(ends[-1] + x.shape[1])
    count = ends[-1] // unit

    def prepare():
        for j, half in [(j, half) for j in range(n) for half in range(2)]:
            place = 2 * off[j] + half - begin

            @pl.when((place >= 0) & (place < count))
            def _():
                here = pl.ds(pl.multiple_of(place * unit, unit), unit)
                rows[:t, here] = pieces[j][:, half * unit : (half + 1) * unit]

        for j in range(chunks):
            here = slice(ends[j], ends[j + 1])

            @pl.when(off[n] == 1)
            def _():
                rows[t:, here] = inner[j][...]

            @pl.when(off[n] == 0)
            def _():
                rows[t:, here] = outer[j][...]

        if with_acc:
            total[...] = acc[...]

    forward_loop(
        g, rows, total, held, sems, lambda j: begin + j, unit, count, True, not with_acc, prepare
    )
    if with_acc:
        split_people(out, total, 0)


def wide_forward(pieces, inner, outer, places, begin, acc, genotypes, columns, name):
    people = genotypes.shape[0]
    n, t, unit = len(pieces), pieces[0].shape[0], pieces[0].shape[1] // 2
    r = t + inner[0].shape[0]
    pb, kb = block_of(people, 1024), block_of(unit, 2048)
    operands = [*pieces, *inner, *outer, *([] if acc is None else [acc]), genotypes]
    span = sum(x.shape[1] for x in inner)
    scratch = [pltpu.VMEM((r, span), BF16), *ring(pb, kb)]
    if acc is None:
        shape = jax.ShapeDtypeStruct((people, r), F32)
    else:
        shape = jax.ShapeDtypeStruct((columns, r, people // columns), BF16)
        scratch.append(pltpu.VMEM((people, r), F32))
    return pl.pallas_call(
        functools.partial(wide_body, n, begin, len(inner), acc is not None),
        grid_spec=pltpu.PrefetchScalarGridSpec(
            num_scalar_prefetch=1,
            grid=(),
            in_specs=[VMEM] * (len(operands) - 1) + [ANY],
            out_specs=VMEM,
            scratch_shapes=scratch,
        ),
        out_shape=shape,
        compiler_params=pltpu.CompilerParams(vmem_limit_bytes=LIMIT),
        cost_estimate=cost(r, people, span),
        name=name,
    )(places, *operands)


def backward_loop(g, rows, total, held, sems, unit_at, span, pieces):
    people = g.shape[0]
    slots, pk, mb = held.shape
    steps, blocks = span // mb, people // pk

    def place(c):
        k, i = c // blocks, lax.rem(c, blocks)
        col = unit_at(k // steps) * span + lax.rem(k, steps) * mb
        return g.at[pl.ds(pl.multiple_of(i * pk, pk), pk), pl.ds(pl.multiple_of(col, mb), mb)]

    def use(c, slot):
        k, i = c // blocks, lax.rem(c, blocks)
        here = pl.ds(pl.multiple_of(k * mb, mb), mb)
        d = rows[:, pl.ds(pl.multiple_of(i * pk, pk), pk)]
        value = jnp.dot(d, slot[...], preferred_element_type=F32)

        @pl.when(i == 0)
        def _():
            total[:, here] = value

        @pl.when(i > 0)
        def _():
            total[:, here] += value

    stream(place, held, sems, pieces * steps * blocks, lambda: None, use)


def first_back_body(unit, begin, t, arrays, off, rows, g, *refs):
    refs = list(refs)
    before = refs.pop(0) if begin else None
    total, held, sems = refs[-3:]
    count = total.shape[1] // unit
    backward_loop(g, rows, total, held, sems, lambda j: begin + j, unit, count)
    if not begin:
        refs[0][...] = total[:t, :]
        chunks = refs[1:-3]
    else:
        whole = refs[-4]
        first = begin * unit
        whole[:, :first] = before[...]
        whole[:, first:] = total[:t, :]
        for k in range(arrays):
            out = refs[k]
            span = out.shape[1]
            out[...] = whole[:, pl.ds(pl.multiple_of(off[k] * span, span), span)]
        chunks = refs[arrays:-4]
    at = 0
    for chunk in chunks:
        chunk[...] = total[t:, at : at + chunk.shape[1]].astype(BF16)
        at += chunk.shape[1]


def first_back(rows, order, genotypes, unit, t, begin, before, sizes, name):
    people, markers = genotypes.shape
    r, n = rows.shape[0], sum(sizes)
    pk, mb = block_of(people, 1024), block_of(unit, 2048)
    arrays = order.shape[0]
    operands = [rows, genotypes]
    scratch = [pltpu.VMEM((r, n * unit), F32)]
    if begin:
        operands.append(before)
        out_shape = [jax.ShapeDtypeStruct((t, markers // arrays), F32)] * arrays
        scratch.insert(0, pltpu.VMEM((t, markers), F32))
    else:
        out_shape = [jax.ShapeDtypeStruct((t, n * unit), F32)]
    out_shape += [jax.ShapeDtypeStruct((r - t, c * unit), BF16) for c in sizes]
    return pl.pallas_call(
        functools.partial(first_back_body, unit, begin, t, arrays),
        grid_spec=pltpu.PrefetchScalarGridSpec(
            num_scalar_prefetch=1,
            grid=(),
            in_specs=[VMEM, ANY] + [VMEM] * (len(operands) - 2),
            out_specs=[VMEM] * len(out_shape),
            scratch_shapes=[*scratch, *ring(pk, mb)],
        ),
        out_shape=out_shape,
        compiler_params=pltpu.CompilerParams(vmem_limit_bytes=LIMIT),
        cost_estimate=cost(r, people, n * unit),
        name=name,
    )(order, *operands)


def second_back_body(n, unit, off, rows, g, *refs):
    outs, (total, held, sems) = refs[:-3], refs[-3:]
    backward_loop(g, rows, total, held, sems, lambda j: off[j], unit, n)
    span = outs[0].shape[1]
    for j, out in enumerate(outs):
        out[...] = total[:, j * span : (j + 1) * span].astype(out.dtype)


def second_back(rows, places, genotypes, unit, types):
    people = genotypes.shape[0]
    r, n = rows.shape[0], places.shape[0]
    pk, mb = block_of(people, 1024), block_of(unit, 2048)
    return pl.pallas_call(
        functools.partial(second_back_body, n, unit),
        grid_spec=pltpu.PrefetchScalarGridSpec(
            num_scalar_prefetch=1,
            grid=(),
            in_specs=[VMEM, ANY],
            out_specs=[VMEM] * len(types),
            scratch_shapes=[pltpu.VMEM((r, n * unit), F32), *ring(pk, mb)],
        ),
        out_shape=[jax.ShapeDtypeStruct((r, n * unit // len(types)), kind) for kind in types],
        compiler_params=pltpu.CompilerParams(vmem_limit_bytes=LIMIT),
        cost_estimate=cost(r, people, n * unit),
        name="second_back",
    )(places, rows, genotypes)


def finish_body(n, copies, off, sums, wide_cols, cols, centre, *refs):
    start_hi, back_hi, low = refs[:n], refs[n : 2 * n], refs[2 * n : 3 * n]
    estimate, lmmse = refs[3 * n :]
    t, unit = start_hi[0].shape[0], start_hi[0].shape[1] // 2
    sums = sums[...].T
    norm_start, du, uu, xx, xw, ww = [sums[:, j : j + 1] for j in range(6)]
    tau, gamma = wide_cols[:, 0:1], wide_cols[:, 1:2]
    second_precision, slab_var, odds = [cols[:, j : j + 1] for j in range(3)]

    step_0 = norm_start / (tau * du + gamma * norm_start)
    left, b = 1.0 - step_0 * gamma, step_0 * tau
    norm_next = left * left * norm_start - 2.0 * left * b * du + b * b * uu
    a = left + norm_next / norm_start
    dir_norm = a * a * norm_start - 2.0 * a * b * du + b * b * uu
    dir_square = a * a * xx - 2.0 * a * b * xw + b * b * ww
    step_1 = norm_next / (tau * dir_square + gamma * dir_norm)

    start_coef = (step_0 + step_1 * a)[:t]
    back_coef = (step_1 * b)[:t]
    dots = step_0 * norm_start + step_1 * (a * norm_start - b * du)
    probe_dot = sum(dots[i * t : (i + 1) * t] for i in range(1, copies))
    probe_norm = sum(norm_start[i * t : (i + 1) * t] for i in range(1, copies))
    second_slope = second_precision * probe_dot / (probe_norm + 1e-06)
    next_precision = second_precision * (1.0 - second_slope) / second_slope
    next_shrink = slab_var * next_precision / (1.0 + slab_var * next_precision)
    next_base = odds + 0.5 * jnp.log(1.0 - next_shrink)
    for j, half in [(j, half) for j in range(n) for half in range(2)]:
        here = pl.ds(pl.multiple_of((2 * off[j] + half) * unit, unit), unit)
        part = slice(half * unit, (half + 1) * unit)
        start = start_hi[j][:, part].astype(F32) + low[j][:, part].astype(F32)
        back = back_hi[j][:, part].astype(F32)
        middle = centre[:, here]
        made = middle + start_coef * start - back_coef * back
        lmmse[:, here] = made
        next_message = (made - second_slope * middle) / (1.0 - second_slope)
        value, _ = denoise(next_message, next_precision, next_shrink, next_base)
        estimate[:, here] = value


def finish(places, sums, wide_cols, cols, centre, start_hi, back_hi, low):
    n = len(low)
    shape = jax.ShapeDtypeStruct(centre.shape, F32)
    copies = sums.shape[1] // centre.shape[0]
    operands = [sums, wide_cols, cols, centre, *start_hi, *back_hi, *low]
    return pl.pallas_call(
        functools.partial(finish_body, n, copies),
        grid_spec=pltpu.PrefetchScalarGridSpec(
            num_scalar_prefetch=1, grid=(), in_specs=[VMEM] * len(operands), out_specs=[VMEM, VMEM]
        ),
        out_shape=[shape, shape],
        compiler_params=pltpu.CompilerParams(vmem_limit_bytes=LIMIT),
        name="finish",
    )(places, *operands)


def per_device(
    genotypes, phenotypes, message, probes, inclusion, slab_ratio, input_precision, noise_precision
):
    samples, columns = lax.axis_size("sample"), lax.axis_size("marker")
    people_here, markers_here = genotypes.shape
    people, markers = people_here * samples, markers_here * columns
    traits = message.shape[0]
    copies = probes.shape[0] // traits + 1
    me, column = lax.axis_index("sample"), lax.axis_index("marker")
    unit, share = markers_here // (2 * samples), people_here // columns
    order = jnp.arange(samples, dtype=jnp.int32) ^ me
    some = samples // 2
    owned = jnp.stack([2 * order, 2 * order + 1], axis=1).reshape(-1)

    cols = jnp.stack([inclusion, slab_ratio, input_precision], axis=1)
    slopes = slope_sum(message, cols)
    slopes = slopes + swap(slopes, "marker", 1)
    probes_b = lax.optimization_barrier((probes, slopes))[0].astype(BF16)
    slopes = sum_direct(slopes, "marker", 2)
    value, centre = first_forward(message, cols, slopes, probes_b, genotypes, columns)
    kept_x = jnp.sum(lax.all_to_all(value, "marker", 0, 0).astype(F32), axis=0)
    kept_x, low_x = kept_x[: traits * copies], kept_x[traits * copies :]
    own = lax.dynamic_slice_in_dim(phenotypes, column * share, share, 1) - (kept_x[:traits] + low_x)
    rows = jnp.concatenate([own, kept_x[traits:]], axis=0).astype(BF16)
    pred_x = rows[traits:].astype(F32)
    rows = lax.all_gather(rows, "marker", axis=1, tiled=True)
    sizes = (some, samples - 1, samples - 1)
    before, *chunks = first_back(
        rows, order, genotypes, unit, traits, 0, None, sizes[:1], "first_back_0"
    )
    rows, before, chunks[0] = lax.optimization_barrier((rows, before, chunks[0]))
    outs = first_back(
        rows, order, genotypes, unit, traits, sizes[0], before, sizes[1:], "first_back_1"
    )
    chunks += outs[samples:]

    def add(x, y):
        return (x.astype(F32) + y.astype(F32)).astype(BF16)

    def tie(values, *others):
        return lax.optimization_barrier((tuple(values), others))[0]

    def inward(c):
        return lax.ppermute(chunks[c], "sample", [(0, 1), (3, 2)])

    def across(x):
        return lax.ppermute(x, "sample", [(1, 2), (2, 1)])

    def outward(x):
        return lax.ppermute(x, "sample", [(1, 0), (2, 3)])

    pair, full, ends = [None] * 3, [None] * 3, [None] * 3
    *parts, pair[0] = tie((*outs[:samples], inward(0)))
    sent = [swap(part, "sample", k) if k else part for k, part in enumerate(parts)]
    pair[0] = add(chunks[0], pair[0])
    scale = (noise_precision / people)[:, None]
    start = scale * tree(sent)
    start_high = lax.reduce_precision(start, 8, 7)
    start_low = (start - start_high).astype(BF16)
    start_high = start_high.astype(BF16)

    start_pieces = [swap(start_high, "sample", k) if k else start_high for k in range(samples)]
    *start_pieces, pair[0], chunks[1] = tie((*start_pieces, pair[0], chunks[1]))
    full[0], pair[1] = across(pair[0]), inward(1)
    value = narrow_forward(start_pieces, owned, None, genotypes, "second_forward")
    value, full[0], pair[1] = tie((value, full[0], pair[1]))
    value = sum_marker(value)
    kept_s = lax.dynamic_slice_in_dim(value, column * share, share, 1)
    full[0], pair[1] = tie((add(pair[0], full[0]), add(chunks[1], pair[1])))
    rows, full[0], pair[1], chunks[2] = tie((value.astype(BF16), full[0], pair[1], chunks[2]))
    ends[0], full[1], pair[2] = outward(full[0]), across(pair[1]), inward(2)
    parts = second_back(rows, owned, genotypes, unit, [F32] + [BF16] * (samples - 1))
    *parts, ends[0] = tie((*parts, ends[0]))
    sent = [swap(part, "sample", k) if k else part for k, part in enumerate(parts)]
    full[1], pair[2] = tie((full[1], pair[2]), *parts)
    full[1], pair[2] = add(pair[1], full[1]), add(chunks[2], pair[2])
    ends[1] = outward(full[1])
    back_high = tree([part.astype(F32) for part in sent]).astype(BF16)
    back = back_high.astype(F32)
    back_pieces = [swap(back_high, "sample", k) if k else back_high for k in range(samples)]
    full[2] = add(*tie((pair[2], across(pair[2])), *back_pieces))
    ends[2] = outward(full[2])

    inner = ((me == 1) | (me == 2)).astype(jnp.int32)
    places = jnp.concatenate([order, inner[None]])
    total = wide_forward(
        back_pieces, full[:2], ends[:2], places, 0, None, genotypes, columns, "third_forward_0"
    )
    (start_low,) = tie((start_low,), total)
    low_pieces = [swap(start_low, "sample", k) if k else start_low for k in range(samples)]
    value = wide_forward(
        back_pieces, full[2:], ends[2:], places, sum(sizes[:2]), total, genotypes, columns, "third_forward_1"
    )
    (value,) = tie((value,), *low_pieces)
    last = lax.all_to_all(value, "marker", 0, 0)
    last = jnp.sum(last.astype(F32), axis=0)
    before = jnp.concatenate([kept_s, kept_x[traits:]], axis=0)

    def dot(x, y):
        return jnp.sum(x * y, axis=1)

    probes_here = lax.dynamic_slice_in_dim(probes, 2 * me * unit, 2 * unit, 1)
    kept_p, last_p = kept_x[traits:], last[traits:]
    norms = jnp.concatenate(
        [
            jnp.stack([dot(start, start), dot(start, back), dot(back, back)]),
            jnp.stack([dot(probes_here, probes_here), dot(kept_p, pred_x), dot(last_p, pred_x)]),
        ],
        axis=1,
    )
    squares = jnp.stack([dot(before, before), dot(before, last), dot(last, last)])
    sums = jnp.concatenate([norms, squares, jnp.zeros((2, norms.shape[1]), F32)], axis=0)
    sums = sum_direct(sum_marker(sums), "sample")

    first_slope = slopes[:, 0] / markers
    second_precision = input_precision * (1.0 - first_slope) / first_slope
    odds = jnp.log(inclusion / (1.0 - inclusion))
    wide_cols = jnp.stack(
        [jnp.tile(noise_precision / people, copies), jnp.tile(second_precision, copies)], axis=1
    )
    cols = jnp.stack([second_precision, slab_ratio / input_precision, odds], axis=1)
    return tuple(
        finish(order, sums, wide_cols, cols, centre, start_pieces, back_pieces, low_pieces)
    )


def solution(mesh):
    return jax.shard_map(
        per_device,
        mesh=mesh,
        in_specs=(
            P("sample", "marker"),
            P(None, "sample"),
            P(None, "marker"),
            P(None, "marker"),
            P(),
            P(),
            P(),
            P(),
        ),
        out_specs=(P(None, "marker"), P(None, "marker")),
        check_vma=False,
    )
```
